32 devices in a mesh: dp: 8 (over y, x, core), blk: 4 (over z).
Axes of the slice: x: 2, y: 2, z: 4, core: 2. Of those that a mesh axis runs over, the one named last changes fastest.
Arguments:
- tokens: bfloat16 [16, 1024, 768], P('dp', 'blk'), may hold values from -6 to 6
- scene_ids: int32 [16, 1024], P('dp', 'blk'), may hold values from 0 to 1, as said below
- query_weight: bfloat16 [768, 768], replicated, may hold values from -0.3125 to 0.3125
- query_bias: float32 [768], replicated, may hold values from -1.8 to 1.8
- key_weight: bfloat16 [768, 768], replicated, may hold values from -0.21875 to 0.21875
- value_weight: bfloat16 [768, 768], replicated, may hold values from -0.21875 to 0.21875
- value_bias: float32 [768], replicated, may hold values from -1.8 to 1.8
- output_weight: bfloat16 [768, 768], replicated, may hold values from -1.75 to 1.75
- output_bias: float32 [768], replicated, may hold values from -1.8 to 1.8
- first_gain: float32 [768], replicated, may hold values from 0.5 to 1.5
- first_shift: float32 [768], replicated, may hold values from -1.8 to 1.8
- second_gain: float32 [768], replicated, may hold values from 0.5 to 1.5
- second_shift: float32 [768], replicated, may hold values from -1.8 to 1.8
- up_weight: bfloat16 [768, 1536], replicated, may hold values from -0.21875 to 0.21875
- up_bias: float32 [1536], replicated, may hold values from -1.8 to 1.8
- down_weight: bfloat16 [1536, 768], replicated, may hold values from -0.15625 to 0.15625
- down_bias: float32 [768], replicated, may hold values from -1.8 to 1.8
- cotangent: bfloat16 [16, 1024, 768], P('dp', 'blk'), may hold values from -6 to 6
Outputs:
- layer_out: bfloat16 [16, 1024, 768], P('dp', 'blk')
- tokens_grad: bfloat16 [16, 1024, 768], P('dp', 'blk')
- query_weight_grad: float32 [768, 768], replicated
- query_bias_grad: float32 [768], replicated
- key_weight_grad: float32 [768, 768], replicated
- value_weight_grad: float32 [768, 768], replicated
- value_bias_grad: float32 [768], replicated
- output_weight_grad: float32 [768, 768], replicated
- output_bias_grad: float32 [768], replicated
- first_gain_grad: float32 [768], replicated
- first_shift_grad: float32 [768], replicated
- second_gain_grad: float32 [768], replicated
- second_shift_grad: float32 [768], replicated
- up_weight_grad: float32 [768, 1536], replicated
- up_bias_grad: float32 [1536], replicated
- down_weight_grad: float32 [1536, 768], replicated
- down_bias_grad: float32 [768], replicated
The draws below stay inside these ranges and needn't reach their ends.
Inputs may be any that keep to these rules, and one draw needn't show every extreme that they name: `scene_ids`: in each sequence the scene number is constant within each aligned run of 256 tokens; among the 2 sequences of each index of dp one is a single scene, and the other one alternates between two scenes from one run to the next.
All inputs are finite; a program needn't handle non-finite values.
Results may differ from the reference program's by a relative error of at most 0.015.
The reference program's roundings to bfloat16 on the way count: a program that leaves them out, or rounds other values in their place, can miss the bound.
Values may be sent and summed in bfloat16 or wider, within the bound.
A program may use at most 128 MiB of HBM per device.

```python
import math
import jax
import jax.numpy as jnp
from jax import lax

D = 768
HEAD = 64
FF = 1536
ROWS_BLK = 256
SEQ_DEV = 2
SEQUENCES = 16
LENGTH = 1024


def draw_scene_ids(key, part):
    key = jax.random.fold_in(key, 7)
    blocks = LENGTH // ROWS_BLK
    numbers = jax.random.randint(jax.random.fold_in(key, 1), (SEQUENCES, blocks), 0, 2)
    groups = SEQUENCES // SEQ_DEV
    chosen = jax.random.randint(jax.random.fold_in(key, 2), (groups,), 0, SEQ_DEV)
    phase = jax.random.randint(jax.random.fold_in(key, 3), (groups,), 0, 2)
    slot = jnp.arange(SEQUENCES) % SEQ_DEV
    single = slot == jnp.repeat(chosen, SEQ_DEV)
    rising = slot == jnp.repeat((chosen + 1) % SEQ_DEV, SEQ_DEV)
    alternate = (jnp.arange(blocks)[None, :] + jnp.repeat(phase, SEQ_DEV)[:, None]) % 2
    numbers = jnp.where(rising[:, None], alternate, numbers)
    numbers = jnp.where(single[:, None], 0, numbers)
    return jnp.repeat(numbers, ROWS_BLK, axis=1).astype(jnp.int32)


def block_levels(rng, shape, cuts, least, largest):
    def one(position, parts):
        steps = jax.random.uniform(jax.random.fold_in(jax.random.fold_in(rng, 6), position), (parts,), jnp.float32, least / len(cuts), largest / len(cuts))
        return jnp.repeat(jnp.exp(steps), shape[position] // parts).reshape((-1,) + (1,) * (len(shape) - position - 1))

    level = one(*cuts[0])
    for cut in cuts[1:]:
        level = level * one(*cut)
    return level


def normal_values(stream_key, shape, spread, bound, pieces=(), held_as=jnp.bfloat16):
    entries = spread * jax.random.normal(stream_key, shape, jnp.float32)
    if pieces:
        entries = entries * block_levels(stream_key, shape, pieces, -0.22, 0.18)
    return jnp.clip(entries, -bound, bound).astype(held_as)


def setup_inputs(seed: int = 0) -> dict:
    arg_keys = jax.random.split(jax.random.key(seed), 19)
    tokens = normal_values(arg_keys[0], (SEQUENCES, LENGTH, D), 1.0, 6.0, ((0, 8), (1, 4)))
    scene_ids = draw_scene_ids(jax.random.fold_in(arg_keys[18], 71), 0)
    query_weight = normal_values(arg_keys[2], (D, D), (D // 2) ** -0.5, 0.3125)
    query_bias = normal_values(arg_keys[3], (D,), 0.3, 1.8, (), jnp.float32)
    key_weight = normal_values(arg_keys[4], (D, D), D ** -0.5, 0.21875)
    value_weight = normal_values(arg_keys[5], (D, D), D ** -0.5, 0.21875)
    value_bias = normal_values(arg_keys[6], (D,), 0.3, 1.8, (), jnp.float32)
    output_weight = normal_values(arg_keys[7], (D, D), (D // 64) ** -0.5, 1.75)
    output_bias = normal_values(arg_keys[8], (D,), 0.3, 1.8, (), jnp.float32)
    first_gain = jnp.clip(1.0 + 0.1 * jax.random.normal(arg_keys[9], (D,), jnp.float32), 0.5, 1.5)
    first_shift = normal_values(arg_keys[10], (D,), 0.3, 1.8, (), jnp.float32)
    second_gain = jnp.clip(1.0 + 0.1 * jax.random.normal(arg_keys[11], (D,), jnp.float32), 0.5, 1.5)
    second_shift = normal_values(arg_keys[12], (D,), 0.3, 1.8, (), jnp.float32)
    up_weight = normal_values(arg_keys[13], (D, FF), D ** -0.5, 0.21875)
    up_bias = normal_values(arg_keys[14], (FF,), 0.3, 1.8, (), jnp.float32)
    down_weight = normal_values(arg_keys[15], (FF, D), FF ** -0.5, 0.15625)
    down_bias = normal_values(arg_keys[16], (D,), 0.3, 1.8, (), jnp.float32)
    cotangent = normal_values(arg_keys[17], (SEQUENCES, LENGTH, D), 1.0, 6.0, ((0, 8), (1, 4)))
    return {"tokens": tokens, "scene_ids": scene_ids, "query_weight": query_weight, "query_bias": query_bias, "key_weight": key_weight, "value_weight": value_weight, "value_bias": value_bias, "output_weight": output_weight, "output_bias": output_bias, "first_gain": first_gain, "first_shift": first_shift, "second_gain": second_gain, "second_shift": second_shift, "up_weight": up_weight, "up_bias": up_bias, "down_weight": down_weight, "down_bias": down_bias, "cotangent": cotangent}


@jax.custom_vjp
def low(v):
    return lax.optimization_barrier(v.astype(jnp.bfloat16)).astype(jnp.float32)

@jax.custom_vjp
def low_back(v):
    return v

def low_keep(v):
    return (low(v), None)

def low_pass(kept, grad):
    return (grad,)

def back_keep(v):
    return (v, None)

def back_low(kept, grad):
    return (low(grad),)
low.defvjp(low_keep, low_pass)
low_back.defvjp(back_keep, back_low)
EPS = 1e-05
FLOOR = -1e+30

def matmul(left, weight):
    return jnp.dot(left, weight, precision=lax.Precision.HIGHEST)

def normalize(values, gain, shift):
    mean = lax.optimization_barrier(jnp.mean(values, -1, keepdims=True))
    centred = values - mean
    variance = lax.optimization_barrier(jnp.mean(centred * centred, -1, keepdims=True))
    return centred * lax.rsqrt(variance + EPS) * gain + shift

def attention(queries, keys, values, scenes):
    groups, length, width = queries.shape
    heads = width // HEAD
    scale = HEAD ** (-0.5)
    block = min(512, length)
    count = length // block
    kheads = keys.reshape(groups, length, heads, HEAD)
    vheads = values.reshape(groups, length, heads, HEAD)
    qblocks = queries.reshape(groups, count, block, heads, HEAD).transpose(1, 0, 2, 3, 4)
    sblocks = scenes.reshape(groups, count, block).transpose(1, 0, 2)

    def one_block(item):
        qpart, spart = item
        raw = jnp.einsum('gqhd,gkhd->ghqk', qpart, kheads, precision=lax.Precision.HIGHEST) * scale
        raw = low_back(raw)
        same = spart[:, None, :, None] == scenes[:, None, None, :]
        masked = jnp.where(same, raw, FLOOR)
        total = jax.nn.logsumexp(masked, axis=-1, keepdims=True)
        probs = low(jnp.exp(masked - total))
        return jnp.einsum('ghqk,gkhd->gqhd', probs, vheads, precision=lax.Precision.HIGHEST)
    result = lax.map(jax.checkpoint(one_block), (qblocks, sblocks))
    return result.transpose(1, 0, 2, 3, 4).reshape(groups, length, width)

def layer(inputs, params, scenes):
    query_weight, query_bias, key_weight, value_weight, value_bias, output_weight, output_bias, first_gain, first_shift, second_gain, second_shift, up_weight, up_bias, down_weight, down_bias = params
    first = low(normalize(inputs, first_gain, first_shift))
    queries = low(low_back(matmul(first, query_weight) + query_bias))
    keys = low(low_back(matmul(first, key_weight)))
    values = low(low_back(matmul(first, value_weight) + value_bias))
    attended = low(low_back(attention(queries, keys, values, scenes)))
    hidden = inputs + low_back(matmul(attended, output_weight) + output_bias)
    second = low(normalize(hidden, second_gain, second_shift))
    inner = low_back(matmul(second, up_weight) + up_bias)
    active = low(jax.nn.gelu(inner, approximate=False))
    return hidden + low_back(matmul(active, down_weight) + down_bias)

def reference(tokens, scene_ids, query_weight, query_bias, key_weight, value_weight, value_bias, output_weight, output_bias, first_gain, first_shift, second_gain, second_shift, up_weight, up_bias, down_weight, down_bias, cotangent):
    params = tuple((item.astype(jnp.float32) for item in (query_weight, query_bias, key_weight, value_weight, value_bias, output_weight, output_bias, first_gain, first_shift, second_gain, second_shift, up_weight, up_bias, down_weight, down_bias)))
    group = math.gcd(SEQUENCES, max(1, 4096 // LENGTH))
    count = SEQUENCES // group
    inputs = tokens.astype(jnp.float32).reshape(count, group, LENGTH, D)
    scenes = scene_ids.reshape(count, group, LENGTH)
    grads_in = cotangent.astype(jnp.float32).reshape(count, group, LENGTH, D)

    def one_group(totals, item):
        block_in, block_scenes, block_grad = item
        result, pull = jax.vjp(lambda values, weights: layer(values, weights, block_scenes), block_in, params)
        grad_values, grad_weights = pull(block_grad)
        totals = tuple((left + right for left, right in zip(totals, grad_weights)))
        return (totals, (result.astype(jnp.bfloat16), grad_values.astype(jnp.bfloat16)))
    zeros = tuple((jnp.zeros_like(item) for item in params))
    totals, (outputs, grads) = lax.scan(one_group, zeros, (inputs, scenes, grads_in))
    layer_out = outputs.reshape(SEQUENCES, LENGTH, D)
    tokens_grad = grads.reshape(SEQUENCES, LENGTH, D)
    return (layer_out, tokens_grad, totals[0], totals[1], totals[2], totals[3], totals[4], totals[5], totals[6], totals[7], totals[8], totals[9], totals[10], totals[11], totals[12], totals[13], totals[14])
```

```python
from functools import partial

import jax
import jax.numpy as jnp
from jax import lax
from jax.experimental import pallas as pl
from jax.experimental.pallas import tpu as pltpu
from jax.sharding import PartitionSpec as P

HEAD = 64
PAIR = 2 * HEAD
EPS = 1e-05
FLOOR = -1e30
MESH = pl.DeviceIdType.MESH
BF = jnp.bfloat16
F32 = jnp.float32
NT = (((1,), (1,)), ((), ()))
TN = (((0,), (0,)), ((), ()))
STEP = 32
TILE = 256
MATRICES = 8
LARGE = ("tokens", "wq", "wk", "wv", "wo", "wu", "wd", "cotangent")
SMALL = ("qb", "vb", "ob", "g1", "s1", "g2", "s2", "db")
QB, VB, OB, G1, S1, G2, S2, DB, UB = range(9)


def mm(a, b):
    return jnp.dot(a, b, preferred_element_type=F32)


def mm_nt(a, b):
    return lax.dot_general(a, b, NT, preferred_element_type=F32)


def mm_tn(a, b):
    return lax.dot_general(a, b, TN, preferred_element_type=F32)


def scaled_rows(values):
    mean = jnp.mean(values, -1, keepdims=True)
    centred = values - mean
    inverse = lax.rsqrt(jnp.mean(centred * centred, -1, keepdims=True) + EPS)
    return centred * inverse, inverse


def norm_back(grad_norm, scaled, inverse, gain):
    grad_scaled = grad_norm * gain
    mean_grad = jnp.mean(grad_scaled, -1, keepdims=True)
    mean_cross = jnp.mean(grad_scaled * scaled, -1, keepdims=True)
    return inverse * (grad_scaled - mean_grad - scaled * mean_cross)


def low_half(shape):
    return lax.broadcasted_iota(jnp.int32, shape, 1) < HEAD


def fold(values):
    return jnp.sum(values.reshape(values.shape[0] // 8, 8, values.shape[1]), 0)


def window(step, size):
    return pl.ds(step * size if isinstance(step, int) else pl.multiple_of(step * size, size), size)


def loop(count, body, first=0, unroll=1):
    unroll = min(unroll, count - first)
    while (count - first) % max(unroll, 1):
        unroll -= 1

    def one(step, carry):
        for inner in range(unroll):
            body(first + step * unroll + inner)
        return carry

    if unroll and unroll == count - first:
        one(0, 0)
    elif unroll:
        lax.fori_loop(0, (count - first) // unroll, one, 0)


class Chain:
    def __init__(self, me, blocks, stride):
        self.stride = stride
        self.count = blocks // stride
        self.place = me // stride
        self.me = me

    def device(self, side):
        return {"blk": self.me + (self.stride if side else -self.stride)}

    def has(self, side, steps=1):
        if side:
            return self.place + steps < self.count
        return self.place - steps >= 0

    def visit(self, number):
        rights, lefts = self.count - 1 - self.place, self.place
        both = jnp.minimum(rights, lefts)
        paired = number < 2 * both
        side = jnp.where(paired, 1 - number % 2, jnp.where(rights > lefts, 1, 0))
        index = jnp.where(paired, number // 2, number - both)
        return jnp.where(side == 1, self.count - 1 - index, index), side


class Plan:
    def __init__(self):
        self.now = 0.0
        self.busy = {}

    def work(self, microseconds):
        self.now += microseconds

    def send(self, link, size, hops=1):
        fast = link == ("dp", 1)
        length = size / 5e5 if fast else hops * 2 * size / 1e5
        end = max(self.now, self.busy.get(link, 0.0)) + length
        self.busy[link] = end
        return end + 1.5


class Sum:
    def __init__(self, plan, held, landing, last, out, send_sems, recv_sems, free_sems, out_sem, bits):
        self.plan, self.held, self.landing, self.last = plan, held, landing, last
        self.out, self.send_sems, self.recv_sems, self.out_sem = out, send_sems, recv_sems, out_sem
        self.free_sems = free_sems
        start, base, wholes = 0, 0, 0
        self.stages = []
        undo = []
        for (axis, bit), (rows, halve) in zip(bits, halving(held.shape[0], len(bits)), strict=True):
            mine = lax.axis_index(axis)
            value = lax.rem(mine // bit, 2)
            partner = {axis: mine + bit * (1 - 2 * value)}
            link = (axis, bit)
            if halve:
                keep, give = start + value * rows, start + (1 - value) * rows
                self.stages.append(("halve", partner, give, keep, rows, base, link))
                undo.append(("back", partner, keep, give, rows, base, link))
                base += rows
                start = keep
            else:
                self.stages.append(("whole", partner, start, start, rows, wholes, link))
                wholes += 1
        self.stages += undo[::-1]
        self.done = -1
        self.ends = 0.0

    def settle(self):
        return pltpu.make_async_copy(self.held, self.out, self.out_sem)

    def copy(self, number):
        kind, partner, source, keep, rows, base, _ = self.stages[number]
        at = pl.ds(pl.multiple_of(source, 16), rows)
        src = self.held.at[at]
        if kind == "halve":
            dst = self.landing.at[pl.ds(base, rows)]
        elif kind == "whole":
            dst = self.last.at[base, pl.ds(0, rows)]
        else:
            dst = src
        return pltpu.make_async_remote_copy(
            src_ref=src,
            dst_ref=dst,
            send_sem=self.send_sems.at[number],
            recv_sem=self.recv_sems.at[number],
            device_id=partner,
            device_id_type=MESH,
        )

    def arrival(self, number):
        kind, partner, source, keep, rows, base, _ = self.stages[number]
        if kind != "back":
            return self.copy(number)
        ref = self.held.at[pl.ds(pl.multiple_of(keep, 16), rows)]
        return pltpu.make_async_remote_copy(
            src_ref=ref,
            dst_ref=ref,
            send_sem=self.send_sems.at[number],
            recv_sem=self.recv_sems.at[number],
            device_id=partner,
            device_id_type=MESH,
        )

    def start(self):
        self.begin(0)

    def begin(self, number):
        self.done = number
        if self.stages[number][0] == "back":
            pl.semaphore_wait(self.free_sems.at[len(self.stages) - 1 - number], 1)
        self.copy(number).start()
        rows, (axis, bit) = self.stages[number][4], self.stages[number][6]
        far = axis == "blk" and bit > 1
        link = ("blk", 1) if axis == "blk" else (axis, bit)
        self.ends = self.plan.send(link, rows * self.held.shape[1] * 2, 2 if far else 1)

    @property
    def active(self):
        return 0 <= self.done < len(self.stages)

    @property
    def over(self):
        return self.done == len(self.stages)

    def step(self):
        number = self.done
        kind, partner, source, keep, rows, base, _ = self.stages[number]
        self.copy(number).wait_send()
        if kind == "halve":
            pl.semaphore_signal(self.free_sems.at[number], inc=1, device_id=partner, device_id_type=MESH)
        self.arrival(number).wait_recv()
        self.plan.now = max(self.plan.now, self.ends)
        if kind != "back":
            block = 48 if rows % 48 == 0 else 16

            def add(step):
                at = pl.ds(pl.multiple_of(keep + step * block, 16), block)
                if kind == "halve":
                    came = self.landing[pl.ds(pl.multiple_of(base + step * block, 16), block)]
                else:
                    came = self.last[base, pl.ds(pl.multiple_of(step * block, 16), block)]
                self.held[at] = (self.held[at].astype(F32) + came.astype(F32)).astype(BF)

            loop(rows // block, add, unroll=2)
            self.plan.work(0.2 + rows * 0.001)
        if number + 1 < len(self.stages):
            self.begin(number + 1)
        else:
            self.done = number + 1
            self.settle().start()


class VectorSum:
    def __init__(self, plan, held, landing, send_sems, recv_sems, bits):
        self.plan, self.held, self.landing = plan, held, landing
        self.send_sems, self.recv_sems = send_sems, recv_sems
        self.partners = []
        for axis, bit in bits:
            mine = lax.axis_index(axis)
            self.partners.append({axis: mine + bit * (1 - 2 * lax.rem(mine // bit, 2))})
        self.done = -1
        self.ends = 0.0

    def copy(self, number):
        return pltpu.make_async_remote_copy(
            src_ref=self.held,
            dst_ref=self.landing.at[number],
            send_sem=self.send_sems.at[number],
            recv_sem=self.recv_sems.at[number],
            device_id=self.partners[number],
            device_id_type=MESH,
        )

    def start(self):
        self.begin(0)

    def begin(self, number):
        self.done = number
        self.copy(number).start()
        self.ends = self.plan.now + 2.5

    @property
    def active(self):
        return 0 <= self.done < len(self.partners)

    def step(self):
        self.copy(self.done).wait()
        self.plan.now = max(self.plan.now, self.ends)
        self.held[...] = self.held[...] + self.landing[self.done]
        if self.done + 1 < len(self.partners):
            self.begin(self.done + 1)
        else:
            self.done += 1


def landing_slot(matrix, blocks):
    return matrix if blocks <= 4 or matrix < 5 else matrix - 4


def halving(rows, bits):
    plan = []
    for position in range(bits):
        halve = rows % 32 == 0 and position < bits - 1
        if halve:
            rows //= 2
        plan.append((rows, halve))
    return plan


def axis_bits(axis, size):
    return [(axis, 1 << bit) for bit in range(size.bit_length() - 1)]


def layer_kernel(blocks, groups, names, *refs):
    r = dict(zip(names, refs, strict=True))
    tokens_in, scenes, cot_in = r["tokens"], r["scenes"], r["cotangent"]
    small = {name: r["rows"].at[n : n + 1] for n, name in enumerate(SMALL)} | {"ub": r["ub_v"]}
    qb, vb, ob, g1, s1, g2, s2, db, ub = (small[name] for name in SMALL + ("ub",))
    flt = r["flt"]
    xg, k_all, v_all, qst, gst = r["xg"], r["k_all"], r["v_all"], r["qst"], r["gst"]
    m, l, lse, delta, ot, att = r["m"], r["l"], r["lse"], r["delta"], r["ot"], r["att"]
    held, hidden = r["held"], r["hidden"]
    vacc, vub = r["vacc"], r["vub"]
    seqs, rows, width = tokens_in.shape
    inner_width = ub.shape[1]
    pairs = width // PAIR
    me = lax.axis_index("blk")
    chains = [Chain(me, blocks, 1), Chain(me, blocks, 2)]
    bases = [0, blocks]
    own = [chains[0].place, blocks + chains[1].place]
    mate = me + 1 - 2 * lax.rem(me, 2)
    dp_bits, blk_bits = axis_bits("dp", groups), axis_bits("blk", blocks)

    vector_loads = []
    for number, name in enumerate(SMALL + ("ub",)):
        place = r["ub_v"].at[0] if name == "ub" else r["rows"].at[number]
        vector_loads.append(pltpu.make_async_copy(r[name], place, r["small_sems"].at[number]))
        vector_loads[-1].start()
    loads = {}
    for number, name in enumerate(LARGE):
        place = r["cot_v"] if name in ("tokens", "cotangent") else r[name + "_v"]
        loads[name] = pltpu.make_async_copy(r[name], place, r["load_sems"].at[number])
        if name != "cotangent":
            loads[name].start()
    tokens = cot = r["cot_v"]
    wq, wk, wv, wo, wu, wd = (r[n + "_v"] for n in ("wq", "wk", "wv", "wo", "wu", "wd"))

    barrier = pltpu.get_barrier_semaphore()
    total = 0
    for chain in chains:
        for side in (0, 1):

            @pl.when(chain.has(side))
            def _():
                pl.semaphore_signal(barrier, inc=1, device_id=chain.device(side), device_id_type=MESH)

            total = total + chain.has(side).astype(jnp.int32)
    for axis, bit in dp_bits + blk_bits:
        mine = lax.axis_index(axis)
        partner = {axis: mine + bit * (1 - 2 * lax.rem(mine // bit, 2))}
        pl.semaphore_signal(barrier, inc=1, device_id=partner, device_id_type=MESH)
        total = total + 1
    pl.semaphore_wait(barrier, total)

    swap = pltpu.make_async_remote_copy(
        src_ref=scenes,
        dst_ref=r["theirs"],
        send_sem=r["scene_sems"].at[0],
        recv_sem=r["scene_sems"].at[1],
        device_id={"blk": mate},
        device_id_type=MESH,
    )
    swap.start()
    for load in vector_loads:
        load.wait()
    loads["tokens"].wait()
    swap.wait()
    ordered = jnp.where(scenes[0:1, 0:1] == r["theirs"][0:1, 0:1], 1.0, 0.0)

    def sort(first, second):
        w = jnp.broadcast_to(ordered, first.shape)
        return w * first + (1.0 - w) * second, w * second + (1.0 - w) * first

    def place_rows(step):
        at = window(step, STEP)
        first, second = sort(tokens[0, at, :].astype(F32), tokens[1, at, :].astype(F32))
        xg[own[0], at, :] = first.astype(BF)
        xg[own[1], at, :] = second.astype(BF)

    loop(rows // STEP, place_rows, unroll=4)
    loads["cotangent"].start()

    def passing(which, side, step, slot):
        return pltpu.make_async_remote_copy(
            src_ref=xg.at[bases[which] + slot],
            dst_ref=xg.at[bases[which] + slot],
            send_sem=r["x_send"].at[which, side, step],
            recv_sem=r["x_recv"].at[which, 1 - side, step],
            device_id=chains[which].device(side),
            device_id_type=MESH,
        )

    for which in (0, 1):
        for side in (0, 1):

            @pl.when(chains[which].has(side))
            def _():
                passing(which, side, 1, chains[which].place).start()

    loads["wq"].wait()
    loads["wk"].wait()
    loads["wv"].wait()

    def project(which, slot, fl, with_queries):
        index = bases[which] + slot

        def norm_rows(step):
            at = window(step, STEP)
            scaled, _ = scaled_rows(xg[index, at, :].astype(F32))
            fl[at, :] = (scaled * g1[...] + s1[...]).astype(BF)

        loop(rows // STEP, norm_rows, unroll=4)

        def columns(step):
            at = window(step, TILE)
            left = fl[...]
            keys = mm(left, wk[:, at]).astype(BF)
            values = (mm(left, wv[:, at]) + vb[:, at]).astype(BF)
            for half in range(2):
                lanes = slice(half * PAIR, (half + 1) * PAIR)
                k_all[2 * step + half, index] = keys[:, lanes]
                v_all[2 * step + half, index] = values[:, lanes]
            flt[at, window(index, rows)] = jnp.transpose(fl[:, at])
            if with_queries:
                queries = (mm(left, wq[:, at]) + qb[:, at]).astype(BF).astype(F32) * HEAD**-0.5
                for half in range(2):
                    part = queries[:, half * PAIR : (half + 1) * PAIR]
                    low = low_half(part.shape)
                    qst[which, 2 * step + half, 0:rows] = jnp.where(low, part, 0.0).astype(BF)
                    qst[which, 2 * step + half, rows : 2 * rows] = jnp.where(low, 0.0, part).astype(BF)

        loop(width // TILE, columns, unroll=3)

    def attend(which, slot):
        index = bases[which] + slot

        def pair_step(pair):
            s = mm_nt(k_all[pair, index], qst[which, pair])
            before = m[which, pair]
            now = jnp.maximum(before, jnp.max(s, axis=0, keepdims=True))
            e = jnp.exp(s - now)
            decay = jnp.exp(before - now)
            m[which, pair] = now
            l[which, pair] = l[which, pair] * decay + jnp.sum(e, axis=0, keepdims=True)
            low = e.astype(BF)
            vt = jnp.transpose(v_all[pair, index])
            for head in range(2):
                feats = slice(head * HEAD, (head + 1) * HEAD)
                cols = slice(head * rows, (head + 1) * rows)
                ot[which, pair, feats] = ot[which, pair, feats] * decay[:, cols] + mm(vt[feats], low[:, cols])

        loop(pairs, pair_step, unroll=3)

    def attention_forward(fl):
        m[...] = jnp.full(m.shape, FLOOR, F32)
        l[...] = jnp.zeros(l.shape, F32)
        ot[...] = jnp.zeros(ot.shape, F32)
        def receive(which, step):
            chain = chains[which]
            for side in (0, 1):

                @pl.when(chain.has(side, step))
                def _():
                    slot = chain.place + (step if side else -step)
                    passing(which, 1 - side, step, slot).wait_recv()

                    @pl.when(chain.has(1 - side))
                    def _():
                        passing(which, 1 - side, step + 1, slot).start()

        def use(which, step, side):
            chain = chains[which]

            @pl.when(chain.has(side, step))
            def _():
                slot = chain.place + (step if side else -step)
                project(which, slot, fl, False)
                attend(which, slot)

        project(0, chains[0].place, fl, True)
        attend(0, chains[0].place)
        project(1, chains[1].place, fl, True)
        receive(0, 1)
        attend(1, chains[1].place)

        def alternate(step):
            receive(1, step)
            use(1, step, 0)
            use(1, step, 1)

        loop(chains[1].count, alternate, 1)

        def single(step):
            use(0, step, 0)

            @pl.when(step + 1 < chains[0].count)
            def _():
                receive(0, step + 1)

            use(0, step, 1)

        loop(chains[0].count, single, 1)

        for which in (0, 1):

            def finish(pair):
                total = l[which, pair]
                lse[which, pair] = m[which, pair] + jnp.log(total)
                share = 1.0 / total
                for head in range(2):
                    feats = slice(head * HEAD, (head + 1) * HEAD)
                    cols = slice(head * rows, (head + 1) * rows)
                    ot[which, pair, feats] = ot[which, pair, feats] * share[:, cols]
                att[which, pair] = jnp.transpose(ot[which, pair])

            loop(pairs, finish, unroll=3)

        for which in (0, 1):
            chain = chains[which]

            def sent(step):
                for side in (0, 1):
                    @pl.when(jnp.logical_and(chain.has(side), chain.has(1 - side, step - 1)))
                    def _():
                        passing(which, side, step, chain.place + (1 - step if side else step - 1)).wait_send()

            loop(chain.count, sent, 1)

    pl.run_scoped(attention_forward, pltpu.VMEM((rows, width), BF))

    plan = Plan()
    places = [(number, 0, width) for number in range(MATRICES - 1)]
    places += [(MATRICES - 1, half * width // 2, width // 2) for half in (0, 1)]
    sums = []
    wholes = 0
    for number, (matrix, start, size) in enumerate(places):
        rest = dp_bits[1:]
        bits = dp_bits[:1] + (rest if number % 2 == 0 else rest[::-1]) + blk_bits
        halves = halving(size, len(bits))
        count = sum(not halve for _, halve in halves)
        space = r["landing"].shape[1] // 2 if size < width else r["landing"].shape[1]
        slot = landing_slot(matrix, blocks)
        sums.append(
            Sum(
                plan,
                held.at[matrix, pl.ds(start, size)],
                r["landing"].at[slot, pl.ds(space if start else 0, space)],
                r["last"].at[pl.ds(wholes, count)],
                r["sums"].at[matrix, pl.ds(start, size)],
                r["sum_send"].at[number],
                r["sum_recv"].at[number],
                r["sum_free"].at[number],
                r["sum_out"].at[number],
                bits,
            )
        )
        wholes += count
    vector_sum = VectorSum(
        plan, r["vectors"], r["vector_landing"], r["vector_send"], r["vector_recv"], dp_bits + blk_bits
    )

    def pump(microseconds=0.0):
        plan.work(microseconds)
        for s in sums + [vector_sum]:
            if s.active and s.ends <= plan.now:
                s.step()

    def begin(number):
        slot = landing_slot(places[number][0], blocks)
        for other in range(number):
            if landing_slot(places[other][0], blocks) == slot and places[other][0] != places[number][0]:
                while not sums[other].over:
                    min((s for s in sums if s.active), key=lambda s: s.ends).step()
        sums[number].start()

    vacc[...] = jnp.zeros(vacc.shape, F32)
    vub[...] = jnp.zeros(vub.shape, F32)
    both = seqs * rows
    halves = [slice(0, rows), slice(rows, both)]

    def feed_forward(alow, slow, active, ginner, gbranch):
        loads["wo"].wait()
        loads["cotangent"].wait()

        def sort_rows(step):
            at = window(step, STEP)
            first, second = sort(cot[0, at, :].astype(F32), cot[1, at, :].astype(F32))
            vacc[DB] += fold(first) + fold(second)
            cot[0, at, :] = first.astype(BF)
            cot[1, at, :] = second.astype(BF)

        loop(rows // STEP, sort_rows, unroll=4)

        def join_heads(pair):
            at = window(pair, PAIR)
            for which in (0, 1):
                alow[halves[which], at] = att[which, pair].astype(BF)

        loop(pairs, join_heads, unroll=3)

        def branch(step):
            at = window(step, TILE)
            for which in (0, 1):
                here = halves[which]
                hidden[here, at] = xg[own[which], :, at].astype(F32) + (mm(alow[here, :], wo[:, at]) + ob[:, at])

        loop(width // TILE, branch, unroll=3)

        def norm_rows(step):
            at = window(step, STEP)
            scaled, _ = scaled_rows(hidden[at, :])
            slow[at, :] = (scaled * g2[...] + s2[...]).astype(BF)

        loop(both // STEP, norm_rows, unroll=4)
        loads["wu"].wait()
        loads["wd"].wait()

        for part in (0, 1):

            def up(step):
                block = part * (width // TILE) + step
                at = window(block, TILE)
                for which in (0, 1):
                    here = halves[which]
                    inner = mm(slow[here, :], wu[:, at]) + ub[:, at]
                    grad_active = mm_nt(cot[which], wd[at, :])
                    share = 0.5 * (1.0 + lax.erf(inner * (0.5**0.5)))
                    slope = share + inner * (jnp.exp(-0.5 * inner * inner) * 0.3989422804014327)
                    active[here, at] = (inner * share).astype(BF)
                    low = (grad_active * slope).astype(BF)
                    ginner[here, at] = low
                    vub[:, at] += fold(low.astype(F32))
                held[2 * part, window(step, TILE), :] = mm_tn(active[:, at], cot[...].reshape(both, width)).astype(BF)

            for step in range(width // TILE):
                up(step)
                pump(1.8)
            begin(2 * part)

            def up_weights(step):
                at = window(step, TILE)
                held[2 * part + 1, at, :] = mm_tn(slow[:, at], ginner[:, part * width : (part + 1) * width]).astype(BF)

            loop(width // TILE, up_weights, unroll=3)
            plan.work(1.2)
            begin(2 * part + 1)
            pump()

        def down(step):
            at = window(step, TILE)
            ys = [hidden[here, at] + (mm(active[here, :], wd[:, at]) + db[:, at]) for here in halves]
            first, second = sort(*ys)
            slow[halves[0], at] = first.astype(BF)
            slow[halves[1], at] = second.astype(BF)

        loop(width // TILE, down, unroll=3)
        pump(2.0)
        layer_out = [
            pltpu.make_async_copy(slow.at[halves[n]], r["layer_out"].at[n], r["out_sems"].at[n]) for n in (0, 1)
        ]
        for copy in layer_out:
            copy.start()

        def second_back(step):
            at = window(step, TILE)
            for which in (0, 1):
                back = mm_nt(ginner[halves[which], :], wu[at, :])
                for part in range(rows // PAIR):
                    ot[which, part * (width // TILE) + step] = back[part * PAIR : (part + 1) * PAIR]

        loop(width // TILE, second_back, unroll=3)
        pump(2.0)

        def hidden_back(which, step):
            rows_at = window(step, STEP)
            at = window(which * (rows // STEP) + step, STEP)
            scaled, inverse = scaled_rows(hidden[at, :])
            inside = window(lax.rem(step, PAIR // STEP), STEP)
            block = step // (PAIR // STEP) * (width // TILE)
            grad = jnp.concatenate([ot[which, block + part, inside, :] for part in range(width // TILE)], 1)
            vacc[G2] += fold(grad * scaled)
            vacc[S2] += fold(grad)
            grad_hidden = cot[which, rows_at, :].astype(F32) + norm_back(grad, scaled, inverse, g2[...])
            hidden[at, :] = grad_hidden
            low = grad_hidden.astype(BF)
            gbranch[at, :] = low
            vacc[OB] += fold(low.astype(F32))

        for which in (0, 1):
            loop(rows // STEP, partial(hidden_back, which), unroll=2)
            pump(0.7)

        def output_weights(step):
            at = window(step, TILE)
            held[4, at, :] = mm_tn(alow[:, at], gbranch[...]).astype(BF)

        loop(width // TILE, output_weights, unroll=3)
        plan.work(1.2)
        begin(4)

        def branch_back(step):
            at = window(step, TILE)
            for which in (0, 1):
                low = mm_nt(gbranch[halves[which], :], wo[at, :]).astype(BF).astype(F32)
                for half in range(2):
                    pair = 2 * step + half
                    part = low[:, half * PAIR : (half + 1) * PAIR]
                    lower = low_half(part.shape)
                    gst[which, pair, 0:rows] = jnp.where(lower, part, 0.0).astype(BF)
                    gst[which, pair, rows : 2 * rows] = jnp.where(lower, 0.0, part).astype(BF)
                    product = jnp.transpose(part * att[which, pair])
                    delta[which, pair, :, 0:rows] = jnp.sum(product[0:HEAD], 0, keepdims=True)
                    delta[which, pair, :, rows : 2 * rows] = jnp.sum(product[HEAD:PAIR], 0, keepdims=True)

        loop(width // TILE, branch_back, unroll=3)
        pump(2.0)
        for copy in layer_out:
            copy.wait()

    pl.run_scoped(
        feed_forward,
        pltpu.VMEM((both, width), BF),
        pltpu.VMEM((both, width), BF),
        pltpu.VMEM((both, inner_width), BF),
        pltpu.VMEM((both, inner_width), BF),
        pltpu.VMEM((both, width), BF),
    )

    ot[...] = jnp.zeros(ot.shape, F32)
    grad_in, grad_out = r["grad_in"], xg
    in_bases = [0, blocks + 1]

    def returning(which, side, slot):
        chain = chains[which]
        arrives = jnp.logical_and(slot == chain.place + (1 if side else -1), side == 0)
        index = in_bases[which] + jnp.where(arrives, chain.count, slot)
        return pltpu.make_async_remote_copy(
            src_ref=grad_out.at[bases[which] + slot],
            dst_ref=grad_in.at[index],
            send_sem=r["g_send"].at[which, slot],
            recv_sem=r["g_recv"].at[index],
            device_id=chain.device(side),
            device_id_type=MESH,
        )

    def arrived(which, side, slot):
        index = in_bases[which] + jnp.where(jnp.logical_and(slot == chains[which].place, side == 0), chains[which].count, slot)
        ref = grad_in.at[index]
        pltpu.make_async_remote_copy(
            src_ref=ref,
            dst_ref=ref,
            send_sem=r["g_send"].at[which, 0],
            recv_sem=r["g_recv"].at[index],
            device_id={"blk": mate},
            device_id_type=MESH,
        ).wait_recv()
        return index

    def attention_backward(grad):
        dq = cot

        def pair_back(which, index, pair):
            k, v, q, g = k_all[pair, index], v_all[pair, index], qst[which, pair], gst[which, pair]
            p = jnp.exp(mm_nt(k, q) - lse[which, pair])
            low = (p * (mm_nt(v, g) - delta[which, pair])).astype(BF)
            value_grad = mm(p.astype(BF), g)
            vacc[VB, :, window(pair, PAIR)] += fold(value_grad)
            v_all[pair, index] = value_grad.astype(BF)
            k_all[pair, index] = mm(low, q).astype(BF)
            kt = jnp.transpose(k)
            for head in range(2):
                feats = slice(head * HEAD, (head + 1) * HEAD)
                ot[which, pair, feats] += mm(kt[feats], low[:, head * rows : (head + 1) * rows])

        def slot_back(which, index, group):
            for pair in group:
                pair_back(which, index, pair)
                pump(1.1)

        def joined(values, index):
            return jnp.concatenate([values[pair, index] for pair in range(pairs)], 1)

        def give(which, number):
            chain = chains[which]
            slot, side = chain.visit(number)
            index = bases[which] + slot

            def first_back(step):
                at = window(step, TILE)
                grad[0:rows, at] = mm_nt(joined(k_all, index), wk[at, :]) + mm_nt(joined(v_all, index), wv[at, :])

            loop(width // TILE, first_back, unroll=3)

            def gather_rows(step):
                at = window(step, STEP)
                scaled, _ = scaled_rows(xg[index, at, :].astype(F32))
                values = grad[at, :]
                vacc[G1] += fold(values * scaled)
                vacc[S1] += fold(values)
                grad_out[index, at, :] = values.astype(BF)

            loop(rows // STEP, gather_rows, unroll=2)
            for toward in (0, 1):

                @pl.when(jnp.logical_and(side == toward, jnp.logical_not(chain.has(1 - toward))))
                def _():
                    returning(which, toward, slot).start()

            plan.send(("blk", 1), rows * width * 2)
            pump(1.8)

        def relay(which, number):
            chain = chains[which]
            slot, side = chain.visit(number)
            for toward in (0, 1):

                @pl.when(jnp.logical_and(side == toward, chain.has(1 - toward)))
                def _():
                    place = arrived(which, toward, slot)

                    def add(step):
                        at = window(step, STEP)
                        out = bases[which] + slot
                        grad_out[out, at, :] = (
                            grad_out[out, at, :].astype(F32) + grad_in[place, at, :].astype(F32)
                        ).astype(BF)

                    loop(rows // STEP, add, unroll=4)
                    returning(which, toward, slot).start()

            pump(0.3)

        def other(which, number):
            return bases[which] + chains[which].visit(number)[0]

        def query_rows(which, pair):
            value = jnp.transpose(ot[which, pair]) * HEAD**-0.5
            vacc[QB, :, window(pair, PAIR)] += fold(value)
            dq[which, :, window(pair, PAIR)] = value.astype(BF)

        def weights(group, step):
            at = window(step, TILE)
            number = 5 + group
            pair = 2 * group
            flat = (k_all.shape[1] * rows, PAIR)
            right = jnp.concatenate(
                [k_all[pair].reshape(flat), k_all[pair + 1].reshape(flat)]
                + [v_all[pair].reshape(flat), v_all[pair + 1].reshape(flat)],
                1,
            )
            held[number, at, TILE : 3 * TILE] = mm(flt[at, :], right).astype(BF)
            columns = window(group, TILE)
            held[number, at, 0:TILE] = sum(
                mm(flt[at, window(own[which], rows)], dq[which, :, columns]) for which in (0, 1)
            ).astype(BF)

        groups_of_heads = [(2 * group, 2 * group + 1) for group in range(pairs // 2)]
        alternate = [(1, n) for n in range(chains[1].count - 1)]
        singles = [(0, n) for n in range(chains[0].count - 1)]
        for which, number in alternate:
            slot_back(which, other(which, number), range(pairs))
            give(which, number)
        slot_back(1, own[1], range(pairs))
        waiting = list(alternate)
        for pair in range(pairs):
            query_rows(1, pair)
        for group, members in enumerate(groups_of_heads):
            final = group == len(groups_of_heads) - 1
            for which, number in singles:
                slot_back(which, other(which, number), members)
                if final:
                    give(which, number)
                    waiting.append((which, number))
                    if len(waiting) > 1:
                        relay(*waiting.pop(0))
            if not final and waiting:
                relay(*waiting.pop(0))
            slot_back(0, own[0], members)
            for pair in members:
                query_rows(0, pair)
            for step in range(width // TILE):
                weights(group, step)
                pump(0.8)
                if final and step == (width // TILE) // 2:
                    begin(7)
            begin(8 if final else 5 + group)
            pump()
        for item in waiting:
            relay(*item)

        def first_back(step):
            at = window(step, TILE)
            for which in (0, 1):
                grad[halves[which], at] = (
                    mm_nt(joined(k_all, own[which]), wk[at, :])
                    + mm_nt(joined(v_all, own[which]), wv[at, :])
                    + mm_nt(dq[which], wq[at, :])
                )

        loop(width // TILE, first_back, unroll=3)
        pump(2.5)
        for which in (0, 1):

            def own_rows(step):
                at = window(step, STEP)
                to = window(which * (rows // STEP) + step, STEP)
                scaled, _ = scaled_rows(xg[own[which], at, :].astype(F32))
                values = grad[to, :]
                vacc[G1] += fold(values * scaled)
                vacc[S1] += fold(values)

            loop(rows // STEP, own_rows, unroll=2)

        vectors = r["vectors"]
        vectors[...] = jnp.zeros(vectors.shape, F32)
        for number in range(UB):
            vectors[number : number + 1, :] = jnp.sum(vacc[number], 0, keepdims=True)
        for part in range(inner_width // width):
            vectors[UB + part : UB + part + 1, :] = jnp.sum(vub[:, part * width : (part + 1) * width], 0, keepdims=True)
        vector_sum.start()
        pump(1.0)

        def drain(until):
            while True:
                left = [s for s in sums + [vector_sum] if s.active]
                if not left or min(s.ends for s in left) > until:
                    return
                min(left, key=lambda s: s.ends).step()

        drain(plan.busy.get(("blk", 1), 0.0))
        for which in (0, 1):
            for side in (0, 1):

                @pl.when(chains[which].has(1 - side))
                def _():
                    place = arrived(which, side, chains[which].place)

                    def add(step):
                        to = window(which * (rows // STEP) + step, STEP)
                        grad[to, :] += grad_in[place, window(step, STEP), :].astype(F32)

                    loop(rows // STEP, add, unroll=4)

        pump(0.8)

        def tokens_back(step):
            at = window(step, STEP)
            parts = []
            for which in (0, 1):
                to = window(which * (rows // STEP) + step, STEP)
                scaled, inverse = scaled_rows(xg[own[which], at, :].astype(F32))
                parts.append(hidden[to, :] + norm_back(grad[to, :], scaled, inverse, g1[...]))
            first, second = sort(*parts)
            cot[0, at, :] = first.astype(BF)
            cot[1, at, :] = second.astype(BF)

        loop(rows // STEP, tokens_back, unroll=2)
        tokens_out = pltpu.make_async_copy(cot, r["tokens_grad"], r["out_sems"].at[2])
        tokens_out.start()
        pump(1.0)

        for which, number in alternate + singles:
            slot, side = chains[which].visit(number)
            for toward in (0, 1):

                @pl.when(side == toward)
                def _():
                    returning(which, toward, slot).wait_send()

        drain(float("inf"))
        for s in sums:
            s.settle().wait()
        tokens_out.wait()

    pl.run_scoped(attention_backward, pltpu.VMEM((both, width), F32))


def run_layer(operands):
    blocks, groups = lax.axis_size("blk"), lax.axis_size("dp")
    seqs, rows, width = operands["tokens"].shape
    inner = operands["ub"].shape[0]
    pairs = width // PAIR
    slots = blocks + blocks // 2
    bits = (blocks * groups).bit_length() - 1
    plans = [halving(width, bits)] * (MATRICES - 1) + [halving(width // 2, bits)] * 2
    landing = max(
        sum(size for size, halve in plans[0] if halve), 2 * sum(size for size, halve in plans[-1] if halve)
    )
    landing = (landing + 31) // 32 * 32
    wholes = [size for plan in plans for size, halve in plan if not halve]
    landings = 1 + max(landing_slot(matrix, blocks) for matrix in range(MATRICES))
    vmem = pl.BlockSpec(memory_space=pltpu.VMEM)
    hbm = pl.BlockSpec(memory_space=pl.ANY)
    out_shape = {
        "layer_out": jax.ShapeDtypeStruct((seqs, rows, width), BF),
        "tokens_grad": jax.ShapeDtypeStruct((seqs, rows, width), BF),
        "sums": jax.ShapeDtypeStruct((MATRICES, width, width), BF),
        "vectors": jax.ShapeDtypeStruct((16, width), F32),
    }
    dma = pltpu.SemaphoreType.DMA
    scratch = {name + "_v": pltpu.VMEM(operands[name].shape, BF) for name in LARGE if name[0] == "w"}
    scratch |= {
        "cot_v": pltpu.VMEM((seqs, rows, width), BF),
        "rows": pltpu.VMEM((len(SMALL), width), F32),
        "ub_v": pltpu.VMEM((1, inner), F32),
        "small_sems": dma((len(SMALL) + 1,)),
        "theirs": pltpu.VMEM((seqs, rows), jnp.int32),
        "xg": pltpu.VMEM((slots, rows, width), BF),
        "flt": pltpu.VMEM((width, slots * rows), BF),
        "k_all": pltpu.VMEM((pairs, slots, rows, PAIR), BF),
        "v_all": pltpu.VMEM((pairs, slots, rows, PAIR), BF),
        "qst": pltpu.VMEM((seqs, pairs, 2 * rows, PAIR), BF),
        "gst": pltpu.VMEM((seqs, pairs, 2 * rows, PAIR), BF),
        "m": pltpu.VMEM((seqs, pairs, 1, 2 * rows), F32),
        "l": pltpu.VMEM((seqs, pairs, 1, 2 * rows), F32),
        "lse": pltpu.VMEM((seqs, pairs, 1, 2 * rows), F32),
        "delta": pltpu.VMEM((seqs, pairs, 1, 2 * rows), F32),
        "ot": pltpu.VMEM((seqs, pairs, PAIR, rows), F32),
        "att": pltpu.VMEM((seqs, pairs, rows, PAIR), F32),
        "hidden": pltpu.VMEM((seqs * rows, width), F32),
        "vacc": pltpu.VMEM((UB, 8, width), F32),
        "vub": pltpu.VMEM((8, inner), F32),
        "held": pltpu.VMEM((MATRICES, width, width), BF),
        "landing": pltpu.VMEM((landings, landing, width), BF),
        "last": pltpu.VMEM((len(wholes), max(wholes), width), BF),
        "vector_landing": pltpu.VMEM((bits, 16, width), F32),
        "grad_in": pltpu.VMEM((slots + 2, rows, width), BF),
        "out_sems": dma((3,)),
        "load_sems": dma((len(LARGE),)),
        "scene_sems": dma((2,)),
        "x_send": dma((2, 2, blocks + 1)),
        "x_recv": dma((2, 2, blocks + 1)),
        "g_send": dma((2, blocks)),
        "g_recv": dma((slots + 2,)),
        "sum_send": dma((len(plans), 2 * bits)),
        "sum_recv": dma((len(plans), 2 * bits)),
        "sum_free": pltpu.SemaphoreType.REGULAR((len(plans), bits)),
        "sum_out": dma((len(plans),)),
        "vector_send": dma((bits,)),
        "vector_recv": dma((bits,)),
    }
    names = tuple(operands) + tuple(out_shape) + tuple(scratch)
    return pl.pallas_call(
        partial(layer_kernel, blocks, groups, names),
        out_shape=tuple(out_shape.values()),
        in_specs=[vmem if name == "scenes" else hbm for name in operands],
        out_specs=(hbm, hbm, hbm, vmem),
        scratch_shapes=list(scratch.values()),
        compiler_params=pltpu.CompilerParams(
            collective_id=0, has_side_effects=True, vmem_limit_bytes=int(63.8 * 2**20)
        ),
    )(*operands.values())


def spread_kernel(layer_out, tokens_grad, sums, vectors, *refs):
    outs, (narrow, wide, passed, in_sems, out_sems, pass_sems, vector_sems) = refs[:17], refs[17:]
    down, up, out, query, key, value = outs[2:8]
    width = sums.shape[1]
    half = width // 2
    loads = []
    for number in range(MATRICES):
        for part in range(2):
            at = pl.ds(part * half, half)
            loads.append(
                pltpu.make_async_copy(sums.at[number, at], narrow.at[number, at], in_sems.at[number, part])
            )
            loads[-1].start()
    passing = []
    for n, source in enumerate((layer_out, tokens_grad)):
        passing.append(pltpu.make_async_copy(source, passed.at[n], pass_sems.at[0, n]))
        passing[-1].start()
    stores = [pltpu.make_async_copy(vectors.at[n], outs[8 + n], vector_sems.at[n]) for n in range(UB)]
    for part in range(2):
        target = outs[8 + UB].at[pl.ds(part * width, width)]
        stores.append(pltpu.make_async_copy(vectors.at[UB + part], target, vector_sems.at[UB + part]))
    for store in stores:
        store.start()

    def send(number, part, target):
        at = pl.ds(part * half, half)
        stores.append(pltpu.make_async_copy(wide.at[number, at], target, out_sems.at[number, part]))
        stores[-1].start()

    for number in range(MATRICES):
        for part in range(2):
            loads[2 * number + part].wait()

            def widen(step):
                at = window(part * (half // STEP) + step, STEP)
                if number < 5:
                    wide[number, at] = narrow[number, at].astype(F32)
                else:
                    columns = pl.ds((number - 5) * TILE, TILE)
                    for n in range(3):
                        wide[5 + n, at, columns] = narrow[number, at, n * TILE : (n + 1) * TILE].astype(F32)

            loop(half // STEP, widen, unroll=4)
            at = pl.ds(part * half, half)
            if number in (0, 2):
                send(number, part, down.at[pl.ds(number // 2 * width + part * half, half)])
            elif number in (1, 3):
                send(number, part, up.at[at, pl.ds(number // 2 * width, width)])
            elif number == 4:
                send(number, part, out.at[at])
            elif number == MATRICES - 1:
                for n, matrix in enumerate((query, key, value)):
                    send(5 + n, part, matrix.at[at])
        if number == 4:
            for n in (0, 1):
                passing[n].wait()
                stores.append(pltpu.make_async_copy(passed.at[n], outs[n], pass_sems.at[1, n]))
                stores[-1].start()
    for store in stores:
        store.wait()


def spread(layer_out, tokens_grad, sums, vectors):
    width = sums.shape[1]
    matrices = [(2 * width, width), (width, 2 * width)] + [(width, width)] * 4
    shapes = [jax.ShapeDtypeStruct(value.shape, BF) for value in (layer_out, tokens_grad)]
    shapes += [jax.ShapeDtypeStruct(shape, F32) for shape in matrices + [(width,)] * UB + [(2 * width,)]]
    hbm = pl.BlockSpec(memory_space=pl.ANY)
    return pl.pallas_call(
        spread_kernel,
        out_shape=tuple(shapes),
        in_specs=[hbm, hbm, hbm, pl.BlockSpec(memory_space=pltpu.VMEM)],
        out_specs=(hbm,) * len(shapes),
        scratch_shapes=[
            pltpu.VMEM(sums.shape, BF),
            pltpu.VMEM(sums.shape, F32),
            pltpu.VMEM((2,) + layer_out.shape, BF),
            pltpu.SemaphoreType.DMA((MATRICES, 2)),
            pltpu.SemaphoreType.DMA((MATRICES, 2)),
            pltpu.SemaphoreType.DMA((2, 2)),
            pltpu.SemaphoreType.DMA((UB + 2,)),
        ],
        compiler_params=pltpu.CompilerParams(vmem_limit_bytes=63 * 2**20),
    )(layer_out, tokens_grad, sums, vectors)


def on_device(
    tokens,
    scene_ids,
    query_weight,
    query_bias,
    key_weight,
    value_weight,
    value_bias,
    output_weight,
    output_bias,
    first_gain,
    first_shift,
    second_gain,
    second_shift,
    up_weight,
    up_bias,
    down_weight,
    down_bias,
    cotangent,
):
    operands = {
        "tokens": tokens,
        "scenes": scene_ids,
        "wq": query_weight,
        "wk": key_weight,
        "wv": value_weight,
        "wo": output_weight,
        "wu": up_weight,
        "wd": down_weight,
        "cotangent": cotangent,
        "qb": query_bias,
        "vb": value_bias,
        "ob": output_bias,
        "g1": first_gain,
        "s1": first_shift,
        "g2": second_gain,
        "s2": second_shift,
        "ub": up_bias,
        "db": down_bias,
    }
    (
        layer_out,
        tokens_grad,
        down_grad,
        up_grad,
        output_grad,
        query_grad,
        key_grad,
        value_grad,
        query_bias_grad,
        value_bias_grad,
        output_bias_grad,
        first_gain_grad,
        first_shift_grad,
        second_gain_grad,
        second_shift_grad,
        down_bias_grad,
        up_bias_grad,
    ) = spread(*run_layer(operands))
    return (
        layer_out,
        tokens_grad,
        query_grad,
        query_bias_grad,
        key_grad,
        value_grad,
        value_bias_grad,
        output_grad,
        output_bias_grad,
        first_gain_grad,
        first_shift_grad,
        second_gain_grad,
        second_shift_grad,
        up_grad,
        up_bias_grad,
        down_grad,
        down_bias_grad,
    )


def solution(mesh):
    split = P("dp", "blk", None)
    in_specs = (split, P("dp", "blk")) + (P(),) * 15 + (split,)
    out_specs = (split, split) + (P(),) * 15
    return jax.shard_map(on_device, mesh=mesh, in_specs=in_specs, out_specs=out_specs, check_vma=False)
```

```python
from functools import partial

import jax
import jax.numpy as jnp
from jax import lax
from jax.experimental import pallas as pl
from jax.experimental.pallas import tpu as pltpu
from jax.sharding import PartitionSpec as P

HEAD = 64
PAIR = 2 * HEAD
EPS = 1e-05
FLOOR = -1e30
MESH = pl.DeviceIdType.MESH
BF = jnp.bfloat16
F32 = jnp.float32
NT = (((1,), (1,)), ((), ()))
TN = (((0,), (0,)), ((), ()))
STEP = 32
TILE = 256
MATRICES = 8
PIECES = 1
HOP = 4.0
LARGE = ("tokens", "wq", "wk", "wv", "wo", "wu", "wd", "cotangent")
SMALL = ("qb", "vb", "ob", "g1", "s1", "g2", "s2", "db")
QB, VB, OB, G1, S1, G2, S2, DB, UB = range(9)


def mm(a, b):
    return jnp.dot(a, b, preferred_element_type=F32)


def mm_nt(a, b):
    return lax.dot_general(a, b, NT, preferred_element_type=F32)


def mm_tn(a, b):
    return lax.dot_general(a, b, TN, preferred_element_type=F32)


def scaled_rows(values):
    mean = jnp.mean(values, -1, keepdims=True)
    centred = values - mean
    inverse = lax.rsqrt(jnp.mean(centred * centred, -1, keepdims=True) + EPS)
    return centred * inverse, inverse


def norm_back(grad_norm, scaled, inverse, gain):
    grad_scaled = grad_norm * gain
    mean_grad = jnp.mean(grad_scaled, -1, keepdims=True)
    mean_cross = jnp.mean(grad_scaled * scaled, -1, keepdims=True)
    return inverse * (grad_scaled - mean_grad - scaled * mean_cross)


def low_half(shape):
    return lax.broadcasted_iota(jnp.int32, shape, 1) < HEAD


def fold(values):
    return jnp.sum(values.reshape(values.shape[0] // 8, 8, values.shape[1]), 0)


def window(step, size):
    return pl.ds(step * size if isinstance(step, int) else pl.multiple_of(step * size, size), size)


def loop(count, body, first=0, unroll=1):
    unroll = min(unroll, count - first)
    while (count - first) % max(unroll, 1):
        unroll -= 1

    def one(step, carry):
        for inner in range(unroll):
            body(first + step * unroll + inner)
        return carry

    if unroll and unroll == count - first:
        one(0, 0)
    elif unroll:
        lax.fori_loop(0, (count - first) // unroll, one, 0)


class Pieces:
    def __init__(self, src, dst, rows, send_sems, recv_sems, device):
        count = pieces(rows)
        size = rows // count
        self.copies = [
            pltpu.make_async_remote_copy(
                src_ref=src.at[pl.ds(n * size, size)],
                dst_ref=dst.at[pl.ds(n * size, size)],
                send_sem=send_sems.at[n],
                recv_sem=recv_sems.at[n],
                device_id=device,
                device_id_type=MESH,
            )
            for n in range(count)
        ]

    def start(self):
        for copy in self.copies:
            copy.start()

    def wait_send(self):
        for copy in self.copies:
            copy.wait_send()

    def wait_recv(self):
        for copy in self.copies:
            copy.wait_recv()


def pieces(rows):
    return max(1, min(PIECES, rows // 48))


class Chain:
    def __init__(self, me, blocks, stride):
        self.stride = stride
        self.count = blocks // stride
        self.place = me // stride
        self.me = me

    def device(self, side):
        return {"blk": self.me + (self.stride if side else -self.stride)}

    def has(self, side, steps=1):
        if side:
            return self.place + steps < self.count
        return self.place - steps >= 0

    def visit(self, number):
        rights, lefts = self.count - 1 - self.place, self.place
        both = jnp.minimum(rights, lefts)
        paired = number < 2 * both
        side = jnp.where(paired, 1 - number % 2, jnp.where(rights > lefts, 1, 0))
        index = jnp.where(paired, number // 2, number - both)
        return jnp.where(side == 1, self.count - 1 - index, index), side


class Plan:
    def __init__(self):
        self.now = 0.0
        self.busy = {}

    def work(self, microseconds):
        self.now += 0.75 * microseconds

    def send(self, link, size, hops=1):
        fast = link == ("dp", 1)
        length = size / 3e5 if fast else hops * 2 * size / 1e5
        end = max(self.now, self.busy.get(link, 0.0)) + length
        self.busy[link] = end
        return end + HOP


class Sum:
    def __init__(self, plan, held, landing, last, out, send_sems, recv_sems, free_sems, out_sem, bits):
        self.plan, self.held, self.landing, self.last = plan, held, landing, last
        self.out, self.send_sems, self.recv_sems, self.out_sem = out, send_sems, recv_sems, out_sem
        self.free_sems = free_sems
        start, base, wholes = 0, 0, 0
        self.stages = []
        undo = []
        for (axis, bit), (rows, halve) in zip(bits, halving(held.shape[0], len(bits)), strict=True):
            mine = lax.axis_index(axis)
            value = lax.rem(mine // bit, 2)
            partner = {axis: mine + bit * (1 - 2 * value)}
            link = (axis, bit)
            if halve:
                keep, give = start + value * rows, start + (1 - value) * rows
                self.stages.append(("halve", partner, give, keep, rows, base, link))
                undo.append(("back", partner, keep, give, rows, base, link))
                base += rows
                start = keep
            else:
                self.stages.append(("whole", partner, start, start, rows, wholes, link))
                wholes += 1
        self.stages += undo[::-1]
        self.done = -1
        self.ends = 0.0

    def settle(self):
        return pltpu.make_async_copy(self.held, self.out, self.out_sem)

    def copy(self, number):
        kind, partner, source, keep, rows, base, _ = self.stages[number]
        at = pl.ds(pl.multiple_of(source, 16), rows)
        src = self.held.at[at]
        if kind == "halve":
            dst = self.landing.at[pl.ds(base, rows)]
        elif kind == "whole":
            dst = self.last.at[base, pl.ds(0, rows)]
        else:
            dst = src
        return Pieces(src, dst, rows, self.send_sems.at[number], self.recv_sems.at[number], partner)

    def arrival(self, number):
        kind, partner, source, keep, rows, base, _ = self.stages[number]
        if kind != "back":
            return self.copy(number)
        ref = self.held.at[pl.ds(pl.multiple_of(keep, 16), rows)]
        return Pieces(ref, ref, rows, self.send_sems.at[number], self.recv_sems.at[number], partner)

    def start(self):
        self.begin(0)

    def begin(self, number):
        self.done = number
        if self.stages[number][0] == "back":
            pl.semaphore_wait(self.free_sems.at[len(self.stages) - 1 - number], 1)
        self.copy(number).start()
        rows, (axis, bit) = self.stages[number][4], self.stages[number][6]
        far = axis == "blk" and bit > 1
        link = ("blk", 1) if axis == "blk" else (axis, bit)
        self.ends = self.plan.send(link, rows * self.held.shape[1] * 2, 2 if far else 1)

    @property
    def active(self):
        return 0 <= self.done < len(self.stages)

    @property
    def over(self):
        return self.done == len(self.stages)

    def step(self):
        number = self.done
        kind, partner, source, keep, rows, base, _ = self.stages[number]
        self.copy(number).wait_send()
        if kind == "halve":
            pl.semaphore_signal(self.free_sems.at[number], inc=1, device_id=partner, device_id_type=MESH)
        self.arrival(number).wait_recv()
        self.plan.now = max(self.plan.now, self.ends)
        if kind != "back":
            block = 48 if rows % 48 == 0 else 16

            def add(step):
                at = pl.ds(pl.multiple_of(keep + step * block, 16), block)
                if kind == "halve":
                    came = self.landing[pl.ds(pl.multiple_of(base + step * block, 16), block)]
                else:
                    came = self.last[base, pl.ds(pl.multiple_of(step * block, 16), block)]
                self.held[at] = (self.held[at].astype(F32) + came.astype(F32)).astype(BF)

            loop(rows // block, add, unroll=2)
            self.plan.work(0.2 + rows * 0.001)
        if number + 1 < len(self.stages):
            self.begin(number + 1)
        else:
            self.done = number + 1
            self.settle().start()


class VectorSum:
    def __init__(self, plan, held, landing, send_sems, recv_sems, bits):
        self.plan, self.held, self.landing = plan, held, landing
        self.send_sems, self.recv_sems = send_sems, recv_sems
        self.partners = []
        for axis, bit in bits:
            mine = lax.axis_index(axis)
            self.partners.append({axis: mine + bit * (1 - 2 * lax.rem(mine // bit, 2))})
        self.done = -1
        self.ends = 0.0

    def copy(self, number):
        return pltpu.make_async_remote_copy(
            src_ref=self.held,
            dst_ref=self.landing.at[number],
            send_sem=self.send_sems.at[number],
            recv_sem=self.recv_sems.at[number],
            device_id=self.partners[number],
            device_id_type=MESH,
        )

    def start(self):
        self.begin(0)

    def begin(self, number):
        self.done = number
        self.copy(number).start()
        self.ends = self.plan.now + HOP

    @property
    def active(self):
        return 0 <= self.done < len(self.partners)

    def step(self):
        self.copy(self.done).wait()
        self.plan.now = max(self.plan.now, self.ends)
        self.held[...] = self.held[...] + self.landing[self.done]
        if self.done + 1 < len(self.partners):
            self.begin(self.done + 1)
        else:
            self.done += 1


def landing_slot(matrix, blocks):
    return matrix if blocks <= 4 else matrix % 4


def halving(rows, bits):
    plan = []
    for position in range(bits):
        halve = rows % 32 == 0 and position < bits - 1
        if halve:
            rows //= 2
        plan.append((rows, halve))
    return plan


def axis_bits(axis, size):
    return [(axis, 1 << bit) for bit in range(size.bit_length() - 1)]


def layer_kernel(blocks, groups, names, *refs):
    r = dict(zip(names, refs, strict=True))
    tokens_in, scenes, cot_in = r["tokens"], r["scenes"], r["cotangent"]
    small = {name: r["rows"].at[n : n + 1] for n, name in enumerate(SMALL)} | {"ub": r["ub_v"]}
    qb, vb, ob, g1, s1, g2, s2, db, ub = (small[name] for name in SMALL + ("ub",))
    flt = r["flt"]
    xg, k_all, v_all, qst, gst = r["xg"], r["k_all"], r["v_all"], r["qst"], r["gst"]
    m, l, lse, delta, ot, att = r["m"], r["l"], r["lse"], r["delta"], r["ot"], r["att"]
    held, hidden = r["held"], r["hidden"]
    vacc, vub = r["vacc"], r["vub"]
    seqs, rows, width = tokens_in.shape
    inner_width = ub.shape[1]
    pairs = width // PAIR
    me = lax.axis_index("blk")
    chains = [Chain(me, blocks, 1), Chain(me, blocks, 2)]
    bases = [0, blocks]
    own = [chains[0].place, blocks + chains[1].place]
    mate = me + 1 - 2 * lax.rem(me, 2)
    dp_bits, blk_bits = axis_bits("dp", groups), axis_bits("blk", blocks)

    vector_loads = []
    for number, name in enumerate(SMALL + ("ub",)):
        place = r["ub_v"].at[0] if name == "ub" else r["rows"].at[number]
        vector_loads.append(pltpu.make_async_copy(r[name], place, r["small_sems"].at[number]))
        vector_loads[-1].start()
    loads = {}
    for number, name in enumerate(LARGE):
        place = r["cot_v"] if name in ("tokens", "cotangent") else r[name + "_v"]
        loads[name] = pltpu.make_async_copy(r[name], place, r["load_sems"].at[number])
        if name != "cotangent":
            loads[name].start()
    tokens = cot = r["cot_v"]
    wq, wk, wv, wo, wu, wd = (r[n + "_v"] for n in ("wq", "wk", "wv", "wo", "wu", "wd"))

    barrier = pltpu.get_barrier_semaphore()
    total = 0
    for chain in chains:
        for side in (0, 1):

            @pl.when(chain.has(side))
            def _():
                pl.semaphore_signal(barrier, inc=1, device_id=chain.device(side), device_id_type=MESH)

            total = total + chain.has(side).astype(jnp.int32)
    for axis, bit in dp_bits + blk_bits:
        mine = lax.axis_index(axis)
        partner = {axis: mine + bit * (1 - 2 * lax.rem(mine // bit, 2))}
        pl.semaphore_signal(barrier, inc=1, device_id=partner, device_id_type=MESH)
        total = total + 1
    pl.semaphore_wait(barrier, total)

    swap = pltpu.make_async_remote_copy(
        src_ref=scenes,
        dst_ref=r["theirs"],
        send_sem=r["scene_sems"].at[0],
        recv_sem=r["scene_sems"].at[1],
        device_id={"blk": mate},
        device_id_type=MESH,
    )
    swap.start()
    for load in vector_loads:
        load.wait()
    loads["tokens"].wait()
    swap.wait()
    ordered = jnp.where(scenes[0:1, 0:1] == r["theirs"][0:1, 0:1], 1.0, 0.0)

    def sort(first, second):
        w = jnp.broadcast_to(ordered, first.shape)
        return w * first + (1.0 - w) * second, w * second + (1.0 - w) * first

    def place_rows(step):
        at = window(step, STEP)
        first, second = sort(tokens[0, at, :].astype(F32), tokens[1, at, :].astype(F32))
        xg[own[0], at, :] = first.astype(BF)
        xg[own[1], at, :] = second.astype(BF)

    loop(rows // STEP, place_rows, unroll=4)
    loads["cotangent"].start()

    def passing(which, side, step, slot):
        place = xg.at[bases[which] + slot]
        send, recv = r["x_send"].at[which, side, step], r["x_recv"].at[which, 1 - side, step]
        return Pieces(place, place, rows, send, recv, chains[which].device(side))

    for which in (0, 1):
        for side in (0, 1):

            @pl.when(chains[which].has(side))
            def _():
                passing(which, side, 1, chains[which].place).start()

    loads["wq"].wait()
    loads["wk"].wait()
    loads["wv"].wait()

    def project(which, slot, fl, with_queries):
        index = bases[which] + slot

        def norm_rows(step):
            at = window(step, STEP)
            scaled, _ = scaled_rows(xg[index, at, :].astype(F32))
            fl[at, :] = (scaled * g1[...] + s1[...]).astype(BF)

        loop(rows // STEP, norm_rows, unroll=4)

        left = fl[...]
        flt[:, window(index, rows)] = jnp.transpose(left)
        keys = mm(left, wk[...]).astype(BF)
        for pair in range(pairs):
            k_all[pair, index] = keys[:, pair * PAIR : (pair + 1) * PAIR]
        values = (mm(left, wv[...]) + vb[...]).astype(BF)
        for pair in range(pairs):
            v_all[pair, index] = values[:, pair * PAIR : (pair + 1) * PAIR]
        if with_queries:
            queries = (mm(left, wq[...]) + qb[...]).astype(BF).astype(F32) * HEAD**-0.5
            for pair in range(pairs):
                part = queries[:, pair * PAIR : (pair + 1) * PAIR]
                low = low_half(part.shape)
                qst[which, pair, 0:rows] = jnp.where(low, part, 0.0).astype(BF)
                qst[which, pair, rows : 2 * rows] = jnp.where(low, 0.0, part).astype(BF)

    def attend(which, slot):
        index = bases[which] + slot

        def pair_step(pair):
            s = mm_nt(k_all[pair, index], qst[which, pair])
            before = m[which, pair]
            now = jnp.maximum(before, jnp.max(s, axis=0, keepdims=True))
            e = jnp.exp(s - now)
            decay = jnp.exp(before - now)
            m[which, pair] = now
            l[which, pair] = l[which, pair] * decay + jnp.sum(e, axis=0, keepdims=True)
            low = e.astype(BF)
            vt = jnp.transpose(v_all[pair, index])
            for head in range(2):
                feats = slice(head * HEAD, (head + 1) * HEAD)
                cols = slice(head * rows, (head + 1) * rows)
                ot[which, pair, feats] = ot[which, pair, feats] * decay[:, cols] + mm(vt[feats], low[:, cols])

        loop(pairs, pair_step, unroll=3)

    def attention_forward(fl):
        m[...] = jnp.full(m.shape, FLOOR, F32)
        l[...] = jnp.zeros(l.shape, F32)
        ot[...] = jnp.zeros(ot.shape, F32)
        def receive(which, step):
            chain = chains[which]
            for side in (0, 1):

                @pl.when(chain.has(side, step))
                def _():
                    slot = chain.place + (step if side else -step)
                    passing(which, 1 - side, step, slot).wait_recv()

                    @pl.when(chain.has(1 - side))
                    def _():
                        passing(which, 1 - side, step + 1, slot).start()

        def use(which, step, side):
            chain = chains[which]

            @pl.when(chain.has(side, step))
            def _():
                slot = chain.place + (step if side else -step)
                project(which, slot, fl, False)
                attend(which, slot)

        project(0, chains[0].place, fl, True)
        attend(0, chains[0].place)
        project(1, chains[1].place, fl, True)
        receive(0, 1)
        attend(1, chains[1].place)

        def alternate(step):
            receive(1, step)
            use(1, step, 0)
            use(1, step, 1)

        loop(chains[1].count, alternate, 1)

        def single(step):
            use(0, step, 0)

            @pl.when(step + 1 < chains[0].count)
            def _():
                receive(0, step + 1)

            use(0, step, 1)

        loop(chains[0].count, single, 1)

        for which in (0, 1):

            def finish(pair):
                total = l[which, pair]
                lse[which, pair] = m[which, pair] + jnp.log(total)
                share = 1.0 / total
                for head in range(2):
                    feats = slice(head * HEAD, (head + 1) * HEAD)
                    cols = slice(head * rows, (head + 1) * rows)
                    ot[which, pair, feats] = ot[which, pair, feats] * share[:, cols]
                att[which, pair] = jnp.transpose(ot[which, pair])

            loop(pairs, finish, unroll=3)

        for which in (0, 1):
            chain = chains[which]

            def sent(step):
                for side in (0, 1):
                    @pl.when(jnp.logical_and(chain.has(side), chain.has(1 - side, step - 1)))
                    def _():
                        passing(which, side, step, chain.place + (1 - step if side else step - 1)).wait_send()

            loop(chain.count, sent, 1)

    pl.run_scoped(attention_forward, pltpu.VMEM((rows, width), BF))

    plan = Plan()
    places = [(number, 0, width) for number in range(MATRICES - 1)]
    places += [(MATRICES - 1, half * width // 2, width // 2) for half in (0, 1)]
    sums = []
    wholes = 0
    for number, (matrix, start, size) in enumerate(places):
        rest = dp_bits[1:]
        bits = dp_bits[:1] + (rest if number % 2 == 0 else rest[::-1]) + blk_bits
        halves = halving(size, len(bits))
        count = sum(not halve for _, halve in halves)
        space = r["landing"].shape[1] // 2 if size < width else r["landing"].shape[1]
        slot = landing_slot(matrix, blocks)
        sums.append(
            Sum(
                plan,
                held.at[matrix, pl.ds(start, size)],
                r["landing"].at[slot, pl.ds(space if start else 0, space)],
                r["last"].at[pl.ds(wholes, count)],
                r["sums"].at[matrix, pl.ds(start, size)],
                r["sum_send"].at[number],
                r["sum_recv"].at[number],
                r["sum_free"].at[number],
                r["sum_out"].at[number],
                bits,
            )
        )
        wholes += count
    vector_sum = VectorSum(
        plan, r["vectors"], r["vector_landing"], r["vector_send"], r["vector_recv"], dp_bits + blk_bits
    )

    def pump(microseconds=0.0):
        plan.work(microseconds)
        for s in sums + [vector_sum]:
            if s.active and s.ends <= plan.now:
                s.step()

    def begin(number):
        slot = landing_slot(places[number][0], blocks)
        for other in range(number):
            if landing_slot(places[other][0], blocks) == slot and places[other][0] != places[number][0]:
                while not sums[other].over:
                    min((s for s in sums if s.active), key=lambda s: s.ends).step()
        sums[number].start()

    vacc[...] = jnp.zeros(vacc.shape, F32)
    vub[...] = jnp.zeros(vub.shape, F32)
    both = seqs * rows
    halves = [slice(0, rows), slice(rows, both)]

    def feed_forward(slow, active, ginner, gbranch):
        loads["wo"].wait()
        loads["cotangent"].wait()

        def sort_rows(step):
            at = window(step, STEP)
            first, second = sort(cot[0, at, :].astype(F32), cot[1, at, :].astype(F32))
            vacc[DB] += fold(first) + fold(second)
            cot[0, at, :] = first.astype(BF)
            cot[1, at, :] = second.astype(BF)

        loop(rows // STEP, sort_rows, unroll=4)

        for which in (0, 1):
            for pair in range(pairs):
                gst[which, pair, 0:rows] = att[which, pair].astype(BF)

        def attended(which, some):
            return jnp.concatenate([gst[which, pair, 0:rows] for pair in some], 1)

        for which in (0, 1):
            here = halves[which]
            hidden[here, :] = xg[own[which]].astype(F32) + (mm(attended(which, range(pairs)), wo[...]) + ob[...])

        def norm_rows(step):
            at = window(step, STEP)
            scaled, _ = scaled_rows(hidden[at, :])
            slow[at, :] = (scaled * g2[...] + s2[...]).astype(BF)

        loop(both // STEP, norm_rows, unroll=4)
        loads["wu"].wait()
        loads["wd"].wait()

        for part in (0, 1):

            at = slice(part * width, (part + 1) * width)
            for which in (0, 1):
                here = halves[which]
                inner = mm(slow[here, :], wu[:, at]) + ub[:, at]
                grad_active = mm_nt(cot[which], wd[at, :])
                share = 0.5 * (1.0 + lax.erf(inner * (0.5**0.5)))
                slope = share + inner * (jnp.exp(-0.5 * inner * inner) * 0.3989422804014327)
                active[here, at] = (inner * share).astype(BF)
                low = (grad_active * slope).astype(BF)
                ginner[here, at] = low
                vub[:, at] += fold(low.astype(F32))
                pump(2.0)

            def down_weights(step):
                rows_at = window(part * (width // TILE) + step, TILE)
                held[2 * part, window(step, TILE), :] = mm_tn(active[:, rows_at], cot[...].reshape(both, width)).astype(BF)

            for step in range(width // TILE):
                down_weights(step)
                pump(0.4)
            begin(2 * part)

            def up_weights(step):
                at = window(step, TILE)
                held[2 * part + 1, at, :] = mm_tn(slow[:, at], ginner[:, part * width : (part + 1) * width]).astype(BF)

            loop(width // TILE, up_weights, unroll=3)
            plan.work(1.2)
            begin(2 * part + 1)
            pump()

        ys = [hidden[here, :] + (mm(active[here, :], wd[...]) + db[...]) for here in halves]
        first, second = sort(*ys)
        slow[halves[0], :] = first.astype(BF)
        slow[halves[1], :] = second.astype(BF)
        pump(2.0)
        layer_out = [
            pltpu.make_async_copy(slow.at[halves[n]], r["layer_out"].at[n], r["out_sems"].at[n]) for n in (0, 1)
        ]
        for copy in layer_out:
            copy.start()

        for which in (0, 1):
            back = mm_nt(ginner[halves[which], :], wu[...])
            for part in range(rows // PAIR):
                for step in range(width // TILE):
                    ot[which, part * (width // TILE) + step] = back[
                        part * PAIR : (part + 1) * PAIR, step * TILE : (step + 1) * TILE
                    ]
        pump(2.0)

        def hidden_back(which, step):
            rows_at = window(step, STEP)
            at = window(which * (rows // STEP) + step, STEP)
            scaled, inverse = scaled_rows(hidden[at, :])
            inside = window(lax.rem(step, PAIR // STEP), STEP)
            block = step // (PAIR // STEP) * (width // TILE)
            grad = jnp.concatenate([ot[which, block + part, inside, :] for part in range(width // TILE)], 1)
            vacc[G2] += fold(grad * scaled)
            vacc[S2] += fold(grad)
            grad_hidden = cot[which, rows_at, :].astype(F32) + norm_back(grad, scaled, inverse, g2[...])
            hidden[at, :] = grad_hidden
            low = grad_hidden.astype(BF)
            gbranch[at, :] = low
            vacc[OB] += fold(low.astype(F32))

        for which in (0, 1):
            loop(rows // STEP, partial(hidden_back, which), unroll=2)
            pump(0.7)

        def output_weights(step):
            at = window(step, TILE)
            left = jnp.concatenate([attended(which, (2 * step, 2 * step + 1)) for which in (0, 1)], 0)
            held[4, at, :] = mm_tn(left, gbranch[...]).astype(BF)

        loop(width // TILE, output_weights, unroll=3)
        plan.work(1.2)
        begin(4)

        for which in (0, 1):
            low = mm_nt(gbranch[halves[which], :], wo[...]).astype(BF).astype(F32)
            for pair in range(pairs):
                part = low[:, pair * PAIR : (pair + 1) * PAIR]
                lower = low_half(part.shape)
                gst[which, pair, 0:rows] = jnp.where(lower, part, 0.0).astype(BF)
                gst[which, pair, rows : 2 * rows] = jnp.where(lower, 0.0, part).astype(BF)
                product = jnp.transpose(part * att[which, pair])
                delta[which, pair, :, 0:rows] = jnp.sum(product[0:HEAD], 0, keepdims=True)
                delta[which, pair, :, rows : 2 * rows] = jnp.sum(product[HEAD:PAIR], 0, keepdims=True)
        pump(2.0)
        for copy in layer_out:
            copy.wait()

    pl.run_scoped(
        feed_forward,
        pltpu.VMEM((both, width), BF),
        pltpu.VMEM((both, inner_width), BF),
        pltpu.VMEM((both, inner_width), BF),
        pltpu.VMEM((both, width), BF),
    )

    ot[...] = jnp.zeros(ot.shape, F32)
    grad_in, grad_out = r["grad_in"], xg
    in_bases = [0, blocks + 1]

    def returning(which, side, slot):
        chain = chains[which]
        arrives = jnp.logical_and(slot == chain.place + (1 if side else -1), side == 0)
        index = in_bases[which] + jnp.where(arrives, chain.count, slot)
        return Pieces(
            grad_out.at[bases[which] + slot],
            grad_in.at[index],
            rows,
            r["g_send"].at[which, slot],
            r["g_recv"].at[index],
            chain.device(side),
        )

    def arrived(which, side, slot):
        index = in_bases[which] + jnp.where(jnp.logical_and(slot == chains[which].place, side == 0), chains[which].count, slot)
        ref = grad_in.at[index]
        Pieces(ref, ref, rows, r["g_send"].at[which, 0], r["g_recv"].at[index], {"blk": mate}).wait_recv()
        return index

    def attention_backward(grad):
        dq = cot

        def pair_back(which, index, pair):
            k, v, q, g = k_all[pair, index], v_all[pair, index], qst[which, pair], gst[which, pair]
            p = jnp.exp(mm_nt(k, q) - lse[which, pair])
            low = (p * (mm_nt(v, g) - delta[which, pair])).astype(BF)
            value_grad = mm(p.astype(BF), g)
            vacc[VB, :, window(pair, PAIR)] += fold(value_grad)
            v_all[pair, index] = value_grad.astype(BF)
            k_all[pair, index] = mm(low, q).astype(BF)
            kt = jnp.transpose(k)
            for head in range(2):
                feats = slice(head * HEAD, (head + 1) * HEAD)
                ot[which, pair, feats] += mm(kt[feats], low[:, head * rows : (head + 1) * rows])

        def slot_back(which, index, group):
            for pair in group:
                pair_back(which, index, pair)
                pump(1.1)

        def joined(values, index):
            return jnp.concatenate([values[pair, index] for pair in range(pairs)], 1)

        def give(which, number):
            chain = chains[which]
            slot, side = chain.visit(number)
            index = bases[which] + slot
            grad[0:rows, :] = mm_nt(joined(k_all, index), wk[...]) + mm_nt(joined(v_all, index), wv[...])

            def gather_rows(step):
                at = window(step, STEP)
                scaled, _ = scaled_rows(xg[index, at, :].astype(F32))
                values = grad[at, :]
                vacc[G1] += fold(values * scaled)
                vacc[S1] += fold(values)
                grad_out[index, at, :] = values.astype(BF)

            loop(rows // STEP, gather_rows, unroll=2)
            for toward in (0, 1):

                @pl.when(jnp.logical_and(side == toward, jnp.logical_not(chain.has(1 - toward))))
                def _():
                    returning(which, toward, slot).start()

            plan.send(("blk", 1), rows * width * 2)
            pump(1.8)

        def relay(which, distance, number):
            chain = chains[which]
            slot, side = chain.visit(number)
            for toward in (0, 1):
                behind = chain.place if toward else chain.count - 1 - chain.place

                @pl.when(jnp.logical_and(side == toward, behind == distance))
                def _():
                    place = arrived(which, toward, slot)

                    def add(step):
                        at = window(step, STEP)
                        out = bases[which] + slot
                        grad_out[out, at, :] = (
                            grad_out[out, at, :].astype(F32) + grad_in[place, at, :].astype(F32)
                        ).astype(BF)

                    loop(rows // STEP, add, unroll=4)
                    returning(which, toward, slot).start()

        def other(which, number):
            return bases[which] + chains[which].visit(number)[0]

        def query_rows(which, pair):
            value = jnp.transpose(ot[which, pair]) * HEAD**-0.5
            vacc[QB, :, window(pair, PAIR)] += fold(value)
            dq[which, :, window(pair, PAIR)] = value.astype(BF)

        def weights(group, step):
            at = window(step, TILE)
            number = 5 + group
            pair = 2 * group
            flat = (k_all.shape[1] * rows, PAIR)
            right = jnp.concatenate(
                [k_all[pair].reshape(flat), k_all[pair + 1].reshape(flat)]
                + [v_all[pair].reshape(flat), v_all[pair + 1].reshape(flat)],
                1,
            )
            held[number, at, TILE : 3 * TILE] = mm(flt[at, :], right).astype(BF)
            columns = window(group, TILE)
            held[number, at, 0:TILE] = sum(
                mm(flt[at, window(own[which], rows)], dq[which, :, columns]) for which in (0, 1)
            ).astype(BF)

        groups_of_heads = [(2 * group, 2 * group + 1) for group in range(pairs // 2)]
        alternate = [(1, n) for n in range(chains[1].count - 1)]
        singles = [(0, n) for n in range(chains[0].count - 1)]
        for which, number in alternate:
            slot_back(which, other(which, number), range(pairs))
            give(which, number)
        slot_back(1, own[1], range(pairs))
        for pair in range(pairs):
            query_rows(1, pair)
        for group, members in enumerate(groups_of_heads):
            final = group == len(groups_of_heads) - 1
            for which, number in singles:
                slot_back(which, other(which, number), members)
            slot_back(0, own[0], members)
            for pair in members:
                query_rows(0, pair)
            for step in range(width // TILE):
                weights(group, step)
                pump(0.8)
                if final and step == (width // TILE) // 2:
                    begin(7)
            begin(8 if final else 5 + group)
            pump()
        for which, number in singles:
            give(which, number)
        given = plan.now

        for which in (0, 1):
            grad[halves[which], :] = (
                mm_nt(joined(k_all, own[which]), wk[...])
                + mm_nt(joined(v_all, own[which]), wv[...])
                + mm_nt(dq[which], wq[...])
            )
        pump(2.5)
        for which in (0, 1):

            def own_rows(step):
                at = window(step, STEP)
                to = window(which * (rows // STEP) + step, STEP)
                scaled, _ = scaled_rows(xg[own[which], at, :].astype(F32))
                values = grad[to, :]
                vacc[G1] += fold(values * scaled)
                vacc[S1] += fold(values)

            loop(rows // STEP, own_rows, unroll=2)

        vectors = r["vectors"]
        vectors[...] = jnp.zeros(vectors.shape, F32)
        for number in range(UB):
            vectors[number : number + 1, :] = jnp.sum(vacc[number], 0, keepdims=True)
        for part in range(inner_width // width):
            vectors[UB + part : UB + part + 1, :] = jnp.sum(vub[:, part * width : (part + 1) * width], 0, keepdims=True)
        vector_sum.start()
        pump(1.0)

        def drain(until):
            while True:
                left = [s for s in sums + [vector_sum] if s.active]
                if not left or min(s.ends for s in left) > until:
                    return
                min(left, key=lambda s: s.ends).step()

        hop = HOP + rows * width * 4 / 1e5
        for distance in range(1, chains[0].count - 1):
            drain(given + distance * hop)
            for which in (1, 0):
                if distance < chains[which].count - 1:
                    loop(chains[which].count - 1, partial(relay, which, distance))
        drain(given + (chains[0].count - 1) * hop)
        for which in (0, 1):
            for side in (0, 1):

                @pl.when(chains[which].has(1 - side))
                def _():
                    place = arrived(which, side, chains[which].place)

                    def add(step):
                        to = window(which * (rows // STEP) + step, STEP)
                        grad[to, :] += grad_in[place, window(step, STEP), :].astype(F32)

                    loop(rows // STEP, add, unroll=4)

        pump(0.8)

        def tokens_back(step):
            at = window(step, STEP)
            parts = []
            for which in (0, 1):
                to = window(which * (rows // STEP) + step, STEP)
                scaled, inverse = scaled_rows(xg[own[which], at, :].astype(F32))
                parts.append(hidden[to, :] + norm_back(grad[to, :], scaled, inverse, g1[...]))
            first, second = sort(*parts)
            cot[0, at, :] = first.astype(BF)
            cot[1, at, :] = second.astype(BF)

        loop(rows // STEP, tokens_back, unroll=2)
        tokens_out = pltpu.make_async_copy(cot, r["tokens_grad"], r["out_sems"].at[2])
        tokens_out.start()
        pump(1.0)

        for which, number in alternate + singles:
            slot, side = chains[which].visit(number)
            for toward in (0, 1):

                @pl.when(side == toward)
                def _():
                    returning(which, toward, slot).wait_send()

        drain(float("inf"))
        for s in sums:
            s.settle().wait()
        tokens_out.wait()

    pl.run_scoped(attention_backward, pltpu.VMEM((both, width), F32))


def run_layer(operands):
    blocks, groups = lax.axis_size("blk"), lax.axis_size("dp")
    seqs, rows, width = operands["tokens"].shape
    inner = operands["ub"].shape[0]
    pairs = width // PAIR
    slots = blocks + blocks // 2
    bits = (blocks * groups).bit_length() - 1
    plans = [halving(width, bits)] * (MATRICES - 1) + [halving(width // 2, bits)] * 2
    landing = max(
        sum(size for size, halve in plans[0] if halve), 2 * sum(size for size, halve in plans[-1] if halve)
    )
    landing = (landing + 31) // 32 * 32
    wholes = [size for plan in plans for size, halve in plan if not halve]
    landings = 1 + max(landing_slot(matrix, blocks) for matrix in range(MATRICES))
    vmem = pl.BlockSpec(memory_space=pltpu.VMEM)
    hbm = pl.BlockSpec(memory_space=pl.ANY)
    out_shape = {
        "layer_out": jax.ShapeDtypeStruct((seqs, rows, width), BF),
        "tokens_grad": jax.ShapeDtypeStruct((seqs, rows, width), BF),
        "sums": jax.ShapeDtypeStruct((MATRICES, width, width), BF),
        "vectors": jax.ShapeDtypeStruct((16, width), F32),
    }
    dma = pltpu.SemaphoreType.DMA
    scratch = {name + "_v": pltpu.VMEM(operands[name].shape, BF) for name in LARGE if name[0] == "w"}
    scratch |= {
        "cot_v": pltpu.VMEM((seqs, rows, width), BF),
        "rows": pltpu.VMEM((len(SMALL), width), F32),
        "ub_v": pltpu.VMEM((1, inner), F32),
        "small_sems": dma((len(SMALL) + 1,)),
        "theirs": pltpu.VMEM((seqs, rows), jnp.int32),
        "xg": pltpu.VMEM((slots, rows, width), BF),
        "flt": pltpu.VMEM((width, slots * rows), BF),
        "k_all": pltpu.VMEM((pairs, slots, rows, PAIR), BF),
        "v_all": pltpu.VMEM((pairs, slots, rows, PAIR), BF),
        "qst": pltpu.VMEM((seqs, pairs, 2 * rows, PAIR), BF),
        "gst": pltpu.VMEM((seqs, pairs, 2 * rows, PAIR), BF),
        "m": pltpu.VMEM((seqs, pairs, 1, 2 * rows), F32),
        "l": pltpu.VMEM((seqs, pairs, 1, 2 * rows), F32),
        "lse": pltpu.VMEM((seqs, pairs, 1, 2 * rows), F32),
        "delta": pltpu.VMEM((seqs, pairs, 1, 2 * rows), F32),
        "ot": pltpu.VMEM((seqs, pairs, PAIR, rows), F32),
        "att": pltpu.VMEM((seqs, pairs, rows, PAIR), F32),
        "hidden": pltpu.VMEM((seqs * rows, width), F32),
        "vacc": pltpu.VMEM((UB, 8, width), F32),
        "vub": pltpu.VMEM((8, inner), F32),
        "held": pltpu.VMEM((MATRICES, width, width), BF),
        "landing": pltpu.VMEM((landings, landing, width), BF),
        "last": pltpu.VMEM((len(wholes), max(wholes), width), BF),
        "vector_landing": pltpu.VMEM((bits, 16, width), F32),
        "grad_in": pltpu.VMEM((slots + 2, rows, width), BF),
        "out_sems": dma((3,)),
        "load_sems": dma((len(LARGE),)),
        "scene_sems": dma((2,)),
        "x_send": dma((2, 2, blocks + 1, PIECES)),
        "x_recv": dma((2, 2, blocks + 1, PIECES)),
        "g_send": dma((2, blocks, PIECES)),
        "g_recv": dma((slots + 2, PIECES)),
        "sum_send": dma((len(plans), 2 * bits, PIECES)),
        "sum_recv": dma((len(plans), 2 * bits, PIECES)),
        "sum_free": pltpu.SemaphoreType.REGULAR((len(plans), bits)),
        "sum_out": dma((len(plans),)),
        "vector_send": dma((bits,)),
        "vector_recv": dma((bits,)),
    }
    names = tuple(operands) + tuple(out_shape) + tuple(scratch)
    return pl.pallas_call(
        partial(layer_kernel, blocks, groups, names),
        out_shape=tuple(out_shape.values()),
        in_specs=[vmem if name == "scenes" else hbm for name in operands],
        out_specs=(hbm, hbm, hbm, vmem),
        scratch_shapes=list(scratch.values()),
        compiler_params=pltpu.CompilerParams(
            collective_id=0, has_side_effects=True, vmem_limit_bytes=int(63.8 * 2**20)
        ),
    )(*operands.values())


def spread_kernel(layer_out, tokens_grad, sums, vectors, *refs):
    outs, (narrow, wide, passed, in_sems, out_sems, pass_sems, vector_sems) = refs[:17], refs[17:]
    down, up, out, query, key, value = outs[2:8]
    width = sums.shape[1]
    half = width // 2
    order = [5, 6, 7, 0, 1, 2, 3, 4]
    loads = {}
    for number in order:
        for part in range(2):
            at = pl.ds(part * half, half)
            loads[number, part] = pltpu.make_async_copy(
                sums.at[number, at], narrow.at[number, at], in_sems.at[number, part]
            )
            loads[number, part].start()
    passing = []
    for n, source in enumerate((layer_out, tokens_grad)):
        passing.append(pltpu.make_async_copy(source, passed.at[n], pass_sems.at[0, n]))
        passing[-1].start()
    stores = [pltpu.make_async_copy(vectors.at[n], outs[8 + n], vector_sems.at[n]) for n in range(UB)]
    for part in range(2):
        target = outs[8 + UB].at[pl.ds(part * width, width)]
        stores.append(pltpu.make_async_copy(vectors.at[UB + part], target, vector_sems.at[UB + part]))
    for store in stores:
        store.start()

    def send(number, part, target):
        at = pl.ds(part * half, half)
        stores.append(pltpu.make_async_copy(wide.at[number, at], target, out_sems.at[number, part]))
        stores[-1].start()

    for number in order:
        for part in range(2):
            loads[number, part].wait()

            def widen(step):
                at = window(part * (half // STEP) + step, STEP)
                if number < 5:
                    wide[number, at] = narrow[number, at].astype(F32)
                else:
                    columns = pl.ds((number - 5) * TILE, TILE)
                    for n in range(3):
                        wide[5 + n, at, columns] = narrow[number, at, n * TILE : (n + 1) * TILE].astype(F32)

            loop(half // STEP, widen, unroll=4)
            at = pl.ds(part * half, half)
            if number in (0, 2):
                send(number, part, down.at[pl.ds(number // 2 * width + part * half, half)])
            elif number in (1, 3):
                send(number, part, up.at[at, pl.ds(number // 2 * width, width)])
            elif number == 4:
                send(number, part, out.at[at])
            elif number == MATRICES - 1:
                for n, matrix in enumerate((query, key, value)):
                    send(5 + n, part, matrix.at[at])
        if number == 7:
            for n in (0, 1):
                passing[n].wait()
                stores.append(pltpu.make_async_copy(passed.at[n], outs[n], pass_sems.at[1, n]))
                stores[-1].start()
    for store in stores:
        store.wait()


def spread(layer_out, tokens_grad, sums, vectors):
    width = sums.shape[1]
    matrices = [(2 * width, width), (width, 2 * width)] + [(width, width)] * 4
    shapes = [jax.ShapeDtypeStruct(value.shape, BF) for value in (layer_out, tokens_grad)]
    shapes += [jax.ShapeDtypeStruct(shape, F32) for shape in matrices + [(width,)] * UB + [(2 * width,)]]
    hbm = pl.BlockSpec(memory_space=pl.ANY)
    return pl.pallas_call(
        spread_kernel,
        out_shape=tuple(shapes),
        in_specs=[hbm, hbm, hbm, pl.BlockSpec(memory_space=pltpu.VMEM)],
        out_specs=(hbm,) * len(shapes),
        scratch_shapes=[
            pltpu.VMEM(sums.shape, BF),
            pltpu.VMEM(sums.shape, F32),
            pltpu.VMEM((2,) + layer_out.shape, BF),
            pltpu.SemaphoreType.DMA((MATRICES, 2)),
            pltpu.SemaphoreType.DMA((MATRICES, 2)),
            pltpu.SemaphoreType.DMA((2, 2)),
            pltpu.SemaphoreType.DMA((UB + 2,)),
        ],
        compiler_params=pltpu.CompilerParams(vmem_limit_bytes=63 * 2**20),
    )(layer_out, tokens_grad, sums, vectors)


def on_device(
    tokens,
    scene_ids,
    query_weight,
    query_bias,
    key_weight,
    value_weight,
    value_bias,
    output_weight,
    output_bias,
    first_gain,
    first_shift,
    second_gain,
    second_shift,
    up_weight,
    up_bias,
    down_weight,
    down_bias,
    cotangent,
):
    operands = {
        "tokens": tokens,
        "scenes": scene_ids,
        "wq": query_weight,
        "wk": key_weight,
        "wv": value_weight,
        "wo": output_weight,
        "wu": up_weight,
        "wd": down_weight,
        "cotangent": cotangent,
        "qb": query_bias,
        "vb": value_bias,
        "ob": output_bias,
        "g1": first_gain,
        "s1": first_shift,
        "g2": second_gain,
        "s2": second_shift,
        "ub": up_bias,
        "db": down_bias,
    }
    (
        layer_out,
        tokens_grad,
        down_grad,
        up_grad,
        output_grad,
        query_grad,
        key_grad,
        value_grad,
        query_bias_grad,
        value_bias_grad,
        output_bias_grad,
        first_gain_grad,
        first_shift_grad,
        second_gain_grad,
        second_shift_grad,
        down_bias_grad,
        up_bias_grad,
    ) = spread(*run_layer(operands))
    return (
        layer_out,
        tokens_grad,
        query_grad,
        query_bias_grad,
        key_grad,
        value_grad,
        value_bias_grad,
        output_grad,
        output_bias_grad,
        first_gain_grad,
        first_shift_grad,
        second_gain_grad,
        second_shift_grad,
        up_grad,
        up_bias_grad,
        down_grad,
        down_bias_grad,
    )


def solution(mesh):
    split = P("dp", "blk", None)
    in_specs = (split, P("dp", "blk")) + (P(),) * 15 + (split,)
    out_specs = (split, split) + (P(),) * 15
    return jax.shard_map(on_device, mesh=mesh, in_specs=in_specs, out_specs=out_specs, check_vma=False)
```

```python
from functools import partial

import jax
import jax.numpy as jnp
from jax import lax
from jax.experimental import pallas as pl
from jax.experimental.pallas import tpu as pltpu
from jax.sharding import PartitionSpec as P

HEAD = 64
PAIR = 2 * HEAD
EPS = 1e-05
FLOOR = -1e30
MESH = pl.DeviceIdType.MESH
BF = jnp.bfloat16
F32 = jnp.float32
NT = (((1,), (1,)), ((), ()))
TN = (((0,), (0,)), ((), ()))
STEP = 32
TILE = 256
MATRICES = 8
PIECES = 1
HOP = 4.0
LARGE = ("tokens", "wq", "wk", "wv", "wo", "wu", "wd", "cotangent")
SMALL = ("qb", "vb", "ob", "g1", "s1", "g2", "s2", "db")
QB, VB, OB, G1, S1, G2, S2, DB, UB = range(9)


def mm(a, b):
    return jnp.dot(a, b, preferred_element_type=F32)


def mm_nt(a, b):
    return lax.dot_general(a, b, NT, preferred_element_type=F32)


def mm_tn(a, b):
    return lax.dot_general(a, b, TN, preferred_element_type=F32)


def scaled_rows(values):
    mean = jnp.mean(values, -1, keepdims=True)
    centred = values - mean
    inverse = lax.rsqrt(jnp.mean(centred * centred, -1, keepdims=True) + EPS)
    return centred * inverse, inverse


def norm_back(grad_norm, scaled, inverse, gain):
    grad_scaled = grad_norm * gain
    mean_grad = jnp.mean(grad_scaled, -1, keepdims=True)
    mean_cross = jnp.mean(grad_scaled * scaled, -1, keepdims=True)
    return inverse * (grad_scaled - mean_grad - scaled * mean_cross)


def low_half(shape):
    return lax.broadcasted_iota(jnp.int32, shape, 1) < HEAD


def fold(values):
    return jnp.sum(values.reshape(values.shape[0] // 8, 8, values.shape[1]), 0)


def window(step, size):
    return pl.ds(step * size if isinstance(step, int) else pl.multiple_of(step * size, size), size)


def loop(count, body, first=0, unroll=1):
    unroll = min(unroll, count - first)
    while (count - first) % max(unroll, 1):
        unroll -= 1

    def one(step, carry):
        for inner in range(unroll):
            body(first + step * unroll + inner)
        return carry

    if unroll and unroll == count - first:
        one(0, 0)
    elif unroll:
        lax.fori_loop(0, (count - first) // unroll, one, 0)


class Pieces:
    def __init__(self, src, dst, rows, send_sems, recv_sems, device):
        count = pieces(rows)
        size = rows // count
        self.copies = [
            pltpu.make_async_remote_copy(
                src_ref=src.at[pl.ds(n * size, size)],
                dst_ref=dst.at[pl.ds(n * size, size)],
                send_sem=send_sems.at[n],
                recv_sem=recv_sems.at[n],
                device_id=device,
                device_id_type=MESH,
            )
            for n in range(count)
        ]

    def start(self):
        for copy in self.copies:
            copy.start()

    def wait_send(self):
        for copy in self.copies:
            copy.wait_send()

    def wait_recv(self):
        for copy in self.copies:
            copy.wait_recv()


def pieces(rows):
    return max(1, min(PIECES, rows // 48))


class Chain:
    def __init__(self, me, blocks, stride):
        self.stride = stride
        self.count = blocks // stride
        self.place = me // stride
        self.me = me

    def device(self, side):
        return {"blk": self.me + (self.stride if side else -self.stride)}

    def has(self, side, steps=1):
        if side:
            return self.place + steps < self.count
        return self.place - steps >= 0

    def visit(self, number):
        rights, lefts = self.count - 1 - self.place, self.place
        both = jnp.minimum(rights, lefts)
        paired = number < 2 * both
        side = jnp.where(paired, 1 - number % 2, jnp.where(rights > lefts, 1, 0))
        index = jnp.where(paired, number // 2, number - both)
        return jnp.where(side == 1, self.count - 1 - index, index), side


class Plan:
    def __init__(self):
        self.now = 0.0
        self.busy = {}

    def work(self, microseconds):
        self.now += 0.75 * microseconds

    def send(self, link, size, hops=1):
        fast = link == ("dp", 1)
        length = size / 3e5 if fast else hops * 2 * size / 1e5
        end = max(self.now, self.busy.get(link, 0.0)) + length
        self.busy[link] = end
        return end + HOP


def others(group):
    values = [lax.rem(lax.axis_index(axis) // bit, 2) for axis, bit in group]
    result = []
    for mask in range(1 << len(group)):
        device, place = {}, 0
        for n, ((axis, bit), value) in enumerate(zip(group, values, strict=True)):
            flip = mask >> n & 1
            place = place + ((1 - value) if flip else value) * (1 << n)
            if flip:
                device[axis] = device.get(axis, lax.axis_index(axis)) + bit * (1 - 2 * value)
        result.append((device, place))
    return result


class Sum:
    def __init__(self, plan, held, landing, last, out, send_sems, recv_sems, free_sems, out_sem, groups):
        self.plan, self.held, self.landing, self.last = plan, held, landing, last
        self.out, self.send_sems, self.recv_sems, self.out_sem = out, send_sems, recv_sems, out_sem
        self.free_sems = free_sems
        start, base, wholes = 0, 0, 0
        self.stages = []
        undo = []
        for group, (rows, split) in zip(groups, halving(held.shape[0], groups), strict=True):
            ways = others(group)
            if split:
                starts = [start + place * rows for _, place in ways]
                self.stages.append(("split", group, ways, starts, rows, base))
                undo.append(("back", group, ways, starts, rows, base))
                base += (len(ways) - 1) * rows
                start = starts[0]
            else:
                self.stages.append(("whole", group, ways, [start] * len(ways), rows, wholes))
                wholes += len(ways) - 1
        self.stages += undo[::-1]
        self.done = -1
        self.ends = 0.0

    def settle(self):
        return pltpu.make_async_copy(self.held, self.out, self.out_sem)

    def part(self, start, rows):
        return self.held.at[pl.ds(pl.multiple_of(start, 16), rows)]

    def copies(self, number):
        kind, _, ways, starts, rows, base = self.stages[number]
        result = []
        for mask in range(1, len(ways)):
            source = self.part(starts[0] if kind == "back" else starts[mask], rows)
            if kind == "split":
                target = self.landing.at[pl.ds(base + (mask - 1) * rows, rows)]
            elif kind == "whole":
                target = self.last.at[base + mask - 1, pl.ds(0, rows)]
            else:
                target = source
            result.append(self.move(number, mask, source, target))
        return result

    def arrivals(self, number):
        kind, _, ways, starts, rows, _ = self.stages[number]
        if kind != "back":
            return self.copies(number)
        parts = [self.part(start, rows) for start in starts]
        return [self.move(number, mask, parts[mask], parts[mask]) for mask in range(1, len(ways))]

    def move(self, number, mask, source, target):
        return pltpu.make_async_remote_copy(
            src_ref=source,
            dst_ref=target,
            send_sem=self.send_sems.at[number, mask],
            recv_sem=self.recv_sems.at[number, mask],
            device_id=self.stages[number][2][mask][0],
            device_id_type=MESH,
        )

    def start(self):
        self.begin(0)

    def begin(self, number):
        self.done = number
        kind, group, ways, _, rows, _ = self.stages[number]
        for mask, copy in enumerate(self.copies(number), 1):
            if kind == "back":
                pl.semaphore_wait(self.free_sems.at[len(self.stages) - 1 - number, mask], 1)
            copy.start()
        size = rows * self.held.shape[1] * 2
        self.ends = 0.0
        for axis, bit in group:
            if axis == "blk":
                inner, outer = (4, 3) if len(group) > 1 else (0, 1) if bit == 1 else (2, 1)
                for link, hops in (("inner", inner), ("outer", outer)):
                    if hops:
                        self.ends = max(self.ends, self.plan.send(link, size, hops))
                break
            self.ends = max(self.ends, self.plan.send((axis, bit), size, len(group)))

    @property
    def active(self):
        return 0 <= self.done < len(self.stages)

    @property
    def over(self):
        return self.done == len(self.stages)

    def step(self):
        number = self.done
        kind, _, ways, starts, rows, base = self.stages[number]
        for mask, copy in enumerate(self.copies(number), 1):
            copy.wait_send()
            if kind == "split":
                pl.semaphore_signal(
                    self.free_sems.at[number, mask], inc=1, device_id=ways[mask][0], device_id_type=MESH
                )
        for copy in self.arrivals(number):
            copy.wait_recv()
        self.plan.now = max(self.plan.now, self.ends)
        if kind != "back":
            block = 48 if rows % 48 == 0 else 16

            def add(step):
                at = pl.ds(pl.multiple_of(starts[0] + step * block, 16), block)
                terms = [self.held[at].astype(F32)]
                for mask in range(1, len(ways)):
                    if kind == "split":
                        here = base + (mask - 1) * rows + step * block
                        came = self.landing[pl.ds(pl.multiple_of(here, 16), block)]
                    else:
                        came = self.last[base + mask - 1, pl.ds(pl.multiple_of(step * block, 16), block)]
                    terms.append(came.astype(F32))
                while len(terms) > 1:
                    terms = [terms[n] + terms[n + 1] for n in range(0, len(terms), 2)]
                self.held[at] = terms[0].astype(BF)

            loop(rows // block, add, unroll=2)
            self.plan.work(0.2 + rows * 0.001)
        if number + 1 < len(self.stages):
            self.begin(number + 1)
        else:
            self.done = number + 1
            self.settle().start()


class VectorSum:
    def __init__(self, plan, held, landing, send_sems, recv_sems, bits):
        self.plan, self.held, self.landing = plan, held, landing
        self.send_sems, self.recv_sems = send_sems, recv_sems
        self.partners = []
        for axis, bit in bits:
            mine = lax.axis_index(axis)
            self.partners.append({axis: mine + bit * (1 - 2 * lax.rem(mine // bit, 2))})
        self.done = -1
        self.ends = 0.0

    def copy(self, number):
        return pltpu.make_async_remote_copy(
            src_ref=self.held,
            dst_ref=self.landing.at[number],
            send_sem=self.send_sems.at[number],
            recv_sem=self.recv_sems.at[number],
            device_id=self.partners[number],
            device_id_type=MESH,
        )

    def start(self):
        self.begin(0)

    def begin(self, number):
        self.done = number
        self.copy(number).start()
        self.ends = self.plan.now + HOP

    @property
    def active(self):
        return 0 <= self.done < len(self.partners)

    def step(self):
        self.copy(self.done).wait()
        self.plan.now = max(self.plan.now, self.ends)
        self.held[...] = self.held[...] + self.landing[self.done]
        if self.done + 1 < len(self.partners):
            self.begin(self.done + 1)
        else:
            self.done += 1


def landing_slot(matrix, blocks):
    return matrix if blocks <= 4 else matrix % 4


def halving(rows, groups):
    plan = []
    for position, group in enumerate(groups):
        parts = 1 << len(group)
        split = rows % (16 * parts) == 0 and position < len(groups) - 1
        if split:
            rows //= parts
        plan.append((rows, split))
    return plan


def whole_count(rows, groups):
    return sum((1 << len(group)) - 1 for group, (_, split) in zip(groups, halving(rows, groups), strict=True) if not split)


def landing_rows(rows, groups):
    return sum(
        ((1 << len(group)) - 1) * part for group, (part, split) in zip(groups, halving(rows, groups), strict=True) if split
    )


def groups_of(number, dp_bits, blk_bits):
    rest = dp_bits[1:] if number % 2 == 0 else dp_bits[:0:-1]
    planar = [rest[:2]] if number >= 2 else [[bit] for bit in rest[:2]]
    groups = [dp_bits[:1]] + planar + [[bit] for bit in rest[2:] + blk_bits]
    return [group for group in groups if group]


def axis_bits(axis, size):
    return [(axis, 1 << bit) for bit in range(size.bit_length() - 1)]


def layer_kernel(blocks, groups, names, *refs):
    r = dict(zip(names, refs, strict=True))
    tokens_in, scenes, cot_in = r["tokens"], r["scenes"], r["cotangent"]
    small = {name: r["rows"].at[n : n + 1] for n, name in enumerate(SMALL)} | {"ub": r["ub_v"]}
    qb, vb, ob, g1, s1, g2, s2, db, ub = (small[name] for name in SMALL + ("ub",))
    flt = r["flt"]
    xg, k_all, v_all, qst, gst = r["xg"], r["k_all"], r["v_all"], r["qst"], r["gst"]
    m, l, lse, delta, ot, att = r["m"], r["l"], r["lse"], r["delta"], r["ot"], r["att"]
    held, hidden = r["held"], r["hidden"]
    vacc, vub = r["vacc"], r["vub"]
    seqs, rows, width = tokens_in.shape
    inner_width = ub.shape[1]
    pairs = width // PAIR
    me = lax.axis_index("blk")
    chains = [Chain(me, blocks, 1), Chain(me, blocks, 2)]
    bases = [0, blocks]
    own = [chains[0].place, blocks + chains[1].place]
    mate = me + 1 - 2 * lax.rem(me, 2)
    dp_bits, blk_bits = axis_bits("dp", groups), axis_bits("blk", blocks)

    vector_loads = []
    for number, name in enumerate(SMALL + ("ub",)):
        place = r["ub_v"].at[0] if name == "ub" else r["rows"].at[number]
        vector_loads.append(pltpu.make_async_copy(r[name], place, r["small_sems"].at[number]))
        vector_loads[-1].start()
    loads = {}
    for number, name in enumerate(LARGE):
        place = r["cot_v"] if name in ("tokens", "cotangent") else r[name + "_v"]
        loads[name] = pltpu.make_async_copy(r[name], place, r["load_sems"].at[number])
        if name != "cotangent":
            loads[name].start()
    tokens = cot = r["cot_v"]
    wq, wk, wv, wo, wu, wd = (r[n + "_v"] for n in ("wq", "wk", "wv", "wo", "wu", "wd"))

    barrier = pltpu.get_barrier_semaphore()
    total = 0
    for chain in chains:
        for side in (0, 1):

            @pl.when(chain.has(side))
            def _():
                pl.semaphore_signal(barrier, inc=1, device_id=chain.device(side), device_id_type=MESH)

            total = total + chain.has(side).astype(jnp.int32)
    everyone = {tuple(group) for n in range(MATRICES + 1) for group in groups_of(n, dp_bits, blk_bits)}
    for group in sorted(everyone):
        for device, _ in others(group)[1:]:
            pl.semaphore_signal(barrier, inc=1, device_id=device, device_id_type=MESH)
            total = total + 1
    pl.semaphore_wait(barrier, total)

    swap = pltpu.make_async_remote_copy(
        src_ref=scenes,
        dst_ref=r["theirs"],
        send_sem=r["scene_sems"].at[0],
        recv_sem=r["scene_sems"].at[1],
        device_id={"blk": mate},
        device_id_type=MESH,
    )
    swap.start()
    for load in vector_loads:
        load.wait()
    loads["tokens"].wait()
    swap.wait()
    ordered = jnp.where(scenes[0:1, 0:1] == r["theirs"][0:1, 0:1], 1.0, 0.0)

    def sort(first, second):
        w = jnp.broadcast_to(ordered, first.shape)
        return w * first + (1.0 - w) * second, w * second + (1.0 - w) * first

    def place_rows(step):
        at = window(step, STEP)
        first, second = sort(tokens[0, at, :].astype(F32), tokens[1, at, :].astype(F32))
        xg[own[0], at, :] = first.astype(BF)
        xg[own[1], at, :] = second.astype(BF)

    loop(rows // STEP, place_rows, unroll=4)
    loads["cotangent"].start()

    def passing(which, side, step, slot):
        place = xg.at[bases[which] + slot]
        send, recv = r["x_send"].at[which, side, step], r["x_recv"].at[which, 1 - side, step]
        return Pieces(place, place, rows, send, recv, chains[which].device(side))

    for which in (0, 1):
        for side in (0, 1):

            @pl.when(chains[which].has(side))
            def _():
                passing(which, side, 1, chains[which].place).start()

    loads["wq"].wait()
    loads["wk"].wait()
    loads["wv"].wait()

    def project(which, slot, fl, with_queries):
        index = bases[which] + slot

        def norm_rows(step):
            at = window(step, STEP)
            scaled, _ = scaled_rows(xg[index, at, :].astype(F32))
            fl[at, :] = (scaled * g1[...] + s1[...]).astype(BF)

        loop(rows // STEP, norm_rows, unroll=4)

        left = fl[...]
        flt[:, window(index, rows)] = jnp.transpose(left)
        keys = mm(left, wk[...]).astype(BF)
        for pair in range(pairs):
            k_all[pair, index] = keys[:, pair * PAIR : (pair + 1) * PAIR]
        values = (mm(left, wv[...]) + vb[...]).astype(BF)
        for pair in range(pairs):
            v_all[pair, index] = values[:, pair * PAIR : (pair + 1) * PAIR]
        if with_queries:
            queries = (mm(left, wq[...]) + qb[...]).astype(BF).astype(F32) * HEAD**-0.5
            for pair in range(pairs):
                part = queries[:, pair * PAIR : (pair + 1) * PAIR]
                low = low_half(part.shape)
                qst[which, pair, 0:rows] = jnp.where(low, part, 0.0).astype(BF)
                qst[which, pair, rows : 2 * rows] = jnp.where(low, 0.0, part).astype(BF)

    def attend(which, slot):
        index = bases[which] + slot

        def pair_step(pair):
            s = mm_nt(k_all[pair, index], qst[which, pair])
            before = m[which, pair]
            now = jnp.maximum(before, jnp.max(s, axis=0, keepdims=True))
            e = jnp.exp(s - now)
            decay = jnp.exp(before - now)
            m[which, pair] = now
            l[which, pair] = l[which, pair] * decay + jnp.sum(e, axis=0, keepdims=True)
            low = e.astype(BF)
            vt = jnp.transpose(v_all[pair, index])
            for head in range(2):
                feats = slice(head * HEAD, (head + 1) * HEAD)
                cols = slice(head * rows, (head + 1) * rows)
                ot[which, pair, feats] = ot[which, pair, feats] * decay[:, cols] + mm(vt[feats], low[:, cols])

        loop(pairs, pair_step, unroll=3)

    plan = Plan()
    places = [(number, 0, width) for number in range(MATRICES - 1)]
    places += [(MATRICES - 1, half * width // 2, width // 2) for half in (0, 1)]
    sums = []
    wholes = 0
    for number, (matrix, start, size) in enumerate(places):
        groups = groups_of(number, dp_bits, blk_bits)
        count = whole_count(size, groups)
        space = r["landing"].shape[1] // 2 if size < width else r["landing"].shape[1]
        slot = landing_slot(matrix, blocks)
        sums.append(
            Sum(
                plan,
                held.at[matrix, pl.ds(start, size)],
                r["landing"].at[slot, pl.ds(space if start else 0, space)],
                r["last"].at[pl.ds(wholes, count)],
                r["sums"].at[matrix, pl.ds(start, size)],
                r["sum_send"].at[number],
                r["sum_recv"].at[number],
                r["sum_free"].at[number],
                r["sum_out"].at[number],
                groups,
            )
        )
        wholes += count
    vector_sum = VectorSum(
        plan, r["vectors"], r["vector_landing"], r["vector_send"], r["vector_recv"], dp_bits + blk_bits
    )

    def pump(microseconds=0.0):
        plan.work(microseconds)
        for s in sums + [vector_sum]:
            if s.active and s.ends <= plan.now:
                s.step()

    def begin(number):
        slot = landing_slot(places[number][0], blocks)
        for other in range(number):
            if landing_slot(places[other][0], blocks) == slot and places[other][0] != places[number][0]:
                while not sums[other].over:
                    min((s for s in sums if s.active), key=lambda s: s.ends).step()
        sums[number].start()

    vacc[...] = jnp.zeros(vacc.shape, F32)
    vub[...] = jnp.zeros(vub.shape, F32)
    both = seqs * rows
    halves = [slice(0, rows), slice(rows, both)]

    def receive(which, step):
        chain = chains[which]
        for side in (0, 1):

            @pl.when(chain.has(side, step))
            def _():
                slot = chain.place + (step if side else -step)
                passing(which, 1 - side, step, slot).wait_recv()

                @pl.when(chain.has(1 - side))
                def _():
                    passing(which, 1 - side, step + 1, slot).start()

    def finish(which):
        def one(pair):
            total = l[which, pair]
            lse[which, pair] = m[which, pair] + jnp.log(total)
            share = 1.0 / total
            for head in range(2):
                feats = slice(head * HEAD, (head + 1) * HEAD)
                cols = slice(head * rows, (head + 1) * rows)
                ot[which, pair, feats] = ot[which, pair, feats] * share[:, cols]
            att[which, pair] = jnp.transpose(ot[which, pair])

        loop(pairs, one, unroll=3)

    def forward_and_feed(slow, active, ginner, gbranch):
        fl = gbranch.at[halves[0]]

        def use(which, step, side):
            chain = chains[which]

            @pl.when(chain.has(side, step))
            def _():
                slot = chain.place + (step if side else -step)
                project(which, slot, fl, False)
                attend(which, slot)

        def sort_rows(step):
            at = window(step, STEP)
            first, second = sort(cot[0, at, :].astype(F32), cot[1, at, :].astype(F32))
            vacc[DB] += fold(first) + fold(second)
            cot[0, at, :] = first.astype(BF)
            cot[1, at, :] = second.astype(BF)

        def attended(which, some):
            return jnp.concatenate([att[which, pair].astype(BF) for pair in some], 1)

        def branch(which):
            here = halves[which]
            hidden[here, :] = xg[own[which]].astype(F32) + (mm(attended(which, range(pairs)), wo[...]) + ob[...])

            def norm_rows(step):
                at = window(which * (rows // STEP) + step, STEP)
                scaled, _ = scaled_rows(hidden[at, :])
                slow[at, :] = (scaled * g2[...] + s2[...]).astype(BF)

            loop(rows // STEP, norm_rows, unroll=4)

        def up(which, part):
            here = halves[which]
            at = slice(part * width, (part + 1) * width)
            inner = mm(slow[here, :], wu[:, at]) + ub[:, at]
            grad_active = mm_nt(cot[which], wd[at, :])
            share = 0.5 * (1.0 + lax.erf(inner * (0.5**0.5)))
            slope = share + inner * (jnp.exp(-0.5 * inner * inner) * 0.3989422804014327)
            active[here, at] = (inner * share).astype(BF)
            low = (grad_active * slope).astype(BF)
            ginner[here, at] = low
            vub[:, at] += fold(low.astype(F32))

        def down(which):
            here = halves[which]
            held[MATRICES - 1, here, :] = (hidden[here, :] + (mm(active[here, :], wd[...]) + db[...])).astype(BF)

        def hidden_back(which, step):
            rows_at = window(step, STEP)
            at = window(which * (rows // STEP) + step, STEP)
            scaled, inverse = scaled_rows(hidden[at, :])
            inside = window(lax.rem(step, PAIR // STEP), STEP)
            block = step // (PAIR // STEP) * (width // TILE)
            grad = jnp.concatenate([ot[which, block + part, inside, :] for part in range(width // TILE)], 1)
            vacc[G2] += fold(grad * scaled)
            vacc[S2] += fold(grad)
            grad_hidden = cot[which, rows_at, :].astype(F32) + norm_back(grad, scaled, inverse, g2[...])
            hidden[at, :] = grad_hidden
            low = grad_hidden.astype(BF)
            gbranch[at, :] = low
            vacc[OB] += fold(low.astype(F32))

        def second_back(which):
            back = mm_nt(ginner[halves[which], :], wu[...])
            for part in range(rows // PAIR):
                for step in range(width // TILE):
                    ot[which, part * (width // TILE) + step] = back[
                        part * PAIR : (part + 1) * PAIR, step * TILE : (step + 1) * TILE
                    ]
            pump(1.0)
            loop(rows // STEP, partial(hidden_back, which), unroll=2)
            pump(0.7)

        def branch_back(which):
            low = mm_nt(gbranch[halves[which], :], wo[...]).astype(BF).astype(F32)
            for pair in range(pairs):
                part = low[:, pair * PAIR : (pair + 1) * PAIR]
                lower = low_half(part.shape)
                gst[which, pair, 0:rows] = jnp.where(lower, part, 0.0).astype(BF)
                gst[which, pair, rows : 2 * rows] = jnp.where(lower, 0.0, part).astype(BF)
                product = jnp.transpose(part * att[which, pair])
                delta[which, pair, :, 0:rows] = jnp.sum(product[0:HEAD], 0, keepdims=True)
                delta[which, pair, :, rows : 2 * rows] = jnp.sum(product[HEAD:PAIR], 0, keepdims=True)
            pump(1.0)

        m[...] = jnp.full(m.shape, FLOOR, F32)
        l[...] = jnp.zeros(l.shape, F32)
        ot[...] = jnp.zeros(ot.shape, F32)
        project(0, chains[0].place, fl, True)
        attend(0, chains[0].place)
        project(1, chains[1].place, fl, True)
        receive(0, 1)
        attend(1, chains[1].place)
        use(0, 1, 0)
        use(0, 1, 1)

        def alternate(step):
            receive(1, step)
            use(1, step, 0)
            use(1, step, 1)

        loop(chains[1].count, alternate, 1)
        if chains[0].count > 2:
            receive(0, 2)
        finish(1)

        for name in ("wo", "cotangent", "wu", "wd"):
            loads[name].wait()
        loop(rows // STEP, sort_rows, unroll=4)
        branch(1)
        up(1, 0)
        up(1, 1)
        down(1)
        second_back(1)
        branch_back(1)

        def single(step):
            use(0, step, 0)

            @pl.when(step + 1 < chains[0].count)
            def _():
                receive(0, step + 1)

            use(0, step, 1)

        loop(chains[0].count, single, 2)
        finish(0)
        for which in (0, 1):
            chain = chains[which]

            def sent(step):
                for side in (0, 1):
                    @pl.when(jnp.logical_and(chain.has(side), chain.has(1 - side, step - 1)))
                    def _():
                        passing(which, side, step, chain.place + (1 - step if side else step - 1)).wait_send()

            loop(chain.count, sent, 1)

        branch(0)
        for part in (0, 1):
            up(0, part)
            pump(2.0)

            def down_weights(step):
                at = window(part * (width // TILE) + step, TILE)
                held[2 * part, window(step, TILE), :] = mm_tn(active[:, at], cot[...].reshape(both, width)).astype(BF)

            for step in range(width // TILE):
                down_weights(step)
                pump(0.4)
            begin(2 * part)

            def up_weights(step):
                at = window(step, TILE)
                held[2 * part + 1, at, :] = mm_tn(slow[:, at], ginner[:, part * width : (part + 1) * width]).astype(BF)

            for step in range(width // TILE):
                up_weights(step)
                pump(0.4)
            begin(2 * part + 1)

        down(0)

        def layer_rows(step):
            at = window(step, STEP)
            to = window(rows // STEP + step, STEP)
            last = MATRICES - 1
            first, second = sort(held[last, at, :].astype(F32), held[last, to, :].astype(F32))
            held[last, at, :] = first.astype(BF)
            held[last, to, :] = second.astype(BF)

        loop(rows // STEP, layer_rows, unroll=4)
        layer_out = [
            pltpu.make_async_copy(held.at[MATRICES - 1, halves[n]], r["layer_out"].at[n], r["out_sems"].at[n])
            for n in (0, 1)
        ]
        for copy in layer_out:
            copy.start()
        pump(1.3)
        second_back(0)

        def output_weights(step):
            at = window(step, TILE)
            left = jnp.concatenate([attended(which, (2 * step, 2 * step + 1)) for which in (0, 1)], 0)
            held[4, at, :] = mm_tn(left, gbranch[...]).astype(BF)

        for step in range(width // TILE):
            output_weights(step)
            pump(0.4)
        begin(4)
        branch_back(0)
        for copy in layer_out:
            copy.wait()

    pl.run_scoped(
        forward_and_feed,
        pltpu.VMEM((both, width), BF),
        pltpu.VMEM((both, inner_width), BF),
        pltpu.VMEM((both, inner_width), BF),
        pltpu.VMEM((both, width), BF),
    )

    ot[...] = jnp.zeros(ot.shape, F32)
    grad_in, grad_out = r["grad_in"], xg
    in_bases = [0, blocks + 1]

    def returning(which, side, slot):
        chain = chains[which]
        arrives = jnp.logical_and(slot == chain.place + (1 if side else -1), side == 0)
        index = in_bases[which] + jnp.where(arrives, chain.count, slot)
        return Pieces(
            grad_out.at[bases[which] + slot],
            grad_in.at[index],
            rows,
            r["g_send"].at[which, slot],
            r["g_recv"].at[index],
            chain.device(side),
        )

    def arrived(which, side, slot):
        index = in_bases[which] + jnp.where(jnp.logical_and(slot == chains[which].place, side == 0), chains[which].count, slot)
        ref = grad_in.at[index]
        Pieces(ref, ref, rows, r["g_send"].at[which, 0], r["g_recv"].at[index], {"blk": mate}).wait_recv()
        return index

    def attention_backward(grad):
        dq = cot

        def pair_back(which, index, pair):
            k, v, q, g = k_all[pair, index], v_all[pair, index], qst[which, pair], gst[which, pair]
            p = jnp.exp(mm_nt(k, q) - lse[which, pair])
            low = (p * (mm_nt(v, g) - delta[which, pair])).astype(BF)
            value_grad = mm(p.astype(BF), g)
            vacc[VB, :, window(pair, PAIR)] += fold(value_grad)
            v_all[pair, index] = value_grad.astype(BF)
            k_all[pair, index] = mm(low, q).astype(BF)
            kt = jnp.transpose(k)
            for head in range(2):
                feats = slice(head * HEAD, (head + 1) * HEAD)
                ot[which, pair, feats] += mm(kt[feats], low[:, head * rows : (head + 1) * rows])

        def slot_back(which, index, group):
            for pair in group:
                pair_back(which, index, pair)
                pump(1.1)

        def joined(values, index):
            return jnp.concatenate([values[pair, index] for pair in range(pairs)], 1)

        def give(which, number):
            chain = chains[which]
            slot, side = chain.visit(number)
            index = bases[which] + slot
            grad[0:rows, :] = mm_nt(joined(k_all, index), wk[...]) + mm_nt(joined(v_all, index), wv[...])

            def gather_rows(step):
                at = window(step, STEP)
                scaled, _ = scaled_rows(xg[index, at, :].astype(F32))
                values = grad[at, :]
                vacc[G1] += fold(values * scaled)
                vacc[S1] += fold(values)
                grad_out[index, at, :] = values.astype(BF)

            loop(rows // STEP, gather_rows, unroll=2)
            for toward in (0, 1):

                @pl.when(jnp.logical_and(side == toward, jnp.logical_not(chain.has(1 - toward))))
                def _():
                    returning(which, toward, slot).start()

            for link in ("inner", "outer"):
                plan.send(link, rows * width * 2)
            pump(1.8)

        def relay(which, distance, number):
            chain = chains[which]
            slot, side = chain.visit(number)
            for toward in (0, 1):
                behind = chain.place if toward else chain.count - 1 - chain.place

                @pl.when(jnp.logical_and(side == toward, behind == distance))
                def _():
                    place = arrived(which, toward, slot)

                    def add(step):
                        at = window(step, STEP)
                        out = bases[which] + slot
                        grad_out[out, at, :] = (
                            grad_out[out, at, :].astype(F32) + grad_in[place, at, :].astype(F32)
                        ).astype(BF)

                    loop(rows // STEP, add, unroll=4)
                    returning(which, toward, slot).start()

        def other(which, number):
            return bases[which] + chains[which].visit(number)[0]

        def query_rows(which, pair):
            value = jnp.transpose(ot[which, pair]) * HEAD**-0.5
            vacc[QB, :, window(pair, PAIR)] += fold(value)
            dq[which, :, window(pair, PAIR)] = value.astype(BF)

        def weights(group, step):
            at = window(step, TILE)
            number = 5 + group
            pair = 2 * group
            flat = (k_all.shape[1] * rows, PAIR)
            right = jnp.concatenate(
                [k_all[pair].reshape(flat), k_all[pair + 1].reshape(flat)]
                + [v_all[pair].reshape(flat), v_all[pair + 1].reshape(flat)],
                1,
            )
            held[number, at, TILE : 3 * TILE] = mm(flt[at, :], right).astype(BF)
            columns = window(group, TILE)
            held[number, at, 0:TILE] = sum(
                mm(flt[at, window(own[which], rows)], dq[which, :, columns]) for which in (0, 1)
            ).astype(BF)

        groups_of_heads = [(2 * group, 2 * group + 1) for group in range(pairs // 2)]
        alternate = [(1, n) for n in range(chains[1].count - 1)]
        singles = [(0, n) for n in range(chains[0].count - 1)]
        for which, number in alternate:
            slot_back(which, other(which, number), range(pairs))
            give(which, number)
        slot_back(1, own[1], range(pairs))
        for pair in range(pairs):
            query_rows(1, pair)
        for group, members in enumerate(groups_of_heads):
            final = group == len(groups_of_heads) - 1
            for which, number in singles:
                slot_back(which, other(which, number), members)
            slot_back(0, own[0], members)
            for pair in members:
                query_rows(0, pair)
            for step in range(width // TILE):
                weights(group, step)
                pump(0.8)
                if final and step == (width // TILE) // 2:
                    begin(7)
            begin(8 if final else 5 + group)
            pump()
        for which, number in singles:
            give(which, number)
        given = plan.now

        for which in (0, 1):
            grad[halves[which], :] = (
                mm_nt(joined(k_all, own[which]), wk[...])
                + mm_nt(joined(v_all, own[which]), wv[...])
                + mm_nt(dq[which], wq[...])
            )
        pump(2.5)
        for which in (0, 1):

            def own_rows(step):
                at = window(step, STEP)
                to = window(which * (rows // STEP) + step, STEP)
                scaled, _ = scaled_rows(xg[own[which], at, :].astype(F32))
                values = grad[to, :]
                vacc[G1] += fold(values * scaled)
                vacc[S1] += fold(values)

            loop(rows // STEP, own_rows, unroll=2)

        vectors = r["vectors"]
        vectors[...] = jnp.zeros(vectors.shape, F32)
        for number in range(UB):
            vectors[number : number + 1, :] = jnp.sum(vacc[number], 0, keepdims=True)
        for part in range(inner_width // width):
            vectors[UB + part : UB + part + 1, :] = jnp.sum(vub[:, part * width : (part + 1) * width], 0, keepdims=True)
        vector_sum.start()
        pump(1.0)

        def drain(until):
            while True:
                left = [s for s in sums + [vector_sum] if s.active]
                if not left or min(s.ends for s in left) > until:
                    return
                min(left, key=lambda s: s.ends).step()

        hop = HOP + rows * width * 4 / 1e5
        for distance in range(1, chains[0].count - 1):
            drain(given + distance * hop)
            for which in (1, 0):
                if distance < chains[which].count - 1:
                    loop(chains[which].count - 1, partial(relay, which, distance))
        drain(given + (chains[0].count - 1) * hop)
        for which in (0, 1):
            for side in (0, 1):

                @pl.when(chains[which].has(1 - side))
                def _():
                    place = arrived(which, side, chains[which].place)

                    def add(step):
                        to = window(which * (rows // STEP) + step, STEP)
                        grad[to, :] += grad_in[place, window(step, STEP), :].astype(F32)

                    loop(rows // STEP, add, unroll=4)

        pump(0.8)

        def tokens_back(step):
            at = window(step, STEP)
            parts = []
            for which in (0, 1):
                to = window(which * (rows // STEP) + step, STEP)
                scaled, inverse = scaled_rows(xg[own[which], at, :].astype(F32))
                parts.append(hidden[to, :] + norm_back(grad[to, :], scaled, inverse, g1[...]))
            first, second = sort(*parts)
            cot[0, at, :] = first.astype(BF)
            cot[1, at, :] = second.astype(BF)

        loop(rows // STEP, tokens_back, unroll=2)
        tokens_out = pltpu.make_async_copy(cot, r["tokens_grad"], r["out_sems"].at[2])
        tokens_out.start()
        pump(1.0)

        for which, number in alternate + singles:
            slot, side = chains[which].visit(number)
            for toward in (0, 1):

                @pl.when(side == toward)
                def _():
                    returning(which, toward, slot).wait_send()

        drain(float("inf"))
        for s in sums:
            s.settle().wait()
        tokens_out.wait()

    pl.run_scoped(attention_backward, pltpu.VMEM((both, width), F32))


def run_layer(operands):
    blocks, groups = lax.axis_size("blk"), lax.axis_size("dp")
    seqs, rows, width = operands["tokens"].shape
    inner = operands["ub"].shape[0]
    pairs = width // PAIR
    slots = blocks + blocks // 2
    bits = (blocks * groups).bit_length() - 1
    places = [width] * (MATRICES - 1) + [width // 2] * 2
    orders = [groups_of(n, axis_bits("dp", groups), axis_bits("blk", blocks)) for n in range(len(places))]
    landing = max(
        landing_rows(size, order) * (width // size) for size, order in zip(places, orders, strict=True)
    )
    landing = (landing + 31) // 32 * 32
    wholes = sum(whole_count(size, order) for size, order in zip(places, orders, strict=True))
    last = max(
        part for size, order in zip(places, orders, strict=True) for part, split in halving(size, order) if not split
    )
    landings = 1 + max(landing_slot(matrix, blocks) for matrix in range(MATRICES))
    vmem = pl.BlockSpec(memory_space=pltpu.VMEM)
    hbm = pl.BlockSpec(memory_space=pl.ANY)
    out_shape = {
        "layer_out": jax.ShapeDtypeStruct((seqs, rows, width), BF),
        "tokens_grad": jax.ShapeDtypeStruct((seqs, rows, width), BF),
        "sums": jax.ShapeDtypeStruct((MATRICES, width, width), BF),
        "vectors": jax.ShapeDtypeStruct((16, width), F32),
    }
    dma = pltpu.SemaphoreType.DMA
    scratch = {name + "_v": pltpu.VMEM(operands[name].shape, BF) for name in LARGE if name[0] == "w"}
    scratch |= {
        "cot_v": pltpu.VMEM((seqs, rows, width), BF),
        "rows": pltpu.VMEM((len(SMALL), width), F32),
        "ub_v": pltpu.VMEM((1, inner), F32),
        "small_sems": dma((len(SMALL) + 1,)),
        "theirs": pltpu.VMEM((seqs, rows), jnp.int32),
        "xg": pltpu.VMEM((slots, rows, width), BF),
        "flt": pltpu.VMEM((width, slots * rows), BF),
        "k_all": pltpu.VMEM((pairs, slots, rows, PAIR), BF),
        "v_all": pltpu.VMEM((pairs, slots, rows, PAIR), BF),
        "qst": pltpu.VMEM((seqs, pairs, 2 * rows, PAIR), BF),
        "gst": pltpu.VMEM((seqs, pairs, 2 * rows, PAIR), BF),
        "m": pltpu.VMEM((seqs, pairs, 1, 2 * rows), F32),
        "l": pltpu.VMEM((seqs, pairs, 1, 2 * rows), F32),
        "lse": pltpu.VMEM((seqs, pairs, 1, 2 * rows), F32),
        "delta": pltpu.VMEM((seqs, pairs, 1, 2 * rows), F32),
        "ot": pltpu.VMEM((seqs, pairs, PAIR, rows), F32),
        "att": pltpu.VMEM((seqs, pairs, rows, PAIR), F32),
        "hidden": pltpu.VMEM((seqs * rows, width), F32),
        "vacc": pltpu.VMEM((UB, 8, width), F32),
        "vub": pltpu.VMEM((8, inner), F32),
        "held": pltpu.VMEM((MATRICES, width, width), BF),
        "landing": pltpu.VMEM((landings, landing, width), BF),
        "last": pltpu.VMEM((wholes, last, width), BF),
        "vector_landing": pltpu.VMEM((bits, 16, width), F32),
        "grad_in": pltpu.VMEM((slots + 2, rows, width), BF),
        "out_sems": dma((3,)),
        "load_sems": dma((len(LARGE),)),
        "scene_sems": dma((2,)),
        "x_send": dma((2, 2, blocks + 1, PIECES)),
        "x_recv": dma((2, 2, blocks + 1, PIECES)),
        "g_send": dma((2, blocks, PIECES)),
        "g_recv": dma((slots + 2, PIECES)),
        "sum_send": dma((len(places), 2 * bits, 4)),
        "sum_recv": dma((len(places), 2 * bits, 4)),
        "sum_free": pltpu.SemaphoreType.REGULAR((len(places), bits, 4)),
        "sum_out": dma((len(places),)),
        "vector_send": dma((bits,)),
        "vector_recv": dma((bits,)),
    }
    names = tuple(operands) + tuple(out_shape) + tuple(scratch)
    return pl.pallas_call(
        partial(layer_kernel, blocks, groups, names),
        out_shape=tuple(out_shape.values()),
        in_specs=[vmem if name == "scenes" else hbm for name in operands],
        out_specs=(hbm, hbm, hbm, vmem),
        scratch_shapes=list(scratch.values()),
        compiler_params=pltpu.CompilerParams(
            collective_id=0, has_side_effects=True, vmem_limit_bytes=int(63.8 * 2**20)
        ),
    )(*operands.values())


def spread_kernel(layer_out, tokens_grad, sums, vectors, *refs):
    outs, (narrow, wide, passed, in_sems, out_sems, pass_sems, vector_sems) = refs[:17], refs[17:]
    down, up, out, query, key, value = outs[2:8]
    width = sums.shape[1]
    half = width // 2
    order = [5, 6, 7, 0, 1, 2, 3, 4]
    loads = {}
    for number in order:
        for part in range(2):
            at = pl.ds(part * half, half)
            loads[number, part] = pltpu.make_async_copy(
                sums.at[number, at], narrow.at[number, at], in_sems.at[number, part]
            )
            loads[number, part].start()
    passing = []
    for n, source in enumerate((layer_out, tokens_grad)):
        passing.append(pltpu.make_async_copy(source, passed.at[n], pass_sems.at[0, n]))
        passing[-1].start()
    stores = [pltpu.make_async_copy(vectors.at[n], outs[8 + n], vector_sems.at[n]) for n in range(UB)]
    for part in range(2):
        target = outs[8 + UB].at[pl.ds(part * width, width)]
        stores.append(pltpu.make_async_copy(vectors.at[UB + part], target, vector_sems.at[UB + part]))
    for store in stores:
        store.start()

    def send(number, part, target):
        at = pl.ds(part * half, half)
        stores.append(pltpu.make_async_copy(wide.at[number, at], target, out_sems.at[number, part]))
        stores[-1].start()

    for number in order:
        for part in range(2):
            loads[number, part].wait()

            def widen(step):
                at = window(part * (half // STEP) + step, STEP)
                if number < 5:
                    wide[number, at] = narrow[number, at].astype(F32)
                else:
                    columns = pl.ds((number - 5) * TILE, TILE)
                    for n in range(3):
                        wide[5 + n, at, columns] = narrow[number, at, n * TILE : (n + 1) * TILE].astype(F32)

            loop(half // STEP, widen, unroll=4)
            at = pl.ds(part * half, half)
            if number in (0, 2):
                send(number, part, down.at[pl.ds(number // 2 * width + part * half, half)])
            elif number in (1, 3):
                send(number, part, up.at[at, pl.ds(number // 2 * width, width)])
            elif number == 4:
                send(number, part, out.at[at])
            elif number == MATRICES - 1:
                for n, matrix in enumerate((query, key, value)):
                    send(5 + n, part, matrix.at[at])
        if number == 7:
            for n in (0, 1):
                passing[n].wait()
                stores.append(pltpu.make_async_copy(passed.at[n], outs[n], pass_sems.at[1, n]))
                stores[-1].start()
    for store in stores:
        store.wait()


def spread(layer_out, tokens_grad, sums, vectors):
    width = sums.shape[1]
    matrices = [(2 * width, width), (width, 2 * width)] + [(width, width)] * 4
    shapes = [jax.ShapeDtypeStruct(value.shape, BF) for value in (layer_out, tokens_grad)]
    shapes += [jax.ShapeDtypeStruct(shape, F32) for shape in matrices + [(width,)] * UB + [(2 * width,)]]
    hbm = pl.BlockSpec(memory_space=pl.ANY)
    return pl.pallas_call(
        spread_kernel,
        out_shape=tuple(shapes),
        in_specs=[hbm, hbm, hbm, pl.BlockSpec(memory_space=pltpu.VMEM)],
        out_specs=(hbm,) * len(shapes),
        scratch_shapes=[
            pltpu.VMEM(sums.shape, BF),
            pltpu.VMEM(sums.shape, F32),
            pltpu.VMEM((2,) + layer_out.shape, BF),
            pltpu.SemaphoreType.DMA((MATRICES, 2)),
            pltpu.SemaphoreType.DMA((MATRICES, 2)),
            pltpu.SemaphoreType.DMA((2, 2)),
            pltpu.SemaphoreType.DMA((UB + 2,)),
        ],
        compiler_params=pltpu.CompilerParams(vmem_limit_bytes=63 * 2**20),
    )(layer_out, tokens_grad, sums, vectors)


def on_device(
    tokens,
    scene_ids,
    query_weight,
    query_bias,
    key_weight,
    value_weight,
    value_bias,
    output_weight,
    output_bias,
    first_gain,
    first_shift,
    second_gain,
    second_shift,
    up_weight,
    up_bias,
    down_weight,
    down_bias,
    cotangent,
):
    operands = {
        "tokens": tokens,
        "scenes": scene_ids,
        "wq": query_weight,
        "wk": key_weight,
        "wv": value_weight,
        "wo": output_weight,
        "wu": up_weight,
        "wd": down_weight,
        "cotangent": cotangent,
        "qb": query_bias,
        "vb": value_bias,
        "ob": output_bias,
        "g1": first_gain,
        "s1": first_shift,
        "g2": second_gain,
        "s2": second_shift,
        "ub": up_bias,
        "db": down_bias,
    }
    (
        layer_out,
        tokens_grad,
        down_grad,
        up_grad,
        output_grad,
        query_grad,
        key_grad,
        value_grad,
        query_bias_grad,
        value_bias_grad,
        output_bias_grad,
        first_gain_grad,
        first_shift_grad,
        second_gain_grad,
        second_shift_grad,
        down_bias_grad,
        up_bias_grad,
    ) = spread(*run_layer(operands))
    return (
        layer_out,
        tokens_grad,
        query_grad,
        query_bias_grad,
        key_grad,
        value_grad,
        value_bias_grad,
        output_grad,
        output_bias_grad,
        first_gain_grad,
        first_shift_grad,
        second_gain_grad,
        second_shift_grad,
        up_grad,
        up_bias_grad,
        down_grad,
        down_bias_grad,
    )


def solution(mesh):
    split = P("dp", "blk", None)
    in_specs = (split, P("dp", "blk")) + (P(),) * 15 + (split,)
    out_specs = (split, split) + (P(),) * 15
    return jax.shard_map(on_device, mesh=mesh, in_specs=in_specs, out_specs=out_specs, check_vma=False)
```

```python
from functools import partial

import jax
import jax.numpy as jnp
from jax import lax
from jax.experimental import pallas as pl
from jax.experimental.pallas import tpu as pltpu
from jax.sharding import PartitionSpec as P

HEAD = 64
PAIR = 2 * HEAD
EPS = 1e-05
FLOOR = -1e30
MESH = pl.DeviceIdType.MESH
BF = jnp.bfloat16
F32 = jnp.float32
NT = (((1,), (1,)), ((), ()))
TN = (((0,), (0,)), ((), ()))
STEP = 32
TILE = 256
MATRICES = 8
PIECES = 1
HOP = 5.0
LARGE = ("tokens", "wq", "wk", "wv", "wo", "wu", "wd", "cotangent")
SMALL = ("qb", "vb", "ob", "g1", "s1", "g2", "s2", "db")
QB, VB, OB, G1, S1, G2, S2, DB, UB = range(9)


def mm(a, b):
    return jnp.dot(a, b, preferred_element_type=F32)


def mm_nt(a, b):
    return lax.dot_general(a, b, NT, preferred_element_type=F32)


def mm_tn(a, b):
    return lax.dot_general(a, b, TN, preferred_element_type=F32)


def scaled_rows(values):
    mean = jnp.mean(values, -1, keepdims=True)
    centred = values - mean
    inverse = lax.rsqrt(jnp.mean(centred * centred, -1, keepdims=True) + EPS)
    return centred * inverse, inverse


def norm_back(grad_norm, scaled, inverse, gain):
    grad_scaled = grad_norm * gain
    mean_grad = jnp.mean(grad_scaled, -1, keepdims=True)
    mean_cross = jnp.mean(grad_scaled * scaled, -1, keepdims=True)
    return inverse * (grad_scaled - mean_grad - scaled * mean_cross)


def low_half(shape):
    return lax.broadcasted_iota(jnp.int32, shape, 1) < HEAD


def fold(values):
    return jnp.sum(values.reshape(values.shape[0] // 8, 8, values.shape[1]), 0)


def window(step, size):
    return pl.ds(step * size if isinstance(step, int) else pl.multiple_of(step * size, size), size)


def loop(count, body, first=0, unroll=1):
    unroll = min(unroll, count - first)
    while (count - first) % max(unroll, 1):
        unroll -= 1

    def one(step, carry):
        for inner in range(unroll):
            body(first + step * unroll + inner)
        return carry

    if unroll and unroll == count - first:
        one(0, 0)
    elif unroll:
        lax.fori_loop(0, (count - first) // unroll, one, 0)


class Pieces:
    def __init__(self, src, dst, rows, send_sems, recv_sems, device):
        count = pieces(rows)
        size = rows // count
        self.copies = [
            pltpu.make_async_remote_copy(
                src_ref=src.at[pl.ds(n * size, size)],
                dst_ref=dst.at[pl.ds(n * size, size)],
                send_sem=send_sems.at[n],
                recv_sem=recv_sems.at[n],
                device_id=device,
                device_id_type=MESH,
            )
            for n in range(count)
        ]

    def start(self):
        for copy in self.copies:
            copy.start()

    def wait_send(self):
        for copy in self.copies:
            copy.wait_send()

    def wait_recv(self):
        for copy in self.copies:
            copy.wait_recv()


def pieces(rows):
    return max(1, min(PIECES, rows // 48))


class Chain:
    def __init__(self, me, blocks, stride):
        self.stride = stride
        self.count = blocks // stride
        self.place = me // stride
        self.me = me

    def device(self, side):
        return {"blk": self.me + (self.stride if side else -self.stride)}

    def has(self, side, steps=1):
        if side:
            return self.place + steps < self.count
        return self.place - steps >= 0

    def visit(self, number):
        rights, lefts = self.count - 1 - self.place, self.place
        both = jnp.minimum(rights, lefts)
        paired = number < 2 * both
        side = jnp.where(paired, 1 - number % 2, jnp.where(rights > lefts, 1, 0))
        index = jnp.where(paired, number // 2, number - both)
        return jnp.where(side == 1, self.count - 1 - index, index), side


class Plan:
    def __init__(self):
        self.now = 0.0
        self.busy = {}

    def work(self, microseconds):
        self.now += 0.5 * microseconds

    def send(self, link, size, hops=1):
        fast = link == ("dp", 1)
        length = size / 3e5 if fast else hops * 2 * size / 1e5
        end = max(self.now, self.busy.get(link, 0.0)) + length
        self.busy[link] = end
        return end + HOP


def others(group):
    values = [lax.rem(lax.axis_index(axis) // bit, 2) for axis, bit in group]
    result = []
    for mask in range(1 << len(group)):
        device, place = {}, 0
        for n, ((axis, bit), value) in enumerate(zip(group, values, strict=True)):
            flip = mask >> n & 1
            place = place + ((1 - value) if flip else value) * (1 << n)
            if flip:
                device[axis] = device.get(axis, lax.axis_index(axis)) + bit * (1 - 2 * value)
        result.append((device, place))
    return result


class Sum:
    def __init__(self, plan, held, landing, last, out, send_sems, recv_sems, free_sems, out_sem, groups):
        self.plan, self.held, self.landing, self.last = plan, held, landing, last
        self.out, self.send_sems, self.recv_sems, self.out_sem = out, send_sems, recv_sems, out_sem
        self.free_sems = free_sems
        start, base, wholes = 0, 0, 0
        self.stages = []
        undo = []
        for group, (rows, split) in zip(groups, halving(held.shape[0], groups), strict=True):
            ways = others(group)
            if split:
                starts = [start + place * rows for _, place in ways]
                self.stages.append(("split", group, ways, starts, rows, base))
                undo.append(("back", group, ways, starts, rows, base))
                base += (len(ways) - 1) * rows
                start = starts[0]
            else:
                self.stages.append(("whole", group, ways, [start] * len(ways), rows, wholes))
                wholes += len(ways) - 1
        self.stages += undo[::-1]
        self.done = -1
        self.ends = 0.0

    def settle(self):
        return pltpu.make_async_copy(self.held, self.out, self.out_sem)

    def part(self, start, rows):
        return self.held.at[pl.ds(pl.multiple_of(start, 16), rows)]

    def copies(self, number):
        kind, _, ways, starts, rows, base = self.stages[number]
        result = []
        for mask in range(1, len(ways)):
            source = self.part(starts[0] if kind == "back" else starts[mask], rows)
            if kind == "split":
                target = self.landing.at[pl.ds(base + (mask - 1) * rows, rows)]
            elif kind == "whole":
                target = self.last.at[base + mask - 1, pl.ds(0, rows)]
            else:
                target = source
            result.append(self.move(number, mask, source, target))
        return result

    def arrivals(self, number):
        kind, _, ways, starts, rows, _ = self.stages[number]
        if kind != "back":
            return self.copies(number)
        parts = [self.part(start, rows) for start in starts]
        return [self.move(number, mask, parts[mask], parts[mask]) for mask in range(1, len(ways))]

    def move(self, number, mask, source, target):
        return pltpu.make_async_remote_copy(
            src_ref=source,
            dst_ref=target,
            send_sem=self.send_sems.at[number, mask],
            recv_sem=self.recv_sems.at[number, mask],
            device_id=self.stages[number][2][mask][0],
            device_id_type=MESH,
        )

    def start(self):
        self.begin(0)

    def begin(self, number):
        self.done = number
        kind, group, ways, _, rows, _ = self.stages[number]
        for mask, copy in enumerate(self.copies(number), 1):
            if kind == "back":
                pl.semaphore_wait(self.free_sems.at[len(self.stages) - 1 - number, mask], 1)
            copy.start()
        size = rows * self.held.shape[1] * 2
        self.ends = 0.0
        for axis, bit in group:
            if axis == "blk":
                inner, outer = (4, 3) if len(group) > 1 else (0, 1) if bit == 1 else (2, 1)
                for link, hops in (("inner", inner), ("outer", outer)):
                    if hops:
                        self.ends = max(self.ends, self.plan.send(link, size, hops))
                break
            self.ends = max(self.ends, self.plan.send((axis, bit), size, len(group)))

    @property
    def active(self):
        return 0 <= self.done < len(self.stages)

    @property
    def over(self):
        return self.done == len(self.stages)

    def step(self):
        number = self.done
        kind, _, ways, starts, rows, base = self.stages[number]
        for mask, copy in enumerate(self.copies(number), 1):
            copy.wait_send()
            if kind == "split":
                pl.semaphore_signal(
                    self.free_sems.at[number, mask], inc=1, device_id=ways[mask][0], device_id_type=MESH
                )
        for copy in self.arrivals(number):
            copy.wait_recv()
        self.plan.now = max(self.plan.now, self.ends)
        if kind != "back":
            block = 48 if rows % 48 == 0 else 16

            def add(step):
                at = pl.ds(pl.multiple_of(starts[0] + step * block, 16), block)
                terms = [self.held[at].astype(F32)]
                for mask in range(1, len(ways)):
                    if kind == "split":
                        here = base + (mask - 1) * rows + step * block
                        came = self.landing[pl.ds(pl.multiple_of(here, 16), block)]
                    else:
                        came = self.last[base + mask - 1, pl.ds(pl.multiple_of(step * block, 16), block)]
                    terms.append(came.astype(F32))
                while len(terms) > 1:
                    terms = [terms[n] + terms[n + 1] for n in range(0, len(terms), 2)]
                self.held[at] = terms[0].astype(BF)

            loop(rows // block, add, unroll=2)
            self.plan.work(0.2 + rows * 0.001)
        if number + 1 < len(self.stages):
            self.begin(number + 1)
        else:
            self.done = number + 1
            self.settle().start()


class VectorSum:
    def __init__(self, plan, held, landing, send_sems, recv_sems, bits):
        self.plan, self.held, self.landing = plan, held, landing
        self.send_sems, self.recv_sems = send_sems, recv_sems
        self.partners = []
        for axis, bit in bits:
            mine = lax.axis_index(axis)
            self.partners.append({axis: mine + bit * (1 - 2 * lax.rem(mine // bit, 2))})
        self.done = -1
        self.ends = 0.0

    def copy(self, number):
        return pltpu.make_async_remote_copy(
            src_ref=self.held,
            dst_ref=self.landing.at[number],
            send_sem=self.send_sems.at[number],
            recv_sem=self.recv_sems.at[number],
            device_id=self.partners[number],
            device_id_type=MESH,
        )

    def start(self):
        self.begin(0)

    def begin(self, number):
        self.done = number
        self.copy(number).start()
        self.ends = self.plan.now + HOP

    @property
    def active(self):
        return 0 <= self.done < len(self.partners)

    def step(self):
        self.copy(self.done).wait()
        self.plan.now = max(self.plan.now, self.ends)
        self.held[...] = self.held[...] + self.landing[self.done]
        if self.done + 1 < len(self.partners):
            self.begin(self.done + 1)
        else:
            self.done += 1


def landing_slot(matrix, blocks):
    return matrix if blocks <= 4 else matrix % 4


def halving(rows, groups):
    plan = []
    for position, group in enumerate(groups):
        parts = 1 << len(group)
        split = rows % (16 * parts) == 0 and position < len(groups) - 1
        if split:
            rows //= parts
        plan.append((rows, split))
    return plan


def whole_count(rows, groups):
    return sum((1 << len(group)) - 1 for group, (_, split) in zip(groups, halving(rows, groups), strict=True) if not split)


def landing_rows(rows, groups):
    return sum(
        ((1 << len(group)) - 1) * part for group, (part, split) in zip(groups, halving(rows, groups), strict=True) if split
    )


def groups_of(number, dp_bits, blk_bits):
    rest = dp_bits[1:] if number % 2 == 0 else dp_bits[:0:-1]
    planar = [rest[:2]] if number >= 5 else [[bit] for bit in rest[:2]]
    groups = [dp_bits[:1]] + planar + [[bit] for bit in rest[2:] + blk_bits]
    return [group for group in groups if group]


def axis_bits(axis, size):
    return [(axis, 1 << bit) for bit in range(size.bit_length() - 1)]


def layer_kernel(blocks, groups, names, *refs):
    r = dict(zip(names, refs, strict=True))
    tokens_in, scenes, cot_in = r["tokens"], r["scenes"], r["cotangent"]
    small = {name: r["rows"].at[n : n + 1] for n, name in enumerate(SMALL)} | {"ub": r["ub_v"]}
    qb, vb, ob, g1, s1, g2, s2, db, ub = (small[name] for name in SMALL + ("ub",))
    flt = r["flt"]
    xg, k_all, v_all, qst, gst = r["xg"], r["k_all"], r["v_all"], r["qst"], r["gst"]
    m, l, lse, delta, ot, att = r["m"], r["l"], r["lse"], r["delta"], r["ot"], r["att"]
    held, hidden = r["held"], r["hidden"]
    vacc, vub = r["vacc"], r["vub"]
    seqs, rows, width = tokens_in.shape
    inner_width = ub.shape[1]
    pairs = width // PAIR
    me = lax.axis_index("blk")
    chains = [Chain(me, blocks, 1), Chain(me, blocks, 2)]
    bases = [0, blocks]
    own = [chains[0].place, blocks + chains[1].place]
    mate = me + 1 - 2 * lax.rem(me, 2)
    dp_bits, blk_bits = axis_bits("dp", groups), axis_bits("blk", blocks)

    vector_loads = []
    for number, name in enumerate(SMALL + ("ub",)):
        place = r["ub_v"].at[0] if name == "ub" else r["rows"].at[number]
        vector_loads.append(pltpu.make_async_copy(r[name], place, r["small_sems"].at[number]))
        vector_loads[-1].start()
    loads = {}
    for number, name in enumerate(LARGE):
        place = r["cot_v"] if name in ("tokens", "cotangent") else r[name + "_v"]
        loads[name] = pltpu.make_async_copy(r[name], place, r["load_sems"].at[number])
        if name != "cotangent":
            loads[name].start()
    tokens = cot = r["cot_v"]
    wq, wk, wv, wo, wu, wd = (r[n + "_v"] for n in ("wq", "wk", "wv", "wo", "wu", "wd"))

    barrier = pltpu.get_barrier_semaphore()
    total = 0
    for chain in chains:
        for side in (0, 1):

            @pl.when(chain.has(side))
            def _():
                pl.semaphore_signal(barrier, inc=1, device_id=chain.device(side), device_id_type=MESH)

            total = total + chain.has(side).astype(jnp.int32)
    everyone = {tuple(group) for n in range(MATRICES + 1) for group in groups_of(n, dp_bits, blk_bits)}
    for group in sorted(everyone):
        for device, _ in others(group)[1:]:
            pl.semaphore_signal(barrier, inc=1, device_id=device, device_id_type=MESH)
            total = total + 1
    pl.semaphore_wait(barrier, total)

    swap = pltpu.make_async_remote_copy(
        src_ref=scenes,
        dst_ref=r["theirs"],
        send_sem=r["scene_sems"].at[0],
        recv_sem=r["scene_sems"].at[1],
        device_id={"blk": mate},
        device_id_type=MESH,
    )
    swap.start()
    for load in vector_loads:
        load.wait()
    loads["tokens"].wait()
    swap.wait()
    ordered = jnp.where(scenes[0:1, 0:1] == r["theirs"][0:1, 0:1], 1.0, 0.0)

    def sort(first, second):
        w = jnp.broadcast_to(ordered, first.shape)
        return w * first + (1.0 - w) * second, w * second + (1.0 - w) * first

    def place_rows(step):
        at = window(step, STEP)
        first, second = sort(tokens[0, at, :].astype(F32), tokens[1, at, :].astype(F32))
        xg[own[0], at, :] = first.astype(BF)
        xg[own[1], at, :] = second.astype(BF)

    loop(rows // STEP, place_rows, unroll=4)
    loads["cotangent"].start()

    def passing(which, side, step, slot):
        place = xg.at[bases[which] + slot]
        send, recv = r["x_send"].at[which, side, step], r["x_recv"].at[which, 1 - side, step]
        return Pieces(place, place, rows, send, recv, chains[which].device(side))

    for which in (0, 1):
        for side in (0, 1):

            @pl.when(chains[which].has(side))
            def _():
                passing(which, side, 1, chains[which].place).start()

    loads["wq"].wait()
    loads["wk"].wait()
    loads["wv"].wait()

    def project(which, slot, fl, with_queries):
        index = bases[which] + slot

        def norm_rows(step):
            at = window(step, STEP)
            scaled, _ = scaled_rows(xg[index, at, :].astype(F32))
            fl[at, :] = (scaled * g1[...] + s1[...]).astype(BF)

        loop(rows // STEP, norm_rows, unroll=4)

        left = fl[...]
        flt[:, window(index, rows)] = jnp.transpose(left)
        keys = mm(left, wk[...]).astype(BF)
        for pair in range(pairs):
            k_all[pair, index] = keys[:, pair * PAIR : (pair + 1) * PAIR]
        values = (mm(left, wv[...]) + vb[...]).astype(BF)
        for pair in range(pairs):
            v_all[pair, index] = values[:, pair * PAIR : (pair + 1) * PAIR]
        if with_queries:
            queries = (mm(left, wq[...]) + qb[...]).astype(BF).astype(F32) * HEAD**-0.5
            for pair in range(pairs):
                part = queries[:, pair * PAIR : (pair + 1) * PAIR]
                low = low_half(part.shape)
                qst[which, pair, 0:rows] = jnp.where(low, part, 0.0).astype(BF)
                qst[which, pair, rows : 2 * rows] = jnp.where(low, 0.0, part).astype(BF)

    def attend(which, slot):
        index = bases[which] + slot

        def pair_step(pair):
            s = mm_nt(k_all[pair, index], qst[which, pair])
            before = m[which, pair]
            now = jnp.maximum(before, jnp.max(s, axis=0, keepdims=True))
            low = jnp.exp(s - now).astype(BF)
            decay = jnp.exp(before - now)
            m[which, pair] = now
            vt = jnp.transpose(v_all[pair, index])
            ones = jnp.ones((16, rows), BF)
            for head in range(2):
                feats = slice(head * HEAD, (head + 1) * HEAD)
                cols = slice(head * rows, (head + 1) * rows)
                mixed = mm(jnp.concatenate([vt[feats], ones], 0), low[:, cols])
                ot[which, pair, feats] = ot[which, pair, feats] * decay[:, cols] + mixed[0:HEAD]
                l[which, pair, :, cols] = l[which, pair, :, cols] * decay[:, cols] + mixed[HEAD : HEAD + 1]

        loop(pairs, pair_step, unroll=3)

    plan = Plan()
    places = [(number, 0, width) for number in range(MATRICES - 1)]
    places += [(MATRICES - 1, half * width // 2, width // 2) for half in (0, 1)]
    sums = []
    wholes = 0
    for number, (matrix, start, size) in enumerate(places):
        groups = groups_of(number, dp_bits, blk_bits)
        count = whole_count(size, groups)
        space = r["landing"].shape[1] // 2 if size < width else r["landing"].shape[1]
        slot = landing_slot(matrix, blocks)
        sums.append(
            Sum(
                plan,
                held.at[matrix, pl.ds(start, size)],
                r["landing"].at[slot, pl.ds(space if start else 0, space)],
                r["last"].at[pl.ds(wholes, count)],
                r["sums"].at[matrix, pl.ds(start, size)],
                r["sum_send"].at[number],
                r["sum_recv"].at[number],
                r["sum_free"].at[number],
                r["sum_out"].at[number],
                groups,
            )
        )
        wholes += count
    vector_sum = VectorSum(
        plan, r["vectors"], r["vector_landing"], r["vector_send"], r["vector_recv"], dp_bits + blk_bits
    )

    def pump(microseconds=0.0):
        plan.work(microseconds)
        for s in sums + [vector_sum]:
            if s.active and s.ends <= plan.now:
                s.step()

    def begin(number):
        slot = landing_slot(places[number][0], blocks)
        for other in range(number):
            if landing_slot(places[other][0], blocks) == slot and places[other][0] != places[number][0]:
                while not sums[other].over:
                    min((s for s in sums if s.active), key=lambda s: s.ends).step()
        sums[number].start()

    vacc[...] = jnp.zeros(vacc.shape, F32)
    vub[...] = jnp.zeros(vub.shape, F32)
    both = seqs * rows
    halves = [slice(0, rows), slice(rows, both)]

    def receive(which, step):
        chain = chains[which]
        for side in (0, 1):

            @pl.when(chain.has(side, step))
            def _():
                slot = chain.place + (step if side else -step)
                passing(which, 1 - side, step, slot).wait_recv()

                @pl.when(chain.has(1 - side))
                def _():
                    passing(which, 1 - side, step + 1, slot).start()

    def finish(which):
        def one(pair):
            total = l[which, pair]
            lse[which, pair] = m[which, pair] + jnp.log(total)
            share = 1.0 / total
            for head in range(2):
                feats = slice(head * HEAD, (head + 1) * HEAD)
                cols = slice(head * rows, (head + 1) * rows)
                ot[which, pair, feats] = ot[which, pair, feats] * share[:, cols]
            att[which, pair] = jnp.transpose(ot[which, pair])

        loop(pairs, one, unroll=3)

    def forward_and_feed(slow, active, ginner, gbranch):
        fl = gbranch.at[halves[0]]

        def use(which, step, side):
            chain = chains[which]

            @pl.when(chain.has(side, step))
            def _():
                slot = chain.place + (step if side else -step)
                project(which, slot, fl, False)
                attend(which, slot)

        def sort_rows(step):
            at = window(step, STEP)
            first, second = sort(cot[0, at, :].astype(F32), cot[1, at, :].astype(F32))
            vacc[DB] += fold(first) + fold(second)
            cot[0, at, :] = first.astype(BF)
            cot[1, at, :] = second.astype(BF)

        def attended(which, some):
            return jnp.concatenate([att[which, pair].astype(BF) for pair in some], 1)

        def branch(which):
            here = halves[which]
            hidden[here, :] = xg[own[which]].astype(F32) + (mm(attended(which, range(pairs)), wo[...]) + ob[...])

            def norm_rows(step):
                at = window(which * (rows // STEP) + step, STEP)
                scaled, _ = scaled_rows(hidden[at, :])
                slow[at, :] = (scaled * g2[...] + s2[...]).astype(BF)

            loop(rows // STEP, norm_rows, unroll=4)

        def up(which, part):
            here = halves[which]
            at = slice(part * width, (part + 1) * width)
            inner = mm(slow[here, :], wu[:, at]) + ub[:, at]
            grad_active = mm_nt(cot[which], wd[at, :])
            share = 0.5 * (1.0 + lax.erf(inner * (0.5**0.5)))
            slope = share + inner * (jnp.exp(-0.5 * inner * inner) * 0.3989422804014327)
            active[here, at] = (inner * share).astype(BF)
            low = (grad_active * slope).astype(BF)
            ginner[here, at] = low
            vub[:, at] += fold(low.astype(F32))

        def down(which):
            here = halves[which]
            held[MATRICES - 1, here, :] = (hidden[here, :] + (mm(active[here, :], wd[...]) + db[...])).astype(BF)

        def hidden_back(which, step):
            rows_at = window(step, STEP)
            at = window(which * (rows // STEP) + step, STEP)
            scaled, inverse = scaled_rows(hidden[at, :])
            inside = window(lax.rem(step, PAIR // STEP), STEP)
            block = step // (PAIR // STEP) * (width // TILE)
            grad = jnp.concatenate([ot[which, block + part, inside, :] for part in range(width // TILE)], 1)
            vacc[G2] += fold(grad * scaled)
            vacc[S2] += fold(grad)
            grad_hidden = cot[which, rows_at, :].astype(F32) + norm_back(grad, scaled, inverse, g2[...])
            hidden[at, :] = grad_hidden
            low = grad_hidden.astype(BF)
            gbranch[at, :] = low
            vacc[OB] += fold(low.astype(F32))

        def second_back(which):
            back = mm_nt(ginner[halves[which], :], wu[...])
            for part in range(rows // PAIR):
                for step in range(width // TILE):
                    ot[which, part * (width // TILE) + step] = back[
                        part * PAIR : (part + 1) * PAIR, step * TILE : (step + 1) * TILE
                    ]
            pump(1.0)
            loop(rows // STEP, partial(hidden_back, which), unroll=2)
            pump(0.7)

        def branch_back(which):
            low = mm_nt(gbranch[halves[which], :], wo[...]).astype(BF).astype(F32)
            for pair in range(pairs):
                part = low[:, pair * PAIR : (pair + 1) * PAIR]
                lower = low_half(part.shape)
                gst[which, pair, 0:rows] = jnp.where(lower, part, 0.0).astype(BF)
                gst[which, pair, rows : 2 * rows] = jnp.where(lower, 0.0, part).astype(BF)
                product = jnp.transpose(part * att[which, pair])
                delta[which, pair, :, 0:rows] = jnp.sum(product[0:HEAD], 0, keepdims=True)
                delta[which, pair, :, rows : 2 * rows] = jnp.sum(product[HEAD:PAIR], 0, keepdims=True)
            pump(1.0)

        m[...] = jnp.full(m.shape, FLOOR, F32)
        l[...] = jnp.zeros(l.shape, F32)
        ot[...] = jnp.zeros(ot.shape, F32)
        project(0, chains[0].place, fl, True)
        attend(0, chains[0].place)
        project(1, chains[1].place, fl, True)
        receive(0, 1)
        attend(1, chains[1].place)
        use(0, 1, 0)
        use(0, 1, 1)

        def alternate(step):
            receive(1, step)
            use(1, step, 0)
            use(1, step, 1)

        loop(chains[1].count, alternate, 1)
        if chains[0].count > 2:
            receive(0, 2)
        finish(1)

        for name in ("wo", "cotangent", "wu", "wd"):
            loads[name].wait()
        loop(rows // STEP, sort_rows, unroll=4)
        branch(1)
        up(1, 0)
        up(1, 1)
        down(1)
        second_back(1)
        branch_back(1)

        def single(step):
            use(0, step, 0)

            @pl.when(step + 1 < chains[0].count)
            def _():
                receive(0, step + 1)

            use(0, step, 1)

        loop(chains[0].count, single, 2)
        finish(0)
        for which in (0, 1):
            chain = chains[which]

            def sent(step):
                for side in (0, 1):
                    @pl.when(jnp.logical_and(chain.has(side), chain.has(1 - side, step - 1)))
                    def _():
                        passing(which, side, step, chain.place + (1 - step if side else step - 1)).wait_send()

            loop(chain.count, sent, 1)

        branch(0)
        for part in (0, 1):
            up(0, part)
            pump(2.0)

            def down_weights(step):
                at = window(part * (width // TILE) + step, TILE)
                held[2 * part, window(step, TILE), :] = mm_tn(active[:, at], cot[...].reshape(both, width)).astype(BF)

            for step in range(width // TILE):
                down_weights(step)
                pump(0.4)
            begin(2 * part)

            def up_weights(step):
                at = window(step, TILE)
                held[2 * part + 1, at, :] = mm_tn(slow[:, at], ginner[:, part * width : (part + 1) * width]).astype(BF)

            for step in range(width // TILE):
                up_weights(step)
                pump(0.4)
            begin(2 * part + 1)

        down(0)

        def layer_rows(step):
            at = window(step, STEP)
            to = window(rows // STEP + step, STEP)
            last = MATRICES - 1
            first, second = sort(held[last, at, :].astype(F32), held[last, to, :].astype(F32))
            held[last, at, :] = first.astype(BF)
            held[last, to, :] = second.astype(BF)

        loop(rows // STEP, layer_rows, unroll=4)
        layer_out = [
            pltpu.make_async_copy(held.at[MATRICES - 1, halves[n]], r["layer_out"].at[n], r["out_sems"].at[n])
            for n in (0, 1)
        ]
        for copy in layer_out:
            copy.start()
        pump(1.3)
        second_back(0)

        def output_weights(step):
            at = window(step, TILE)
            left = jnp.concatenate([attended(which, (2 * step, 2 * step + 1)) for which in (0, 1)], 0)
            held[4, at, :] = mm_tn(left, gbranch[...]).astype(BF)

        for step in range(width // TILE):
            output_weights(step)
            pump(0.4)
        begin(4)
        branch_back(0)
        for copy in layer_out:
            copy.wait()

    pl.run_scoped(
        forward_and_feed,
        pltpu.VMEM((both, width), BF),
        pltpu.VMEM((both, inner_width), BF),
        pltpu.VMEM((both, inner_width), BF),
        pltpu.VMEM((both, width), BF),
    )

    ot[...] = jnp.zeros(ot.shape, F32)
    grad_in, grad_out = r["grad_in"], xg
    in_bases = [0, blocks + 1]

    def returning(which, side, slot):
        chain = chains[which]
        arrives = jnp.logical_and(slot == chain.place + (1 if side else -1), side == 0)
        index = in_bases[which] + jnp.where(arrives, chain.count, slot)
        return Pieces(
            grad_out.at[bases[which] + slot],
            grad_in.at[index],
            rows,
            r["g_send"].at[which, slot],
            r["g_recv"].at[index],
            chain.device(side),
        )

    def arrived(which, side, slot):
        index = in_bases[which] + jnp.where(jnp.logical_and(slot == chains[which].place, side == 0), chains[which].count, slot)
        ref = grad_in.at[index]
        Pieces(ref, ref, rows, r["g_send"].at[which, 0], r["g_recv"].at[index], {"blk": mate}).wait_recv()
        return index

    def attention_backward(grad):
        dq = cot

        def pair_back(which, index, pair):
            k, v, q, g = k_all[pair, index], v_all[pair, index], qst[which, pair], gst[which, pair]
            p = jnp.exp(mm_nt(k, q) - lse[which, pair])
            low = (p * (mm_nt(v, g) - delta[which, pair])).astype(BF)
            value_grad = mm(p.astype(BF), g)
            vacc[VB, :, window(pair, PAIR)] += fold(value_grad)
            v_all[pair, index] = value_grad.astype(BF)
            k_all[pair, index] = mm(low, q).astype(BF)
            kt = jnp.transpose(k)
            for head in range(2):
                feats = slice(head * HEAD, (head + 1) * HEAD)
                ot[which, pair, feats] += mm(kt[feats], low[:, head * rows : (head + 1) * rows])

        def slot_back(which, index, group):
            for pair in group:
                pair_back(which, index, pair)
                pump(1.1)

        def joined(values, index):
            return jnp.concatenate([values[pair, index] for pair in range(pairs)], 1)

        def give(which, number):
            chain = chains[which]
            slot, side = chain.visit(number)
            index = bases[which] + slot
            grad[0:rows, :] = mm_nt(joined(k_all, index), wk[...]) + mm_nt(joined(v_all, index), wv[...])

            def gather_rows(step):
                at = window(step, STEP)
                scaled, _ = scaled_rows(xg[index, at, :].astype(F32))
                values = grad[at, :]
                vacc[G1] += fold(values * scaled)
                vacc[S1] += fold(values)
                grad_out[index, at, :] = values.astype(BF)

            loop(rows // STEP, gather_rows, unroll=2)
            for toward in (0, 1):

                @pl.when(jnp.logical_and(side == toward, jnp.logical_not(chain.has(1 - toward))))
                def _():
                    returning(which, toward, slot).start()

            for link in ("inner", "outer"):
                plan.send(link, rows * width * 2)
            pump(1.8)

        def relay(which, distance, number):
            chain = chains[which]
            slot, side = chain.visit(number)
            for toward in (0, 1):
                behind = chain.place if toward else chain.count - 1 - chain.place

                @pl.when(jnp.logical_and(side == toward, behind == distance))
                def _():
                    place = arrived(which, toward, slot)

                    def add(step):
                        at = window(step, STEP)
                        out = bases[which] + slot
                        grad_out[out, at, :] = (
                            grad_out[out, at, :].astype(F32) + grad_in[place, at, :].astype(F32)
                        ).astype(BF)

                    loop(rows // STEP, add, unroll=4)
                    returning(which, toward, slot).start()

        def other(which, number):
            return bases[which] + chains[which].visit(number)[0]

        def query_rows(which, pair):
            value = jnp.transpose(ot[which, pair]) * HEAD**-0.5
            vacc[QB, :, window(pair, PAIR)] += fold(value)
            dq[which, :, window(pair, PAIR)] = value.astype(BF)

        def weights(group, step):
            at = window(step, TILE)
            number = 5 + group
            pair = 2 * group
            flat = (k_all.shape[1] * rows, PAIR)
            right = jnp.concatenate(
                [k_all[pair].reshape(flat), k_all[pair + 1].reshape(flat)]
                + [v_all[pair].reshape(flat), v_all[pair + 1].reshape(flat)],
                1,
            )
            held[number, at, TILE : 3 * TILE] = mm(flt[at, :], right).astype(BF)
            columns = window(group, TILE)
            held[number, at, 0:TILE] = sum(
                mm(flt[at, window(own[which], rows)], dq[which, :, columns]) for which in (0, 1)
            ).astype(BF)

        groups_of_heads = [(2 * group, 2 * group + 1) for group in range(pairs // 2)]
        alternate = [(1, n) for n in range(chains[1].count - 1)]
        singles = [(0, n) for n in range(chains[0].count - 1)]
        for which, number in alternate:
            slot_back(which, other(which, number), range(pairs))
            give(which, number)
        slot_back(1, own[1], range(pairs))
        for pair in range(pairs):
            query_rows(1, pair)
        for group, members in enumerate(groups_of_heads):
            final = group == len(groups_of_heads) - 1
            for which, number in singles:
                slot_back(which, other(which, number), members)
                if final:
                    give(which, number)
                    given = plan.now
            slot_back(0, own[0], members)
            for pair in members:
                query_rows(0, pair)
            for step in range(width // TILE):
                weights(group, step)
                pump(0.8)
                if final and step == (width // TILE) // 2:
                    begin(7)
            begin(8 if final else 5 + group)
            pump()
        for which in (0, 1):
            grad[halves[which], :] = (
                mm_nt(joined(k_all, own[which]), wk[...])
                + mm_nt(joined(v_all, own[which]), wv[...])
                + mm_nt(dq[which], wq[...])
            )
        pump(2.5)
        for which in (0, 1):

            def own_rows(step):
                at = window(step, STEP)
                to = window(which * (rows // STEP) + step, STEP)
                scaled, _ = scaled_rows(xg[own[which], at, :].astype(F32))
                values = grad[to, :]
                vacc[G1] += fold(values * scaled)
                vacc[S1] += fold(values)

            loop(rows // STEP, own_rows, unroll=2)

        vectors = r["vectors"]
        vectors[...] = jnp.zeros(vectors.shape, F32)
        for number in range(UB):
            vectors[number : number + 1, :] = jnp.sum(vacc[number], 0, keepdims=True)
        for part in range(inner_width // width):
            vectors[UB + part : UB + part + 1, :] = jnp.sum(vub[:, part * width : (part + 1) * width], 0, keepdims=True)
        vector_sum.start()
        pump(1.0)

        def drain(until):
            while True:
                left = [s for s in sums + [vector_sum] if s.active]
                if not left or min(s.ends for s in left) > until:
                    return
                min(left, key=lambda s: s.ends).step()

        hop = HOP + rows * width * 4 / 1e5
        for distance in range(1, chains[0].count - 1):
            drain(given + distance * hop)
            for which in (1, 0):
                if distance < chains[which].count - 1:
                    loop(chains[which].count - 1, partial(relay, which, distance))
        drain(given + (chains[0].count - 1) * hop)
        for which in (0, 1):
            for side in (0, 1):

                @pl.when(chains[which].has(1 - side))
                def _():
                    place = arrived(which, side, chains[which].place)

                    def add(step):
                        to = window(which * (rows // STEP) + step, STEP)
                        grad[to, :] += grad_in[place, window(step, STEP), :].astype(F32)

                    loop(rows // STEP, add, unroll=4)

        pump(0.8)

        def tokens_back(step):
            at = window(step, STEP)
            parts = []
            for which in (0, 1):
                to = window(which * (rows // STEP) + step, STEP)
                scaled, inverse = scaled_rows(xg[own[which], at, :].astype(F32))
                parts.append(hidden[to, :] + norm_back(grad[to, :], scaled, inverse, g1[...]))
            first, second = sort(*parts)
            cot[0, at, :] = first.astype(BF)
            cot[1, at, :] = second.astype(BF)

        loop(rows // STEP, tokens_back, unroll=2)
        tokens_out = pltpu.make_async_copy(cot, r["tokens_grad"], r["out_sems"].at[2])
        tokens_out.start()
        pump(1.0)

        for which, number in alternate + singles:
            slot, side = chains[which].visit(number)
            for toward in (0, 1):

                @pl.when(side == toward)
                def _():
                    returning(which, toward, slot).wait_send()

        drain(float("inf"))
        for s in sums:
            s.settle().wait()
        tokens_out.wait()

    pl.run_scoped(attention_backward, pltpu.VMEM((both, width), F32))


def run_layer(operands):
    blocks, groups = lax.axis_size("blk"), lax.axis_size("dp")
    seqs, rows, width = operands["tokens"].shape
    inner = operands["ub"].shape[0]
    pairs = width // PAIR
    slots = blocks + blocks // 2
    bits = (blocks * groups).bit_length() - 1
    places = [width] * (MATRICES - 1) + [width // 2] * 2
    orders = [groups_of(n, axis_bits("dp", groups), axis_bits("blk", blocks)) for n in range(len(places))]
    landing = max(
        landing_rows(size, order) * (width // size) for size, order in zip(places, orders, strict=True)
    )
    landing = (landing + 31) // 32 * 32
    wholes = sum(whole_count(size, order) for size, order in zip(places, orders, strict=True))
    last = max(
        part for size, order in zip(places, orders, strict=True) for part, split in halving(size, order) if not split
    )
    landings = 1 + max(landing_slot(matrix, blocks) for matrix in range(MATRICES))
    vmem = pl.BlockSpec(memory_space=pltpu.VMEM)
    hbm = pl.BlockSpec(memory_space=pl.ANY)
    out_shape = {
        "layer_out": jax.ShapeDtypeStruct((seqs, rows, width), BF),
        "tokens_grad": jax.ShapeDtypeStruct((seqs, rows, width), BF),
        "sums": jax.ShapeDtypeStruct((MATRICES, width, width), BF),
        "vectors": jax.ShapeDtypeStruct((16, width), F32),
    }
    dma = pltpu.SemaphoreType.DMA
    scratch = {name + "_v": pltpu.VMEM(operands[name].shape, BF) for name in LARGE if name[0] == "w"}
    scratch |= {
        "cot_v": pltpu.VMEM((seqs, rows, width), BF),
        "rows": pltpu.VMEM((len(SMALL), width), F32),
        "ub_v": pltpu.VMEM((1, inner), F32),
        "small_sems": dma((len(SMALL) + 1,)),
        "theirs": pltpu.VMEM((seqs, rows), jnp.int32),
        "xg": pltpu.VMEM((slots, rows, width), BF),
        "flt": pltpu.VMEM((width, slots * rows), BF),
        "k_all": pltpu.VMEM((pairs, slots, rows, PAIR), BF),
        "v_all": pltpu.VMEM((pairs, slots, rows, PAIR), BF),
        "qst": pltpu.VMEM((seqs, pairs, 2 * rows, PAIR), BF),
        "gst": pltpu.VMEM((seqs, pairs, 2 * rows, PAIR), BF),
        "m": pltpu.VMEM((seqs, pairs, 1, 2 * rows), F32),
        "l": pltpu.VMEM((seqs, pairs, 1, 2 * rows), F32),
        "lse": pltpu.VMEM((seqs, pairs, 1, 2 * rows), F32),
        "delta": pltpu.VMEM((seqs, pairs, 1, 2 * rows), F32),
        "ot": pltpu.VMEM((seqs, pairs, PAIR, rows), F32),
        "att": pltpu.VMEM((seqs, pairs, rows, PAIR), F32),
        "hidden": pltpu.VMEM((seqs * rows, width), F32),
        "vacc": pltpu.VMEM((UB, 8, width), F32),
        "vub": pltpu.VMEM((8, inner), F32),
        "held": pltpu.VMEM((MATRICES, width, width), BF),
        "landing": pltpu.VMEM((landings, landing, width), BF),
        "last": pltpu.VMEM((wholes, last, width), BF),
        "vector_landing": pltpu.VMEM((bits, 16, width), F32),
        "grad_in": pltpu.VMEM((slots + 2, rows, width), BF),
        "out_sems": dma((3,)),
        "load_sems": dma((len(LARGE),)),
        "scene_sems": dma((2,)),
        "x_send": dma((2, 2, blocks + 1, PIECES)),
        "x_recv": dma((2, 2, blocks + 1, PIECES)),
        "g_send": dma((2, blocks, PIECES)),
        "g_recv": dma((slots + 2, PIECES)),
        "sum_send": dma((len(places), 2 * bits, 4)),
        "sum_recv": dma((len(places), 2 * bits, 4)),
        "sum_free": pltpu.SemaphoreType.REGULAR((len(places), bits, 4)),
        "sum_out": dma((len(places),)),
        "vector_send": dma((bits,)),
        "vector_recv": dma((bits,)),
    }
    names = tuple(operands) + tuple(out_shape) + tuple(scratch)
    return pl.pallas_call(
        partial(layer_kernel, blocks, groups, names),
        out_shape=tuple(out_shape.values()),
        in_specs=[vmem if name == "scenes" else hbm for name in operands],
        out_specs=(hbm, hbm, hbm, vmem),
        scratch_shapes=list(scratch.values()),
        compiler_params=pltpu.CompilerParams(
            collective_id=0, has_side_effects=True, vmem_limit_bytes=int(63.8 * 2**20)
        ),
    )(*operands.values())


def spread_kernel(layer_out, tokens_grad, sums, vectors, *refs):
    outs, (narrow, wide, passed, in_sems, out_sems, pass_sems, vector_sems) = refs[:17], refs[17:]
    down, up, out, query, key, value = outs[2:8]
    width = sums.shape[1]
    half = width // 2
    order = [5, 6, 7, 0, 1, 2, 3, 4]
    loads = {}
    for number in order:
        for part in range(2):
            at = pl.ds(part * half, half)
            loads[number, part] = pltpu.make_async_copy(
                sums.at[number, at], narrow.at[number, at], in_sems.at[number, part]
            )
            loads[number, part].start()
    passing = []
    for n, source in enumerate((layer_out, tokens_grad)):
        passing.append(pltpu.make_async_copy(source, passed.at[n], pass_sems.at[0, n]))
        passing[-1].start()
    stores = [pltpu.make_async_copy(vectors.at[n], outs[8 + n], vector_sems.at[n]) for n in range(UB)]
    for part in range(2):
        target = outs[8 + UB].at[pl.ds(part * width, width)]
        stores.append(pltpu.make_async_copy(vectors.at[UB + part], target, vector_sems.at[UB + part]))
    for store in stores:
        store.start()

    def send(number, part, target):
        at = pl.ds(part * half, half)
        stores.append(pltpu.make_async_copy(wide.at[number, at], target, out_sems.at[number, part]))
        stores[-1].start()

    for number in order:
        for part in range(2):
            loads[number, part].wait()

            def widen(step):
                at = window(part * (half // STEP) + step, STEP)
                if number < 5:
                    wide[number, at] = narrow[number, at].astype(F32)
                else:
                    columns = pl.ds((number - 5) * TILE, TILE)
                    for n in range(3):
                        wide[5 + n, at, columns] = narrow[number, at, n * TILE : (n + 1) * TILE].astype(F32)

            loop(half // STEP, widen, unroll=4)
            at = pl.ds(part * half, half)
            if number in (0, 2):
                send(number, part, down.at[pl.ds(number // 2 * width + part * half, half)])
            elif number in (1, 3):
                send(number, part, up.at[at, pl.ds(number // 2 * width, width)])
            elif number == 4:
                send(number, part, out.at[at])
            elif number == MATRICES - 1:
                for n, matrix in enumerate((query, key, value)):
                    send(5 + n, part, matrix.at[at])
        if number == 7:
            for n in (0, 1):
                passing[n].wait()
                stores.append(pltpu.make_async_copy(passed.at[n], outs[n], pass_sems.at[1, n]))
                stores[-1].start()
    for store in stores:
        store.wait()


def spread(layer_out, tokens_grad, sums, vectors):
    width = sums.shape[1]
    matrices = [(2 * width, width), (width, 2 * width)] + [(width, width)] * 4
    shapes = [jax.ShapeDtypeStruct(value.shape, BF) for value in (layer_out, tokens_grad)]
    shapes += [jax.ShapeDtypeStruct(shape, F32) for shape in matrices + [(width,)] * UB + [(2 * width,)]]
    hbm = pl.BlockSpec(memory_space=pl.ANY)
    return pl.pallas_call(
        spread_kernel,
        out_shape=tuple(shapes),
        in_specs=[hbm, hbm, hbm, pl.BlockSpec(memory_space=pltpu.VMEM)],
        out_specs=(hbm,) * len(shapes),
        scratch_shapes=[
            pltpu.VMEM(sums.shape, BF),
            pltpu.VMEM(sums.shape, F32),
            pltpu.VMEM((2,) + layer_out.shape, BF),
            pltpu.SemaphoreType.DMA((MATRICES, 2)),
            pltpu.SemaphoreType.DMA((MATRICES, 2)),
            pltpu.SemaphoreType.DMA((2, 2)),
            pltpu.SemaphoreType.DMA((UB + 2,)),
        ],
        compiler_params=pltpu.CompilerParams(vmem_limit_bytes=63 * 2**20),
    )(layer_out, tokens_grad, sums, vectors)


def on_device(
    tokens,
    scene_ids,
    query_weight,
    query_bias,
    key_weight,
    value_weight,
    value_bias,
    output_weight,
    output_bias,
    first_gain,
    first_shift,
    second_gain,
    second_shift,
    up_weight,
    up_bias,
    down_weight,
    down_bias,
    cotangent,
):
    operands = {
        "tokens": tokens,
        "scenes": scene_ids,
        "wq": query_weight,
        "wk": key_weight,
        "wv": value_weight,
        "wo": output_weight,
        "wu": up_weight,
        "wd": down_weight,
        "cotangent": cotangent,
        "qb": query_bias,
        "vb": value_bias,
        "ob": output_bias,
        "g1": first_gain,
        "s1": first_shift,
        "g2": second_gain,
        "s2": second_shift,
        "ub": up_bias,
        "db": down_bias,
    }
    (
        layer_out,
        tokens_grad,
        down_grad,
        up_grad,
        output_grad,
        query_grad,
        key_grad,
        value_grad,
        query_bias_grad,
        value_bias_grad,
        output_bias_grad,
        first_gain_grad,
        first_shift_grad,
        second_gain_grad,
        second_shift_grad,
        down_bias_grad,
        up_bias_grad,
    ) = spread(*run_layer(operands))
    return (
        layer_out,
        tokens_grad,
        query_grad,
        query_bias_grad,
        key_grad,
        value_grad,
        value_bias_grad,
        output_grad,
        output_bias_grad,
        first_gain_grad,
        first_shift_grad,
        second_gain_grad,
        second_shift_grad,
        up_grad,
        up_bias_grad,
        down_grad,
        down_bias_grad,
    )


def solution(mesh):
    split = P("dp", "blk", None)
    in_specs = (split, P("dp", "blk")) + (P(),) * 15 + (split,)
    out_specs = (split, split) + (P(),) * 15
    return jax.shard_map(on_device, mesh=mesh, in_specs=in_specs, out_specs=out_specs, check_vma=False)
```

```python
from functools import partial

import jax
import jax.numpy as jnp
from jax import lax
from jax.experimental import pallas as pl
from jax.experimental.pallas import tpu as pltpu
from jax.sharding import PartitionSpec as P

HEAD = 64
PAIR = 2 * HEAD
EPS = 1e-05
FLOOR = -1e30
MESH = pl.DeviceIdType.MESH
BF = jnp.bfloat16
F32 = jnp.float32
NT = (((1,), (1,)), ((), ()))
TN = (((0,), (0,)), ((), ()))
STEP = 32
TILE = 256
MATRICES = 8
PIECES = 1
HOP = 4.0
LARGE = ("tokens", "wq", "wk", "wv", "wo", "wu", "wd", "cotangent")
SMALL = ("qb", "vb", "ob", "g1", "s1", "g2", "s2", "db")
QB, VB, OB, G1, S1, G2, S2, DB, UB = range(9)


def mm(a, b):
    return jnp.dot(a, b, preferred_element_type=F32)


def mm_nt(a, b):
    return lax.dot_general(a, b, NT, preferred_element_type=F32)


def mm_tn(a, b):
    return lax.dot_general(a, b, TN, preferred_element_type=F32)


def scaled_rows(values):
    mean = jnp.mean(values, -1, keepdims=True)
    centred = values - mean
    inverse = lax.rsqrt(jnp.mean(centred * centred, -1, keepdims=True) + EPS)
    return centred * inverse, inverse


def norm_back(grad_norm, scaled, inverse, gain):
    grad_scaled = grad_norm * gain
    mean_grad = jnp.mean(grad_scaled, -1, keepdims=True)
    mean_cross = jnp.mean(grad_scaled * scaled, -1, keepdims=True)
    return inverse * (grad_scaled - mean_grad - scaled * mean_cross)


def low_half(shape):
    return lax.broadcasted_iota(jnp.int32, shape, 1) < HEAD


def fold(values):
    return jnp.sum(values.reshape(values.shape[0] // 8, 8, values.shape[1]), 0)


def window(step, size):
    return pl.ds(step * size if isinstance(step, int) else pl.multiple_of(step * size, size), size)


def loop(count, body, first=0, unroll=1):
    unroll = min(unroll, count - first)
    while (count - first) % max(unroll, 1):
        unroll -= 1

    def one(step, carry):
        for inner in range(unroll):
            body(first + step * unroll + inner)
        return carry

    if unroll and unroll == count - first:
        one(0, 0)
    elif unroll:
        lax.fori_loop(0, (count - first) // unroll, one, 0)


class Pieces:
    def __init__(self, src, dst, rows, send_sems, recv_sems, device):
        count = pieces(rows)
        size = rows // count
        self.copies = [
            pltpu.make_async_remote_copy(
                src_ref=src.at[pl.ds(n * size, size)],
                dst_ref=dst.at[pl.ds(n * size, size)],
                send_sem=send_sems.at[n],
                recv_sem=recv_sems.at[n],
                device_id=device,
                device_id_type=MESH,
            )
            for n in range(count)
        ]

    def start(self):
        for copy in self.copies:
            copy.start()

    def wait_send(self):
        for copy in self.copies:
            copy.wait_send()

    def wait_recv(self):
        for copy in self.copies:
            copy.wait_recv()


def pieces(rows):
    return max(1, min(PIECES, rows // 48))


class Chain:
    def __init__(self, me, blocks, stride):
        self.stride = stride
        self.count = blocks // stride
        self.place = me // stride
        self.me = me

    def device(self, side):
        return {"blk": self.me + (self.stride if side else -self.stride)}

    def has(self, side, steps=1):
        if side:
            return self.place + steps < self.count
        return self.place - steps >= 0

    def visit(self, number):
        rights, lefts = self.count - 1 - self.place, self.place
        both = jnp.minimum(rights, lefts)
        paired = number < 2 * both
        side = jnp.where(paired, 1 - number % 2, jnp.where(rights > lefts, 1, 0))
        index = jnp.where(paired, number // 2, number - both)
        return jnp.where(side == 1, self.count - 1 - index, index), side


class Plan:
    def __init__(self):
        self.now = 0.0
        self.busy = {}

    def work(self, microseconds):
        self.now += 0.75 * microseconds

    def send(self, link, size, hops=1):
        fast = link == ("dp", 1)
        length = size / 3e5 if fast else hops * 2 * size / 1e5
        end = max(self.now, self.busy.get(link, 0.0)) + length
        self.busy[link] = end
        return end + HOP


def others(group):
    values = [lax.rem(lax.axis_index(axis) // bit, 2) for axis, bit in group]
    result = []
    for mask in range(1 << len(group)):
        device, place = {}, 0
        for n, ((axis, bit), value) in enumerate(zip(group, values, strict=True)):
            flip = mask >> n & 1
            place = place + ((1 - value) if flip else value) * (1 << n)
            if flip:
                device[axis] = device.get(axis, lax.axis_index(axis)) + bit * (1 - 2 * value)
        result.append((device, place))
    return result


class Sum:
    def __init__(self, plan, held, landing, last, out, send_sems, recv_sems, free_sems, out_sem, groups):
        self.plan, self.held, self.landing, self.last = plan, held, landing, last
        self.out, self.send_sems, self.recv_sems, self.out_sem = out, send_sems, recv_sems, out_sem
        self.free_sems = free_sems
        start, base, wholes = 0, 0, 0
        self.stages = []
        undo = []
        for group, (rows, split) in zip(groups, halving(held.shape[0], groups), strict=True):
            ways = others(group)
            if split:
                starts = [start + place * rows for _, place in ways]
                self.stages.append(("split", group, ways, starts, rows, base))
                undo.append(("back", group, ways, starts, rows, base))
                base += (len(ways) - 1) * rows
                start = starts[0]
            else:
                self.stages.append(("whole", group, ways, [start] * len(ways), rows, wholes))
                wholes += len(ways) - 1
        self.stages += undo[::-1]
        self.done = -1
        self.ends = 0.0

    def settle(self):
        return pltpu.make_async_copy(self.held, self.out, self.out_sem)

    def part(self, start, rows):
        return self.held.at[pl.ds(pl.multiple_of(start, 16), rows)]

    def copies(self, number):
        kind, _, ways, starts, rows, base = self.stages[number]
        result = []
        for mask in range(1, len(ways)):
            source = self.part(starts[0] if kind == "back" else starts[mask], rows)
            if kind == "split":
                target = self.landing.at[pl.ds(base + (mask - 1) * rows, rows)]
            elif kind == "whole":
                target = self.last.at[base + mask - 1, pl.ds(0, rows)]
            else:
                target = source
            result.append(self.move(number, mask, source, target))
        return result

    def arrivals(self, number):
        kind, _, ways, starts, rows, _ = self.stages[number]
        if kind != "back":
            return self.copies(number)
        parts = [self.part(start, rows) for start in starts]
        return [self.move(number, mask, parts[mask], parts[mask]) for mask in range(1, len(ways))]

    def move(self, number, mask, source, target):
        return pltpu.make_async_remote_copy(
            src_ref=source,
            dst_ref=target,
            send_sem=self.send_sems.at[number, mask],
            recv_sem=self.recv_sems.at[number, mask],
            device_id=self.stages[number][2][mask][0],
            device_id_type=MESH,
        )

    def start(self):
        self.begin(0)

    def begin(self, number):
        self.done = number
        kind, group, ways, _, rows, _ = self.stages[number]
        for mask, copy in enumerate(self.copies(number), 1):
            if kind == "back":
                pl.semaphore_wait(self.free_sems.at[len(self.stages) - 1 - number, mask], 1)
            copy.start()
        size = rows * self.held.shape[1] * 2
        self.ends = 0.0
        for axis, bit in group:
            if axis == "blk":
                inner, outer = (4, 3) if len(group) > 1 else (0, 1) if bit == 1 else (2, 1)
                for link, hops in (("inner", inner), ("outer", outer)):
                    if hops:
                        self.ends = max(self.ends, self.plan.send(link, size, hops))
                break
            self.ends = max(self.ends, self.plan.send((axis, bit), size, len(group)))

    @property
    def active(self):
        return 0 <= self.done < len(self.stages)

    @property
    def over(self):
        return self.done == len(self.stages)

    def step(self):
        number = self.done
        kind, _, ways, starts, rows, base = self.stages[number]
        for mask, copy in enumerate(self.copies(number), 1):
            copy.wait_send()
            if kind == "split":
                pl.semaphore_signal(
                    self.free_sems.at[number, mask], inc=1, device_id=ways[mask][0], device_id_type=MESH
                )
        for copy in self.arrivals(number):
            copy.wait_recv()
        self.plan.now = max(self.plan.now, self.ends)
        if kind != "back":
            block = 48 if rows % 48 == 0 else 16

            def add(step):
                at = pl.ds(pl.multiple_of(starts[0] + step * block, 16), block)
                terms = [self.held[at].astype(F32)]
                for mask in range(1, len(ways)):
                    if kind == "split":
                        here = base + (mask - 1) * rows + step * block
                        came = self.landing[pl.ds(pl.multiple_of(here, 16), block)]
                    else:
                        came = self.last[base + mask - 1, pl.ds(pl.multiple_of(step * block, 16), block)]
                    terms.append(came.astype(F32))
                while len(terms) > 1:
                    terms = [terms[n] + terms[n + 1] for n in range(0, len(terms), 2)]
                self.held[at] = terms[0].astype(BF)

            loop(rows // block, add, unroll=2)
            self.plan.work(0.2 + rows * 0.001)
        if number + 1 < len(self.stages):
            self.begin(number + 1)
        else:
            self.done = number + 1
            self.settle().start()


class VectorSum:
    def __init__(self, plan, held, landing, send_sems, recv_sems, bits):
        self.plan, self.held, self.landing = plan, held, landing
        self.send_sems, self.recv_sems = send_sems, recv_sems
        self.partners = []
        for axis, bit in bits:
            mine = lax.axis_index(axis)
            self.partners.append({axis: mine + bit * (1 - 2 * lax.rem(mine // bit, 2))})
        self.done = -1
        self.ends = 0.0

    def copy(self, number):
        return pltpu.make_async_remote_copy(
            src_ref=self.held,
            dst_ref=self.landing.at[number],
            send_sem=self.send_sems.at[number],
            recv_sem=self.recv_sems.at[number],
            device_id=self.partners[number],
            device_id_type=MESH,
        )

    def start(self):
        self.begin(0)

    def begin(self, number):
        self.done = number
        self.copy(number).start()
        self.ends = self.plan.now + HOP

    @property
    def active(self):
        return 0 <= self.done < len(self.partners)

    def step(self):
        self.copy(self.done).wait()
        self.plan.now = max(self.plan.now, self.ends)
        self.held[...] = self.held[...] + self.landing[self.done]
        if self.done + 1 < len(self.partners):
            self.begin(self.done + 1)
        else:
            self.done += 1


def landing_slot(matrix, blocks):
    return matrix if blocks <= 4 else matrix % 4


def halving(rows, groups):
    plan = []
    for position, group in enumerate(groups):
        parts = 1 << len(group)
        split = rows % (16 * parts) == 0 and position < len(groups) - 1
        if split:
            rows //= parts
        plan.append((rows, split))
    return plan


def whole_count(rows, groups):
    return sum((1 << len(group)) - 1 for group, (_, split) in zip(groups, halving(rows, groups), strict=True) if not split)


def landing_rows(rows, groups):
    return sum(
        ((1 << len(group)) - 1) * part for group, (part, split) in zip(groups, halving(rows, groups), strict=True) if split
    )


def groups_of(number, dp_bits, blk_bits):
    rest = dp_bits[1:] if number % 2 == 0 else dp_bits[:0:-1]
    planar = [rest[:2]] if number >= 2 else [[bit] for bit in rest[:2]]
    groups = [dp_bits[:1]] + planar + [[bit] for bit in rest[2:] + blk_bits]
    return [group for group in groups if group]


def axis_bits(axis, size):
    return [(axis, 1 << bit) for bit in range(size.bit_length() - 1)]


def layer_kernel(blocks, groups, names, *refs):
    r = dict(zip(names, refs, strict=True))
    tokens_in, scenes, cot_in = r["tokens"], r["scenes"], r["cotangent"]
    small = {name: r["rows"].at[n : n + 1] for n, name in enumerate(SMALL)} | {"ub": r["ub_v"]}
    qb, vb, ob, g1, s1, g2, s2, db, ub = (small[name] for name in SMALL + ("ub",))
    flt = r["flt"]
    xg, k_all, v_all, qst, gst = r["xg"], r["k_all"], r["v_all"], r["qst"], r["gst"]
    m, l, lse, delta, ot, att = r["m"], r["l"], r["lse"], r["delta"], r["ot"], r["att"]
    held, hidden = r["held"], r["hidden"]
    vacc, vub = r["vacc"], r["vub"]
    seqs, rows, width = tokens_in.shape
    inner_width = ub.shape[1]
    pairs = width // PAIR
    me = lax.axis_index("blk")
    chains = [Chain(me, blocks, 1), Chain(me, blocks, 2)]
    bases = [0, blocks]
    own = [chains[0].place, blocks + chains[1].place]
    mate = me + 1 - 2 * lax.rem(me, 2)
    dp_bits, blk_bits = axis_bits("dp", groups), axis_bits("blk", blocks)

    vector_loads = []
    for number, name in enumerate(SMALL + ("ub",)):
        place = r["ub_v"].at[0] if name == "ub" else r["rows"].at[number]
        vector_loads.append(pltpu.make_async_copy(r[name], place, r["small_sems"].at[number]))
        vector_loads[-1].start()
    loads = {}
    for number, name in enumerate(LARGE):
        place = r["cot_v"] if name in ("tokens", "cotangent") else r[name + "_v"]
        loads[name] = pltpu.make_async_copy(r[name], place, r["load_sems"].at[number])
        if name != "cotangent":
            loads[name].start()
    tokens = cot = r["cot_v"]
    wq, wk, wv, wo, wu, wd = (r[n + "_v"] for n in ("wq", "wk", "wv", "wo", "wu", "wd"))

    barrier = pltpu.get_barrier_semaphore()
    total = 0
    for chain in chains:
        for side in (0, 1):

            @pl.when(chain.has(side))
            def _():
                pl.semaphore_signal(barrier, inc=1, device_id=chain.device(side), device_id_type=MESH)

            total = total + chain.has(side).astype(jnp.int32)
    everyone = {tuple(group) for n in range(MATRICES + 1) for group in groups_of(n, dp_bits, blk_bits)}
    for group in sorted(everyone):
        for device, _ in others(group)[1:]:
            pl.semaphore_signal(barrier, inc=1, device_id=device, device_id_type=MESH)
            total = total + 1
    pl.semaphore_wait(barrier, total)

    swap = pltpu.make_async_remote_copy(
        src_ref=scenes,
        dst_ref=r["theirs"],
        send_sem=r["scene_sems"].at[0],
        recv_sem=r["scene_sems"].at[1],
        device_id={"blk": mate},
        device_id_type=MESH,
    )
    swap.start()
    for load in vector_loads:
        load.wait()
    loads["tokens"].wait()
    swap.wait()
    ordered = jnp.where(scenes[0:1, 0:1] == r["theirs"][0:1, 0:1], 1.0, 0.0)

    def sort(first, second):
        w = jnp.broadcast_to(ordered, first.shape)
        return w * first + (1.0 - w) * second, w * second + (1.0 - w) * first

    def place_rows(step):
        at = window(step, STEP)
        first, second = sort(tokens[0, at, :].astype(F32), tokens[1, at, :].astype(F32))
        xg[own[0], at, :] = first.astype(BF)
        xg[own[1], at, :] = second.astype(BF)

    loop(rows // STEP, place_rows, unroll=4)
    loads["cotangent"].start()

    def passing(which, side, step, slot):
        place = xg.at[bases[which] + slot]
        send, recv = r["x_send"].at[which, side, step], r["x_recv"].at[which, 1 - side, step]
        return Pieces(place, place, rows, send, recv, chains[which].device(side))

    for which in (0, 1):
        for side in (0, 1):

            @pl.when(chains[which].has(side))
            def _():
                passing(which, side, 1, chains[which].place).start()

    loads["wq"].wait()
    loads["wk"].wait()
    loads["wv"].wait()

    def project(which, slot, fl, with_queries):
        index = bases[which] + slot

        def norm_rows(step):
            at = window(step, STEP)
            scaled, _ = scaled_rows(xg[index, at, :].astype(F32))
            fl[at, :] = (scaled * g1[...] + s1[...]).astype(BF)

        loop(rows // STEP, norm_rows, unroll=4)

        left = fl[...]
        flt[:, window(index, rows)] = jnp.transpose(left)
        keys = mm(left, wk[...]).astype(BF)
        for pair in range(pairs):
            k_all[pair, index] = keys[:, pair * PAIR : (pair + 1) * PAIR]
        values = (mm(left, wv[...]) + vb[...]).astype(BF)
        for pair in range(pairs):
            v_all[pair, index] = values[:, pair * PAIR : (pair + 1) * PAIR]
        if with_queries:
            queries = (mm(left, wq[...]) + qb[...]).astype(BF).astype(F32) * HEAD**-0.5
            for pair in range(pairs):
                part = queries[:, pair * PAIR : (pair + 1) * PAIR]
                low = low_half(part.shape)
                qst[which, pair, 0:rows] = jnp.where(low, part, 0.0).astype(BF)
                qst[which, pair, rows : 2 * rows] = jnp.where(low, 0.0, part).astype(BF)

    def attend(which, slot):
        index = bases[which] + slot

        def pair_step(pair):
            s = mm_nt(k_all[pair, index], qst[which, pair])
            before = m[which, pair]
            now = jnp.maximum(before, jnp.max(s, axis=0, keepdims=True))
            low = jnp.exp(s - now).astype(BF)
            decay = jnp.exp(before - now)
            m[which, pair] = now
            vt = jnp.transpose(v_all[pair, index])
            ones = jnp.ones((16, rows), BF)
            for head in range(2):
                feats = slice(head * HEAD, (head + 1) * HEAD)
                cols = slice(head * rows, (head + 1) * rows)
                mixed = mm(jnp.concatenate([vt[feats], ones], 0), low[:, cols])
                ot[which, pair, feats] = ot[which, pair, feats] * decay[:, cols] + mixed[0:HEAD]
                l[which, pair, :, cols] = l[which, pair, :, cols] * decay[:, cols] + mixed[HEAD : HEAD + 1]

        loop(pairs, pair_step, unroll=3)

    plan = Plan()
    places = [(number, 0, width) for number in range(MATRICES - 1)]
    places += [(MATRICES - 1, half * width // 2, width // 2) for half in (0, 1)]
    sums = []
    wholes = 0
    for number, (matrix, start, size) in enumerate(places):
        groups = groups_of(number, dp_bits, blk_bits)
        count = whole_count(size, groups)
        space = r["landing"].shape[1] // 2 if size < width else r["landing"].shape[1]
        slot = landing_slot(matrix, blocks)
        sums.append(
            Sum(
                plan,
                held.at[matrix, pl.ds(start, size)],
                r["landing"].at[slot, pl.ds(space if start else 0, space)],
                r["last"].at[pl.ds(wholes, count)],
                r["sums"].at[matrix, pl.ds(start, size)],
                r["sum_send"].at[number],
                r["sum_recv"].at[number],
                r["sum_free"].at[number],
                r["sum_out"].at[number],
                groups,
            )
        )
        wholes += count
    vector_sum = VectorSum(
        plan, r["vectors"], r["vector_landing"], r["vector_send"], r["vector_recv"], dp_bits + blk_bits
    )

    def pump(microseconds=0.0):
        plan.work(microseconds)
        for s in sums + [vector_sum]:
            if s.active and s.ends <= plan.now:
                s.step()

    def begin(number):
        slot = landing_slot(places[number][0], blocks)
        for other in range(number):
            if landing_slot(places[other][0], blocks) == slot and places[other][0] != places[number][0]:
                while not sums[other].over:
                    min((s for s in sums if s.active), key=lambda s: s.ends).step()
        sums[number].start()

    vacc[...] = jnp.zeros(vacc.shape, F32)
    vub[...] = jnp.zeros(vub.shape, F32)
    both = seqs * rows
    halves = [slice(0, rows), slice(rows, both)]

    def receive(which, step):
        chain = chains[which]
        for side in (0, 1):

            @pl.when(chain.has(side, step))
            def _():
                slot = chain.place + (step if side else -step)
                passing(which, 1 - side, step, slot).wait_recv()

                @pl.when(chain.has(1 - side))
                def _():
                    passing(which, 1 - side, step + 1, slot).start()

    def finish(which):
        def one(pair):
            total = l[which, pair]
            lse[which, pair] = m[which, pair] + jnp.log(total)
            share = 1.0 / total
            for head in range(2):
                feats = slice(head * HEAD, (head + 1) * HEAD)
                cols = slice(head * rows, (head + 1) * rows)
                ot[which, pair, feats] = ot[which, pair, feats] * share[:, cols]
            att[which, pair] = jnp.transpose(ot[which, pair])

        loop(pairs, one, unroll=3)

    def forward_and_feed(slow, active, ginner, gbranch):
        fl = gbranch.at[halves[0]]

        def use(which, step, side):
            chain = chains[which]

            @pl.when(chain.has(side, step))
            def _():
                slot = chain.place + (step if side else -step)
                project(which, slot, fl, False)
                attend(which, slot)

        def sort_rows(step):
            at = window(step, STEP)
            first, second = sort(cot[0, at, :].astype(F32), cot[1, at, :].astype(F32))
            vacc[DB] += fold(first) + fold(second)
            cot[0, at, :] = first.astype(BF)
            cot[1, at, :] = second.astype(BF)

        def attended(which, some):
            return jnp.concatenate([att[which, pair].astype(BF) for pair in some], 1)

        def branch(which):
            here = halves[which]
            hidden[here, :] = xg[own[which]].astype(F32) + (mm(attended(which, range(pairs)), wo[...]) + ob[...])

            def norm_rows(step):
                at = window(which * (rows // STEP) + step, STEP)
                scaled, _ = scaled_rows(hidden[at, :])
                slow[at, :] = (scaled * g2[...] + s2[...]).astype(BF)

            loop(rows // STEP, norm_rows, unroll=4)

        def up(which, part):
            here = halves[which]
            at = slice(part * width, (part + 1) * width)
            inner = mm(slow[here, :], wu[:, at]) + ub[:, at]
            grad_active = mm_nt(cot[which], wd[at, :])
            share = 0.5 * (1.0 + lax.erf(inner * (0.5**0.5)))
            slope = share + inner * (jnp.exp(-0.5 * inner * inner) * 0.3989422804014327)
            active[here, at] = (inner * share).astype(BF)
            low = (grad_active * slope).astype(BF)
            ginner[here, at] = low
            vub[:, at] += fold(low.astype(F32))

        def down(which):
            here = halves[which]
            held[MATRICES - 1, here, :] = (hidden[here, :] + (mm(active[here, :], wd[...]) + db[...])).astype(BF)

        def hidden_back(which, step):
            rows_at = window(step, STEP)
            at = window(which * (rows // STEP) + step, STEP)
            scaled, inverse = scaled_rows(hidden[at, :])
            inside = window(lax.rem(step, PAIR // STEP), STEP)
            block = step // (PAIR // STEP) * (width // TILE)
            grad = jnp.concatenate([ot[which, block + part, inside, :] for part in range(width // TILE)], 1)
            vacc[G2] += fold(grad * scaled)
            vacc[S2] += fold(grad)
            grad_hidden = cot[which, rows_at, :].astype(F32) + norm_back(grad, scaled, inverse, g2[...])
            hidden[at, :] = grad_hidden
            low = grad_hidden.astype(BF)
            gbranch[at, :] = low
            vacc[OB] += fold(low.astype(F32))

        def second_back(which):
            back = mm_nt(ginner[halves[which], :], wu[...])
            for part in range(rows // PAIR):
                for step in range(width // TILE):
                    ot[which, part * (width // TILE) + step] = back[
                        part * PAIR : (part + 1) * PAIR, step * TILE : (step + 1) * TILE
                    ]
            pump(1.0)
            loop(rows // STEP, partial(hidden_back, which), unroll=2)
            pump(0.7)

        def branch_back(which):
            low = mm_nt(gbranch[halves[which], :], wo[...]).astype(BF).astype(F32)
            for pair in range(pairs):
                part = low[:, pair * PAIR : (pair + 1) * PAIR]
                lower = low_half(part.shape)
                gst[which, pair, 0:rows] = jnp.where(lower, part, 0.0).astype(BF)
                gst[which, pair, rows : 2 * rows] = jnp.where(lower, 0.0, part).astype(BF)
                product = jnp.transpose(part * att[which, pair])
                delta[which, pair, :, 0:rows] = jnp.sum(product[0:HEAD], 0, keepdims=True)
                delta[which, pair, :, rows : 2 * rows] = jnp.sum(product[HEAD:PAIR], 0, keepdims=True)
            pump(1.0)

        m[...] = jnp.full(m.shape, FLOOR, F32)
        l[...] = jnp.zeros(l.shape, F32)
        ot[...] = jnp.zeros(ot.shape, F32)
        project(0, chains[0].place, fl, True)
        attend(0, chains[0].place)
        project(1, chains[1].place, fl, True)
        receive(0, 1)
        attend(1, chains[1].place)
        use(0, 1, 0)
        use(0, 1, 1)

        def alternate(step):
            receive(1, step)
            use(1, step, 0)
            use(1, step, 1)

        loop(chains[1].count, alternate, 1)
        if chains[0].count > 2:
            receive(0, 2)
        finish(1)

        for name in ("wo", "cotangent", "wu", "wd"):
            loads[name].wait()
        loop(rows // STEP, sort_rows, unroll=4)
        branch(1)
        up(1, 0)
        up(1, 1)
        down(1)
        second_back(1)
        branch_back(1)

        def single(step):
            use(0, step, 0)

            @pl.when(step + 1 < chains[0].count)
            def _():
                receive(0, step + 1)

            use(0, step, 1)

        loop(chains[0].count, single, 2)
        finish(0)
        for which in (0, 1):
            chain = chains[which]

            def sent(step):
                for side in (0, 1):
                    @pl.when(jnp.logical_and(chain.has(side), chain.has(1 - side, step - 1)))
                    def _():
                        passing(which, side, step, chain.place + (1 - step if side else step - 1)).wait_send()

            loop(chain.count, sent, 1)

        branch(0)
        for part in (0, 1):
            up(0, part)
            pump(2.0)

            def down_weights(step):
                at = window(part * (width // TILE) + step, TILE)
                held[2 * part, window(step, TILE), :] = mm_tn(active[:, at], cot[...].reshape(both, width)).astype(BF)

            for step in range(width // TILE):
                down_weights(step)
                pump(0.4)
            begin(2 * part)

            def up_weights(step):
                at = window(step, TILE)
                held[2 * part + 1, at, :] = mm_tn(slow[:, at], ginner[:, part * width : (part + 1) * width]).astype(BF)

            for step in range(width // TILE):
                up_weights(step)
                pump(0.4)
            begin(2 * part + 1)

        down(0)

        def layer_rows(step):
            at = window(step, STEP)
            to = window(rows // STEP + step, STEP)
            last = MATRICES - 1
            first, second = sort(held[last, at, :].astype(F32), held[last, to, :].astype(F32))
            held[last, at, :] = first.astype(BF)
            held[last, to, :] = second.astype(BF)

        loop(rows // STEP, layer_rows, unroll=4)
        layer_out = [
            pltpu.make_async_copy(held.at[MATRICES - 1, halves[n]], r["layer_out"].at[n], r["out_sems"].at[n])
            for n in (0, 1)
        ]
        for copy in layer_out:
            copy.start()
        pump(1.3)
        second_back(0)

        def output_weights(step):
            at = window(step, TILE)
            left = jnp.concatenate([attended(which, (2 * step, 2 * step + 1)) for which in (0, 1)], 0)
            held[4, at, :] = mm_tn(left, gbranch[...]).astype(BF)

        for step in range(width // TILE):
            output_weights(step)
            pump(0.4)
        begin(4)
        branch_back(0)
        for copy in layer_out:
            copy.wait()

    pl.run_scoped(
        forward_and_feed,
        pltpu.VMEM((both, width), BF),
        pltpu.VMEM((both, inner_width), BF),
        pltpu.VMEM((both, inner_width), BF),
        pltpu.VMEM((both, width), BF),
    )

    ot[...] = jnp.zeros(ot.shape, F32)
    grad_in, grad_out = r["grad_in"], xg
    in_bases = [0, blocks + 1]

    def returning(which, side, slot):
        chain = chains[which]
        arrives = jnp.logical_and(slot == chain.place + (1 if side else -1), side == 0)
        index = in_bases[which] + jnp.where(arrives, chain.count, slot)
        return Pieces(
            grad_out.at[bases[which] + slot],
            grad_in.at[index],
            rows,
            r["g_send"].at[which, slot],
            r["g_recv"].at[index],
            chain.device(side),
        )

    def arrived(which, side, slot):
        index = in_bases[which] + jnp.where(jnp.logical_and(slot == chains[which].place, side == 0), chains[which].count, slot)
        ref = grad_in.at[index]
        Pieces(ref, ref, rows, r["g_send"].at[which, 0], r["g_recv"].at[index], {"blk": mate}).wait_recv()
        return index

    def attention_backward(grad):
        dq = cot

        def pair_back(which, index, pair):
            k, v, q, g = k_all[pair, index], v_all[pair, index], qst[which, pair], gst[which, pair]
            p = jnp.exp(mm_nt(k, q) - lse[which, pair])
            low = (p * (mm_nt(v, g) - delta[which, pair])).astype(BF)
            value_grad = mm(p.astype(BF), g)
            vacc[VB, :, window(pair, PAIR)] += fold(value_grad)
            v_all[pair, index] = value_grad.astype(BF)
            k_all[pair, index] = mm(low, q).astype(BF)
            kt = jnp.transpose(k)
            for head in range(2):
                feats = slice(head * HEAD, (head + 1) * HEAD)
                ot[which, pair, feats] += mm(kt[feats], low[:, head * rows : (head + 1) * rows])

        def slot_back(which, index, group):
            for pair in group:
                pair_back(which, index, pair)
                pump(1.1)

        def joined(values, index):
            return jnp.concatenate([values[pair, index] for pair in range(pairs)], 1)

        def give(which, number):
            chain = chains[which]
            slot, side = chain.visit(number)
            index = bases[which] + slot
            grad[0:rows, :] = mm_nt(joined(k_all, index), wk[...]) + mm_nt(joined(v_all, index), wv[...])

            def gather_rows(step):
                at = window(step, STEP)
                scaled, _ = scaled_rows(xg[index, at, :].astype(F32))
                values = grad[at, :]
                vacc[G1] += fold(values * scaled)
                vacc[S1] += fold(values)
                grad_out[index, at, :] = values.astype(BF)

            loop(rows // STEP, gather_rows, unroll=2)
            for toward in (0, 1):

                @pl.when(jnp.logical_and(side == toward, jnp.logical_not(chain.has(1 - toward))))
                def _():
                    returning(which, toward, slot).start()

            for link in ("inner", "outer"):
                plan.send(link, rows * width * 2)
            pump(1.8)

        def relay(which, distance, number):
            chain = chains[which]
            slot, side = chain.visit(number)
            for toward in (0, 1):
                behind = chain.place if toward else chain.count - 1 - chain.place

                @pl.when(jnp.logical_and(side == toward, behind == distance))
                def _():
                    place = arrived(which, toward, slot)

                    def add(step):
                        at = window(step, STEP)
                        out = bases[which] + slot
                        grad_out[out, at, :] = (
                            grad_out[out, at, :].astype(F32) + grad_in[place, at, :].astype(F32)
                        ).astype(BF)

                    loop(rows // STEP, add, unroll=4)
                    returning(which, toward, slot).start()

        def other(which, number):
            return bases[which] + chains[which].visit(number)[0]

        def query_rows(which, pair):
            value = jnp.transpose(ot[which, pair]) * HEAD**-0.5
            vacc[QB, :, window(pair, PAIR)] += fold(value)
            dq[which, :, window(pair, PAIR)] = value.astype(BF)

        def weights(group, step):
            at = window(step, TILE)
            number = 5 + group
            pair = 2 * group
            flat = (k_all.shape[1] * rows, PAIR)
            right = jnp.concatenate(
                [k_all[pair].reshape(flat), k_all[pair + 1].reshape(flat)]
                + [v_all[pair].reshape(flat), v_all[pair + 1].reshape(flat)],
                1,
            )
            held[number, at, TILE : 3 * TILE] = mm(flt[at, :], right).astype(BF)
            columns = window(group, TILE)
            held[number, at, 0:TILE] = sum(
                mm(flt[at, window(own[which], rows)], dq[which, :, columns]) for which in (0, 1)
            ).astype(BF)

        groups_of_heads = [(2 * group, 2 * group + 1) for group in range(pairs // 2)]
        alternate = [(1, n) for n in range(chains[1].count - 1)]
        singles = [(0, n) for n in range(chains[0].count - 1)]
        for which, number in alternate:
            slot_back(which, other(which, number), range(pairs))
            give(which, number)
        slot_back(1, own[1], range(pairs))
        for pair in range(pairs):
            query_rows(1, pair)
        for group, members in enumerate(groups_of_heads):
            final = group == len(groups_of_heads) - 1
            for which, number in singles:
                slot_back(which, other(which, number), members)
                if final:
                    give(which, number)
                    given = plan.now
            slot_back(0, own[0], members)
            for pair in members:
                query_rows(0, pair)
            for step in range(width // TILE):
                weights(group, step)
                pump(0.8)
                if final and step == (width // TILE) // 2:
                    begin(7)
            begin(8 if final else 5 + group)
            pump()
        for which in (0, 1):
            grad[halves[which], :] = (
                mm_nt(joined(k_all, own[which]), wk[...])
                + mm_nt(joined(v_all, own[which]), wv[...])
                + mm_nt(dq[which], wq[...])
            )
        pump(2.5)
        for which in (0, 1):

            def own_rows(step):
                at = window(step, STEP)
                to = window(which * (rows // STEP) + step, STEP)
                scaled, _ = scaled_rows(xg[own[which], at, :].astype(F32))
                values = grad[to, :]
                vacc[G1] += fold(values * scaled)
                vacc[S1] += fold(values)

            loop(rows // STEP, own_rows, unroll=2)

        vectors = r["vectors"]
        vectors[...] = jnp.zeros(vectors.shape, F32)
        for number in range(UB):
            vectors[number : number + 1, :] = jnp.sum(vacc[number], 0, keepdims=True)
        for part in range(inner_width // width):
            vectors[UB + part : UB + part + 1, :] = jnp.sum(vub[:, part * width : (part + 1) * width], 0, keepdims=True)
        vector_sum.start()
        pump(1.0)

        def drain(until):
            while True:
                left = [s for s in sums + [vector_sum] if s.active]
                if not left or min(s.ends for s in left) > until:
                    return
                min(left, key=lambda s: s.ends).step()

        hop = HOP + rows * width * 4 / 1e5
        for distance in range(1, chains[0].count - 1):
            drain(given + distance * hop)
            for which in (1, 0):
                if distance < chains[which].count - 1:
                    loop(chains[which].count - 1, partial(relay, which, distance))
        drain(given + (chains[0].count - 1) * hop)
        for which in (0, 1):
            for side in (0, 1):

                @pl.when(chains[which].has(1 - side))
                def _():
                    place = arrived(which, side, chains[which].place)

                    def add(step):
                        to = window(which * (rows // STEP) + step, STEP)
                        grad[to, :] += grad_in[place, window(step, STEP), :].astype(F32)

                    loop(rows // STEP, add, unroll=4)

        pump(0.8)

        def tokens_back(step):
            at = window(step, STEP)
            parts = []
            for which in (0, 1):
                to = window(which * (rows // STEP) + step, STEP)
                scaled, inverse = scaled_rows(xg[own[which], at, :].astype(F32))
                parts.append(hidden[to, :] + norm_back(grad[to, :], scaled, inverse, g1[...]))
            first, second = sort(*parts)
            cot[0, at, :] = first.astype(BF)
            cot[1, at, :] = second.astype(BF)

        loop(rows // STEP, tokens_back, unroll=2)
        tokens_out = pltpu.make_async_copy(cot, r["tokens_grad"], r["out_sems"].at[2])
        tokens_out.start()
        pump(1.0)

        for which, number in alternate + singles:
            slot, side = chains[which].visit(number)
            for toward in (0, 1):

                @pl.when(side == toward)
                def _():
                    returning(which, toward, slot).wait_send()

        drain(float("inf"))
        for s in sums:
            s.settle().wait()
        tokens_out.wait()

    pl.run_scoped(attention_backward, pltpu.VMEM((both, width), F32))


def run_layer(operands):
    blocks, groups = lax.axis_size("blk"), lax.axis_size("dp")
    seqs, rows, width = operands["tokens"].shape
    inner = operands["ub"].shape[0]
    pairs = width // PAIR
    slots = blocks + blocks // 2
    bits = (blocks * groups).bit_length() - 1
    places = [width] * (MATRICES - 1) + [width // 2] * 2
    orders = [groups_of(n, axis_bits("dp", groups), axis_bits("blk", blocks)) for n in range(len(places))]
    landing = max(
        landing_rows(size, order) * (width // size) for size, order in zip(places, orders, strict=True)
    )
    landing = (landing + 31) // 32 * 32
    wholes = sum(whole_count(size, order) for size, order in zip(places, orders, strict=True))
    last = max(
        part for size, order in zip(places, orders, strict=True) for part, split in halving(size, order) if not split
    )
    landings = 1 + max(landing_slot(matrix, blocks) for matrix in range(MATRICES))
    vmem = pl.BlockSpec(memory_space=pltpu.VMEM)
    hbm = pl.BlockSpec(memory_space=pl.ANY)
    out_shape = {
        "layer_out": jax.ShapeDtypeStruct((seqs, rows, width), BF),
        "tokens_grad": jax.ShapeDtypeStruct((seqs, rows, width), BF),
        "sums": jax.ShapeDtypeStruct((MATRICES, width, width), BF),
        "vectors": jax.ShapeDtypeStruct((16, width), F32),
    }
    dma = pltpu.SemaphoreType.DMA
    scratch = {name + "_v": pltpu.VMEM(operands[name].shape, BF) for name in LARGE if name[0] == "w"}
    scratch |= {
        "cot_v": pltpu.VMEM((seqs, rows, width), BF),
        "rows": pltpu.VMEM((len(SMALL), width), F32),
        "ub_v": pltpu.VMEM((1, inner), F32),
        "small_sems": dma((len(SMALL) + 1,)),
        "theirs": pltpu.VMEM((seqs, rows), jnp.int32),
        "xg": pltpu.VMEM((slots, rows, width), BF),
        "flt": pltpu.VMEM((width, slots * rows), BF),
        "k_all": pltpu.VMEM((pairs, slots, rows, PAIR), BF),
        "v_all": pltpu.VMEM((pairs, slots, rows, PAIR), BF),
        "qst": pltpu.VMEM((seqs, pairs, 2 * rows, PAIR), BF),
        "gst": pltpu.VMEM((seqs, pairs, 2 * rows, PAIR), BF),
        "m": pltpu.VMEM((seqs, pairs, 1, 2 * rows), F32),
        "l": pltpu.VMEM((seqs, pairs, 1, 2 * rows), F32),
        "lse": pltpu.VMEM((seqs, pairs, 1, 2 * rows), F32),
        "delta": pltpu.VMEM((seqs, pairs, 1, 2 * rows), F32),
        "ot": pltpu.VMEM((seqs, pairs, PAIR, rows), F32),
        "att": pltpu.VMEM((seqs, pairs, rows, PAIR), F32),
        "hidden": pltpu.VMEM((seqs * rows, width), F32),
        "vacc": pltpu.VMEM((UB, 8, width), F32),
        "vub": pltpu.VMEM((8, inner), F32),
        "held": pltpu.VMEM((MATRICES, width, width), BF),
        "landing": pltpu.VMEM((landings, landing, width), BF),
        "last": pltpu.VMEM((wholes, last, width), BF),
        "vector_landing": pltpu.VMEM((bits, 16, width), F32),
        "grad_in": pltpu.VMEM((slots + 2, rows, width), BF),
        "out_sems": dma((3,)),
        "load_sems": dma((len(LARGE),)),
        "scene_sems": dma((2,)),
        "x_send": dma((2, 2, blocks + 1, PIECES)),
        "x_recv": dma((2, 2, blocks + 1, PIECES)),
        "g_send": dma((2, blocks, PIECES)),
        "g_recv": dma((slots + 2, PIECES)),
        "sum_send": dma((len(places), 2 * bits, 4)),
        "sum_recv": dma((len(places), 2 * bits, 4)),
        "sum_free": pltpu.SemaphoreType.REGULAR((len(places), bits, 4)),
        "sum_out": dma((len(places),)),
        "vector_send": dma((bits,)),
        "vector_recv": dma((bits,)),
    }
    names = tuple(operands) + tuple(out_shape) + tuple(scratch)
    return pl.pallas_call(
        partial(layer_kernel, blocks, groups, names),
        out_shape=tuple(out_shape.values()),
        in_specs=[vmem if name == "scenes" else hbm for name in operands],
        out_specs=(hbm, hbm, hbm, vmem),
        scratch_shapes=list(scratch.values()),
        compiler_params=pltpu.CompilerParams(
            collective_id=0, has_side_effects=True, vmem_limit_bytes=int(63.8 * 2**20)
        ),
    )(*operands.values())


def spread_kernel(layer_out, tokens_grad, sums, vectors, *refs):
    outs, (narrow, wide, passed, in_sems, out_sems, pass_sems, vector_sems) = refs[:17], refs[17:]
    down, up, out, query, key, value = outs[2:8]
    width = sums.shape[1]
    half = width // 2
    order = [5, 6, 7, 0, 1, 2, 3, 4]
    loads = {}
    for number in order:
        for part in range(2):
            at = pl.ds(part * half, half)
            loads[number, part] = pltpu.make_async_copy(
                sums.at[number, at], narrow.at[number, at], in_sems.at[number, part]
            )
            loads[number, part].start()
    passing = []
    for n, source in enumerate((layer_out, tokens_grad)):
        passing.append(pltpu.make_async_copy(source, passed.at[n], pass_sems.at[0, n]))
        passing[-1].start()
    stores = [pltpu.make_async_copy(vectors.at[n], outs[8 + n], vector_sems.at[n]) for n in range(UB)]
    for part in range(2):
        target = outs[8 + UB].at[pl.ds(part * width, width)]
        stores.append(pltpu.make_async_copy(vectors.at[UB + part], target, vector_sems.at[UB + part]))
    for store in stores:
        store.start()

    def send(number, part, target):
        at = pl.ds(part * half, half)
        stores.append(pltpu.make_async_copy(wide.at[number, at], target, out_sems.at[number, part]))
        stores[-1].start()

    for number in order:
        for part in range(2):
            loads[number, part].wait()

            def widen(step):
                at = window(part * (half // STEP) + step, STEP)
                if number < 5:
                    wide[number, at] = narrow[number, at].astype(F32)
                else:
                    columns = pl.ds((number - 5) * TILE, TILE)
                    for n in range(3):
                        wide[5 + n, at, columns] = narrow[number, at, n * TILE : (n + 1) * TILE].astype(F32)

            loop(half // STEP, widen, unroll=4)
            at = pl.ds(part * half, half)
            if number in (0, 2):
                send(number, part, down.at[pl.ds(number // 2 * width + part * half, half)])
            elif number in (1, 3):
                send(number, part, up.at[at, pl.ds(number // 2 * width, width)])
            elif number == 4:
                send(number, part, out.at[at])
            elif number == MATRICES - 1:
                for n, matrix in enumerate((query, key, value)):
                    send(5 + n, part, matrix.at[at])
        if number == 7:
            for n in (0, 1):
                passing[n].wait()
                stores.append(pltpu.make_async_copy(passed.at[n], outs[n], pass_sems.at[1, n]))
                stores[-1].start()
    for store in stores:
        store.wait()


def spread(layer_out, tokens_grad, sums, vectors):
    width = sums.shape[1]
    matrices = [(2 * width, width), (width, 2 * width)] + [(width, width)] * 4
    shapes = [jax.ShapeDtypeStruct(value.shape, BF) for value in (layer_out, tokens_grad)]
    shapes += [jax.ShapeDtypeStruct(shape, F32) for shape in matrices + [(width,)] * UB + [(2 * width,)]]
    hbm = pl.BlockSpec(memory_space=pl.ANY)
    return pl.pallas_call(
        spread_kernel,
        out_shape=tuple(shapes),
        in_specs=[hbm, hbm, hbm, pl.BlockSpec(memory_space=pltpu.VMEM)],
        out_specs=(hbm,) * len(shapes),
        scratch_shapes=[
            pltpu.VMEM(sums.shape, BF),
            pltpu.VMEM(sums.shape, F32),
            pltpu.VMEM((2,) + layer_out.shape, BF),
            pltpu.SemaphoreType.DMA((MATRICES, 2)),
            pltpu.SemaphoreType.DMA((MATRICES, 2)),
            pltpu.SemaphoreType.DMA((2, 2)),
            pltpu.SemaphoreType.DMA((UB + 2,)),
        ],
        compiler_params=pltpu.CompilerParams(vmem_limit_bytes=63 * 2**20),
    )(layer_out, tokens_grad, sums, vectors)


def on_device(
    tokens,
    scene_ids,
    query_weight,
    query_bias,
    key_weight,
    value_weight,
    value_bias,
    output_weight,
    output_bias,
    first_gain,
    first_shift,
    second_gain,
    second_shift,
    up_weight,
    up_bias,
    down_weight,
    down_bias,
    cotangent,
):
    operands = {
        "tokens": tokens,
        "scenes": scene_ids,
        "wq": query_weight,
        "wk": key_weight,
        "wv": value_weight,
        "wo": output_weight,
        "wu": up_weight,
        "wd": down_weight,
        "cotangent": cotangent,
        "qb": query_bias,
        "vb": value_bias,
        "ob": output_bias,
        "g1": first_gain,
        "s1": first_shift,
        "g2": second_gain,
        "s2": second_shift,
        "ub": up_bias,
        "db": down_bias,
    }
    (
        layer_out,
        tokens_grad,
        down_grad,
        up_grad,
        output_grad,
        query_grad,
        key_grad,
        value_grad,
        query_bias_grad,
        value_bias_grad,
        output_bias_grad,
        first_gain_grad,
        first_shift_grad,
        second_gain_grad,
        second_shift_grad,
        down_bias_grad,
        up_bias_grad,
    ) = spread(*run_layer(operands))
    return (
        layer_out,
        tokens_grad,
        query_grad,
        query_bias_grad,
        key_grad,
        value_grad,
        value_bias_grad,
        output_grad,
        output_bias_grad,
        first_gain_grad,
        first_shift_grad,
        second_gain_grad,
        second_shift_grad,
        up_grad,
        up_bias_grad,
        down_grad,
        down_bias_grad,
    )


def solution(mesh):
    split = P("dp", "blk", None)
    in_specs = (split, P("dp", "blk")) + (P(),) * 15 + (split,)
    out_specs = (split, split) + (P(),) * 15
    return jax.shard_map(on_device, mesh=mesh, in_specs=in_specs, out_specs=out_specs, check_vma=False)
```
